32 devices in a mesh: runs: 2 (over y), tm: 4 (over z), grp: 2 (over x), state: 2 (over core).
Axes of the slice: x: 2, y: 2, z: 4, core: 2. Of those that a mesh axis runs over, the one named last changes fastest.
Arguments:
- rows_h: bfloat16 [4, 64, 128, 512], P(('runs', 'grp'), 'tm', None, 'state'), parts along dimension 0, may hold values from -0.27 to 0.27
- rows_y: bfloat16 [4, 64, 128], P(('runs', 'grp'), 'tm'), parts along dimension 0, may hold values from -6 to 6
- tile_block: int32 [4, 64, 1], P(('runs', 'grp'), 'tm'), parts along dimension 0, may hold values from 0 to 3; in each aligned block of 16 rows (0 to 15, 16 to 31, ..., all dimensions but the last counted through in order) at most 16 rows name the same one
- tile_count: int32 [4, 64], P(('runs', 'grp'), 'tm'), parts along dimension 0, may hold values from 1 to 128
- kappa: float32 [4, 4, 512], P(('runs', 'grp'), 'tm'), parts along dimension 0, may hold values from 0.02 to 0.2
- rate: float32 [4, 4, 512], P(('runs', 'grp'), 'tm'), parts along dimension 0, may hold values from 0.0001 to 0.05
- smooth_gain: float32 [4, 4, 512], P(('runs', 'grp'), 'tm'), parts along dimension 0, may hold values from 0.3 to 0.995
- start_state: float32 [1024], P('runs'), parts along dimension 0, may hold values from -6 to 6
Outputs:
- filtered: float32 [4, 4, 512], P(('runs', 'grp'), 'tm', 'state'), parts along dimension 0
- smoothed: float32 [4, 4, 512], P(('runs', 'grp'), 'tm', 'state'), parts along dimension 0
The draws below stay inside these ranges and needn't reach their ends.
There are 2 independent parts, one for each index of `runs`. The reference program is written for one: setup_inputs(seed, part) draws one part's arguments, and reference() takes and returns one part's arrays. A program takes and returns all parts, laid end to end along the dimension named above; each array names one. Nothing has to cross between parts.
Inputs may be any that keep to these rules, and one draw needn't show every extreme that they name: `tile_block`: among the 16 tiles of one device, at most 16 project to the same time block.
All inputs are finite; a program needn't handle non-finite values.
Results may differ from the reference program's by a relative error of at most 0.0023.
Values may be sent and summed in bfloat16 or wider, within the bound.
No kernel may reach another device: no remote copies, remote signals or barrier semaphores. Data moves between devices by JAX's collectives and lax.ppermute only.
A program may use at most 128 MiB of HBM per device.

```python
import math
import jax
import jax.numpy as jnp
import numpy as np
from jax import lax

S = 512
ROWS = 128
STEPS = 4
TILES_DEV = 16
CAP = 16
N_TM = 4
N_GRP = 2


def draw_rows_h(key, part):
    shape = (N_GRP, N_TM * TILES_DEV, ROWS, S)
    sensitivity = jnp.exp(jax.random.uniform(jax.random.fold_in(key, 11), (S,), jnp.float32, math.log(0.003), 0.0))
    base = jnp.clip(jax.random.normal(jax.random.fold_in(key, 12), shape, jnp.float32), -6.0, 6.0)
    return (base * sensitivity * (1.0 / math.sqrt(512.0))).astype(jnp.bfloat16)


def place_ends(result, own_key, smallest, high):
    longest = result.shape.index(max(result.shape))
    spots = []
    for shift in (0, 1):
        where = [jax.random.randint(jax.random.fold_in(own_key, axis), (), 0, length) for axis, length in enumerate(result.shape)]
        where[longest] = (where[longest] + shift) % result.shape[longest]
        spots.append(tuple(where))
    return result.at[spots[0]].set(smallest).at[spots[1]].set(high)


def steps_of(rng, shape, shards, least, high):
    factor_of = 1.0
    for position, shards_of in shards:
        draws = jax.random.uniform(jax.random.fold_in(jax.random.fold_in(rng, 6), position), (shards_of,), jnp.float32, least / len(shards), high / len(shards))
        factor_of = factor_of * jnp.repeat(jnp.exp(draws), shape[position] // shards_of).reshape((-1,) + (1,) * (len(shape) - 1 - position))
    return factor_of


def routed_block(key, own, number, rows, amount, top, bound, slope):
    ranking = jax.random.permutation(key, amount)
    packed, usual = portions_of(amount, rows * top, bound, slope, True), portions_of(amount, rows * top, bound, slope, False)
    places = jnp.arange(amount)

    def named(lengths, offset_by):
        used = int((lengths > 0).sum())
        fixed = max(1, used // 4)
        passed = fixed + (places - fixed + offset_by * (used - fixed)) % max(1, amount - fixed)
        return jnp.zeros((amount,), jnp.int32).at[ranking[jnp.where(places < fixed, places, passed)]].set(jnp.asarray(lengths, jnp.int32))

    lengths = jnp.where(number % 4 == 0, named(packed, number // 4), named(usual, number - number // 4 - 1))
    mixed = jax.random.permutation(jax.random.fold_in(own, 3), amount)
    donor, sink = mixed[0:amount // 2 * 2:2], mixed[1:amount // 2 * 2:2]
    room = jnp.minimum(lengths[donor] - 1, bound - lengths[sink]) // 2
    room = jnp.where((donor == ranking[0]) | (sink == ranking[0]) | (lengths[sink] == 0), 0, jnp.maximum(room, 0))
    passed = jax.random.randint(jax.random.fold_in(own, 4), (amount // 2,), 0, 1 << 20) % (room + 1)
    lengths = lengths.at[donor].add(-passed).at[sink].add(passed)
    labels = jnp.searchsorted(jnp.cumsum(lengths), jnp.arange(rows * top), side="right").astype(jnp.int32)
    table = labels.reshape(top, rows).T
    table = table[jax.random.permutation(jax.random.fold_in(own, 1), rows)]
    offset_by = jax.random.randint(jax.random.fold_in(own, 2), (rows, 1), 0, top)
    return jnp.take_along_axis(table, (jnp.arange(top)[None, :] + offset_by) % top, axis=1)


def portions_of(count, total, bound, slope, full):
    portions = [(1 << 20) // math.isqrt(grade ** slope) + 1 for grade in range(1, count + 1)]
    largest = bound if full else min(bound, max(-(-total // count), total * portions[0] // sum(portions)))
    least = 1 if total - largest >= count - 1 else 0
    given, spare = [largest] + [least] * (count - 1), total - largest - least * (count - 1)
    while spare > 0:
        candidates = [i for i in range(1, count) if given[i] < largest] or [i for i in range(1, count) if given[i] < bound]
        whole, remaining = sum([portions[i] for i in candidates]), spare
        for i in candidates:
            extra = min(bound - given[i], max(1, remaining * portions[i] // whole), spare)
            given[i] = given[i] + extra
            spare = spare - extra
    return np.array(given)


def normal_values(rng, extent, width, bound, pieces=(), held_as=jnp.bfloat16):
    values = width * jax.random.normal(rng, extent, jnp.float32)
    if pieces:
        values = values * steps_of(rng, extent, pieces, -0.22, 0.18)
    return jnp.clip(values, -bound, bound).astype(held_as)


def setup_inputs(seed: int = 0, part: int = 0) -> dict:
    keys = jax.random.split(jax.random.key(seed), 9)
    own_keys = jax.random.split(jax.random.fold_in(keys[8], part), 9)
    rows_h = draw_rows_h(jax.random.fold_in(jax.random.fold_in(keys[8], part), 71), part)
    rows_y = normal_values(own_keys[1], (N_GRP, N_TM * TILES_DEV, ROWS), 1.0, 6.0, ((0, 2), (1, 4)))
    tile_block_keys = jax.random.split(jax.random.fold_in(own_keys[2], 1), N_GRP * (N_TM * TILES_DEV) // TILES_DEV)
    tile_block_turns = jax.random.permutation(jax.random.fold_in(own_keys[2], 3), N_GRP * (N_TM * TILES_DEV) // TILES_DEV)
    tile_block = jax.vmap(lambda own, number: routed_block(jax.random.fold_in(own_keys[2], 2), own, number, TILES_DEV, N_TM, 1, CAP, 2))(tile_block_keys, tile_block_turns).reshape((N_GRP, N_TM * TILES_DEV, 1))
    tile_count = place_ends(jax.random.randint(own_keys[3], (N_GRP, N_TM * TILES_DEV), 1, ROWS + 1), jax.random.fold_in(own_keys[3], 1), 1, ROWS).astype(jnp.int32)
    kappa = jnp.clip(jnp.exp(math.log(0.2) - 2.3025851 * jax.random.uniform(own_keys[4], (N_GRP, N_TM, S), jnp.float32) ** steps_of(own_keys[4], (N_GRP, N_TM, S), ((0, 2), (1, 4)), -0.2, 0.2)), 0.02, 0.2)
    rate = jnp.clip(jnp.exp(math.log(0.05) - 6.214608 * jax.random.uniform(own_keys[5], (N_GRP, N_TM, S), jnp.float32) ** steps_of(own_keys[5], (N_GRP, N_TM, S), ((0, 2), (1, 4)), -0.2, 0.2)), 0.0001, 0.05)
    smooth_gain = jnp.clip(jnp.exp(math.log(0.995) - 1.1989602 * jax.random.uniform(own_keys[6], (N_GRP, N_TM, S), jnp.float32) ** steps_of(own_keys[6], (N_GRP, N_TM, S), ((0, 2), (1, 4)), -0.2, 0.2)), 0.3, 0.995)
    start_state = normal_values(own_keys[7], (S,), 1.0, 6.0, (), jnp.float32)
    return {"rows_h": rows_h, "rows_y": rows_y, "tile_block": tile_block, "tile_count": tile_count, "kappa": kappa, "rate": rate, "smooth_gain": smooth_gain, "start_state": start_state}


def stencil(field, coeff, decay):
    for step_index in range(STEPS):
        zero_row = jnp.zeros_like(field[:1])
        upper_cell = jnp.concatenate([zero_row, field[:-1]], axis=0)
        lower_cell = jnp.concatenate([field[1:], zero_row], axis=0)
        field = field + coeff * (upper_cell + lower_cell - 2.0 * field) - decay * field
    return field


def reference(rows_h, rows_y, tile_block, tile_count, kappa, rate, smooth_gain, start_state):
    live_rows = jnp.arange(ROWS, dtype=jnp.int32)[None, None, :] < tile_count[:, :, None]
    h_masked = jnp.where(live_rows[..., None], rows_h, jnp.zeros((), rows_h.dtype))
    y_masked = jnp.where(live_rows, rows_y, jnp.zeros((), rows_y.dtype))
    owners = (jnp.arange(N_GRP, dtype=jnp.int32)[:, None] * N_TM + tile_block[:, :, 0]).reshape(-1).astype(jnp.int32)
    h_flat = h_masked.reshape(-1, ROWS, S)
    y_flat = y_masked.reshape(-1, ROWS)
    block_num = N_GRP * N_TM

    def add_tile(carry, item):
        grams, vectors, traces = carry
        owner, tile_h, tile_y = item
        gram_tile = jnp.dot(tile_h.T, tile_h, preferred_element_type=jnp.float32)
        info_tile = jnp.dot(tile_y, tile_h, preferred_element_type=jnp.float32)
        trace_tile = jnp.sum(jnp.square(tile_h.astype(jnp.float32)))
        return (grams.at[owner].add(gram_tile), vectors.at[owner].add(info_tile), traces.at[owner].add(trace_tile)), None

    init = (jnp.zeros((block_num, S, S), jnp.float32), jnp.zeros((block_num, S), jnp.float32), jnp.zeros((block_num,), jnp.float32))
    (grams, vectors, traces), _ = lax.scan(add_tile, init, (owners, h_flat, y_flat))
    kappa_rows = kappa.reshape(block_num, S)
    rate_rows = rate.reshape(block_num, S)

    def forward(current, item):
        gram, vector, trace_val, kappa_row, rate_row = item
        lam_val = S / (2.0 * (S + trace_val))
        transition = stencil(jnp.eye(S, dtype=jnp.float32) - lam_val * gram, kappa_row[:, None], rate_row[:, None])
        forcing = lam_val * stencil(vector, kappa_row, rate_row)
        updated = jnp.dot(transition, current, precision=lax.Precision.HIGHEST) + forcing
        innovation = updated - stencil(current, kappa_row, rate_row)
        return updated, (updated, innovation)

    _, (filtered, innovations) = lax.scan(forward, start_state, (grams, vectors, traces, kappa_rows, rate_rows))

    def backward(residual, item):
        updated, innovation, gain_row = item
        return gain_row * (residual + innovation), updated + residual

    _, smoothed = lax.scan(backward, jnp.zeros((S,), jnp.float32), (filtered, innovations, smooth_gain.reshape(block_num, S)), reverse=True)
    return filtered.reshape(N_GRP, N_TM, S), smoothed.reshape(N_GRP, N_TM, S)
```

```python
import functools

import jax
import jax.numpy as jnp
from jax import lax
from jax.experimental import pallas as pl
from jax.experimental.pallas import tpu as pltpu
from jax.sharding import PartitionSpec as P

STEPS = 4
LANES = 128
GROUP_ROWS = 16
DIRECT_TM = 4

VMEM = pl.BlockSpec(memory_space=pltpu.VMEM)
SMEM = pl.BlockSpec(memory_space=pltpu.SMEM)


def stencil(field, coeff, decay):
    width = field.shape[1]
    cell = lax.broadcasted_iota(jnp.int32, field.shape, 1)
    for _ in range(STEPS):
        upper_cell = jnp.where(cell == 0, 0.0, pltpu.roll(field, 1, 1))
        lower_cell = jnp.where(cell == width - 1, 0.0, pltpu.roll(field, width - 1, 1))
        field = field + coeff * (upper_cell + lower_cell - 2.0 * field) - decay * field
    return field


def row_pass(block, state, meta, y_ref, own_ref, other_ref, acc, part_ref):
    tile_num, row_num, half = own_ref.shape
    core = meta[2 * tile_num]
    own_at = pl.multiple_of(core * half, half)
    other_at = pl.multiple_of((1 - core) * half, half)
    state_own = state[:, pl.ds(own_at, half)]
    state_other = state[:, pl.ds(other_at, half)]
    lane = lax.broadcasted_iota(jnp.int32, (GROUP_ROWS, LANES), 1)
    row = lax.broadcasted_iota(jnp.int32, (GROUP_ROWS, LANES), 0)
    acc[...] = jnp.zeros_like(acc)

    def fold(values):
        total = values[:, :LANES]
        for start in range(LANES, half, LANES):
            total = total + values[:, start : start + LANES]
        return total

    def tile(index, carry):
        @pl.when(meta[index] == block)
        def _():
            live = meta[tile_num + index]
            readings = y_ref[pl.ds(index, 1), :]
            sum_own = jnp.zeros((GROUP_ROWS, half), jnp.float32)
            sum_other = jnp.zeros((GROUP_ROWS, half), jnp.float32)
            squares = jnp.zeros((GROUP_ROWS, LANES), jnp.float32)
            for start in range(0, row_num, GROUP_ROWS):
                own = own_ref[index, start : start + GROUP_ROWS, :].astype(jnp.float32)
                other = other_ref[index, start : start + GROUP_ROWS, :].astype(jnp.float32)
                valid = row + start < live
                product = fold(own * state_own) + fold(other * state_other)
                product = product - jnp.where(lane == row + start, readings, 0.0)
                weight = jnp.sum(product, axis=1, keepdims=True)
                weight = jnp.where(valid[:, :1], weight, 0.0)
                sum_own = sum_own + own * weight
                sum_other = sum_other + other * weight
                squares = squares + jnp.where(valid, fold(own * own) + fold(other * other), 0.0)
            acc[:, :half] += sum_own
            acc[:, half : 2 * half] += sum_other
            acc[:, 2 * half :] += squares

        return carry

    lax.fori_loop(0, tile_num, tile, 0)
    totals = jnp.sum(acc[...], axis=0, keepdims=True)
    part_ref[:, pl.ds(own_at, half)] = totals[:, :half]
    part_ref[:, pl.ds(other_at, half)] = totals[:, half : 2 * half]
    part_ref[:, 2 * half :] = totals[:, 2 * half :]


def first_kernel(block, meta, y_ref, own_ref, other_ref, state_ref, part_ref, acc):
    row_pass(block, state_ref, meta, y_ref, own_ref, other_ref, acc, part_ref)


def advance(parts, state, kappa_ref, rate_ref):
    total = parts[0][...]
    for part in parts[1:]:
        total = total + part[...]
    width = state.shape[1]
    trace_val = jnp.sum(total[:, width:], axis=1, keepdims=True)
    lam_val = width / (2.0 * (width + trace_val))
    innovation = -lam_val * stencil(total[:, :width], kappa_ref, rate_ref)
    return stencil(state, kappa_ref, rate_ref) + innovation, innovation


def step_kernel(block, number, *refs):
    parts, rest = refs[:number], refs[number:]
    meta, y_ref, own_ref, other_ref, state_ref, kappa_ref, rate_ref = rest[:7]
    next_ref, innovation_ref, part_ref, acc = rest[7:]
    updated, innovation = advance(parts, state_ref[...], kappa_ref[...], rate_ref[...])
    next_ref[...] = updated
    innovation_ref[...] = innovation
    if block is None:
        block = meta[2 * y_ref.shape[0] + 1]
    row_pass(block, next_ref, meta, y_ref, own_ref, other_ref, acc, part_ref)


def last_kernel(number, *refs):
    parts, (state_ref, kappa_ref, rate_ref, next_ref, innovation_ref) = refs[:number], refs[number:]
    updated, innovation = advance(parts, state_ref[...], kappa_ref[...], rate_ref[...])
    next_ref[...] = updated
    innovation_ref[...] = innovation


def shards(rows_h, rows_y, tile_block, tile_count, kappa, rate, smooth_gain, start_state):
    tm_size, grp_size = lax.axis_size("tm"), lax.axis_size("grp")
    state_size = lax.axis_size("state")
    tm_index, grp_index, core = (lax.axis_index(name) for name in ("tm", "grp", "state"))
    tile_num, half = rows_h.shape[1], rows_h.shape[3]
    width = kappa.shape[2]
    own = rows_h[0]
    other = lax.ppermute(own, "state", [(i, (i + 1) % state_size) for i in range(state_size)])
    readings = rows_y[0].astype(jnp.float32)
    meta = jnp.concatenate([tile_block[0, :, 0], tile_count[0], core[None].astype(jnp.int32)])
    state = start_state.reshape(1, width)
    direct = tm_size <= DIRECT_TM

    params = jnp.concatenate([kappa[0], rate[0], smooth_gain[0]], axis=0)
    if direct:
        gathered = jnp.zeros((tm_size,) + params.shape, params.dtype)
        gathered = lax.dynamic_update_slice_in_dim(gathered, params[None], tm_index, 0)
        for shift in range(1, tm_size):
            moved = lax.ppermute(params, "tm", [(i, (i + shift) % tm_size) for i in range(tm_size)])
            gathered = lax.dynamic_update_slice_in_dim(
                gathered, moved[None], (tm_index - shift) % tm_size, 0
            )
    else:
        gathered = lax.all_gather(params, "tm")

    vector = jax.ShapeDtypeStruct((1, width), jnp.float32)
    partial = jax.ShapeDtypeStruct((1, width + LANES), jnp.float32)
    acc = pltpu.VMEM((GROUP_ROWS, width + LANES), jnp.float32)

    def first(block, state):
        return pl.pallas_call(
            functools.partial(first_kernel, block),
            out_shape=partial,
            in_specs=[SMEM] + [VMEM] * 4,
            out_specs=VMEM,
            scratch_shapes=[acc],
        )(meta, readings, own, other, state)

    def step(block, parts, state, coeff, decay, meta=meta):
        return pl.pallas_call(
            functools.partial(step_kernel, block, len(parts)),
            out_shape=(vector, vector, partial),
            in_specs=[VMEM] * len(parts) + [SMEM] + [VMEM] * 6,
            out_specs=(VMEM, VMEM, VMEM),
            scratch_shapes=[acc],
        )(*parts, meta, readings, own, other, state, coeff, decay)

    def last(parts, state, coeff, decay):
        return pl.pallas_call(
            functools.partial(last_kernel, len(parts)),
            out_shape=(vector, vector),
            in_specs=[VMEM] * (len(parts) + 3),
            out_specs=(VMEM, VMEM),
        )(*parts, state, coeff, decay)

    def exchange(part, group):
        parts = [part]
        for shift in range(1, tm_size):
            pairs = [
                (i * grp_size + group, (i + shift) % tm_size * grp_size + group)
                for i in range(tm_size)
            ]
            parts.append(lax.ppermute(part, ("tm", "grp"), pairs))
        return parts

    def coefficients(position):
        return gathered[position][0:1], gathered[position][1:2]

    def group_direct(state, group):
        states, innovations = [], []
        part = first(0, state)
        for block in range(tm_size):
            parts = exchange(part, group)
            if block < tm_size - 1:
                state, innovation, part = step(block + 1, parts, state, *coefficients(block))
            else:
                state, innovation = last(parts, state, *coefficients(block))
            states.append(state)
            innovations.append(innovation)
        return jnp.concatenate(states, 0), jnp.concatenate(innovations, 0)

    def group_loop(state, group):
        part = first(0, state)

        def lap(block, carry):
            state, part, states, innovations = carry
            here = lax.dynamic_index_in_dim(gathered, block, 0, False)
            own_meta = jnp.concatenate([meta, (block + 1)[None].astype(jnp.int32)])
            state, innovation, part = step(
                None, [lax.psum(part, "tm")], state, here[0:1], here[1:2], own_meta
            )
            states = lax.dynamic_update_slice_in_dim(states, state, block, 0)
            innovations = lax.dynamic_update_slice_in_dim(innovations, innovation, block, 0)
            return state, part, states, innovations

        empty = jnp.zeros((tm_size, width), jnp.float32)
        return lax.fori_loop(0, tm_size, lap, (state, part, empty, empty))[2:]

    states = innovations = jnp.zeros((tm_size, width), jnp.float32)
    for group in range(grp_size):
        new_states, new_innovations = (group_direct if direct else group_loop)(state, group)
        mine = grp_index == group
        states = jnp.where(mine, new_states, states)
        innovations = jnp.where(mine, new_innovations, innovations)
        if group < grp_size - 1:
            state = lax.ppermute(new_states[-1:], "grp", [(group, group + 1)])

    gains = gathered[:, 2]
    residual = jnp.zeros((1, width), jnp.float32)
    residuals = [None] * tm_size
    for group in reversed(range(grp_size)):
        running = residual
        for block in reversed(range(tm_size)):
            residuals[block] = running
            running = gains[block][None] * (running + innovations[block][None])
        if group > 0:
            arrived = lax.ppermute(running, "grp", [(group, group - 1)])
            residual = jnp.where(grp_index == group - 1, arrived, residual)
    smoothed = states + jnp.concatenate(residuals, 0)

    def out(values):
        piece = lax.dynamic_slice(values, (tm_index, core * half), (1, half))
        return piece.reshape(1, 1, half)

    return out(states), out(smoothed)


def solution(mesh):
    return jax.shard_map(
        shards,
        mesh=mesh,
        in_specs=(
            P(("runs", "grp"), "tm", None, "state"),
            P(("runs", "grp"), "tm", None),
            P(("runs", "grp"), "tm", None),
            P(("runs", "grp"), "tm"),
            P(("runs", "grp"), "tm", None),
            P(("runs", "grp"), "tm", None),
            P(("runs", "grp"), "tm", None),
            P("runs"),
        ),
        out_specs=(P(("runs", "grp"), "tm", "state"), P(("runs", "grp"), "tm", "state")),
        check_vma=False,
    )
```

```python
import functools

import jax
import jax.numpy as jnp
from jax import lax
from jax.experimental import pallas as pl
from jax.experimental.pallas import tpu as pltpu
from jax.sharding import PartitionSpec as P

STEPS = 4
LANES = 128
GROUP_ROWS = 16
DIRECT_TM = 4

VMEM = pl.BlockSpec(memory_space=pltpu.VMEM)
KERNEL = pltpu.CompilerParams(vmem_limit_bytes=8 * 2**20)
SMEM = pl.BlockSpec(memory_space=pltpu.SMEM)


def stencil(field, coeff, decay):
    width = field.shape[1]
    cell = lax.broadcasted_iota(jnp.int32, field.shape, 1)
    for _ in range(STEPS):
        upper_cell = jnp.where(cell == 0, 0.0, pltpu.roll(field, 1, 1))
        lower_cell = jnp.where(cell == width - 1, 0.0, pltpu.roll(field, width - 1, 1))
        field = field + coeff * (upper_cell + lower_cell - 2.0 * field) - decay * field
    return field


def row_pass(block, state, meta, y_ref, own_ref, other_ref, acc, part_ref):
    tile_num, row_num, half = own_ref.shape
    core = meta[2 * tile_num]
    own_at = pl.multiple_of(core * half, half)
    other_at = pl.multiple_of((1 - core) * half, half)
    state_own = state[:, pl.ds(own_at, half)]
    state_other = state[:, pl.ds(other_at, half)]
    lane = lax.broadcasted_iota(jnp.int32, (GROUP_ROWS, LANES), 1)
    row = lax.broadcasted_iota(jnp.int32, (GROUP_ROWS, LANES), 0)
    acc[...] = jnp.zeros_like(acc)

    def fold(values):
        total = values[:, :LANES]
        for start in range(LANES, half, LANES):
            total = total + values[:, start : start + LANES]
        return total

    def tile(index, carry):
        @pl.when(meta[index] == block)
        def _():
            live = meta[tile_num + index]
            readings = y_ref[pl.ds(index, 1), :]
            sum_own = jnp.zeros((GROUP_ROWS, half), jnp.float32)
            sum_other = jnp.zeros((GROUP_ROWS, half), jnp.float32)
            squares = jnp.zeros((GROUP_ROWS, LANES), jnp.float32)
            for start in range(0, row_num, GROUP_ROWS):
                own = own_ref[index, start : start + GROUP_ROWS, :].astype(jnp.float32)
                other = other_ref[index, start : start + GROUP_ROWS, :].astype(jnp.float32)
                valid = row + start < live
                product = fold(own * state_own) + fold(other * state_other)
                product = product - jnp.where(lane == row + start, readings, 0.0)
                weight = jnp.sum(product, axis=1, keepdims=True)
                weight = jnp.where(valid[:, :1], weight, 0.0)
                sum_own = sum_own + own * weight
                sum_other = sum_other + other * weight
                squares = squares + jnp.where(valid, fold(own * own) + fold(other * other), 0.0)
            acc[:, :half] += sum_own
            acc[:, half : 2 * half] += sum_other
            acc[:, 2 * half :] += squares

        return carry

    lax.fori_loop(0, tile_num, tile, 0)
    totals = jnp.sum(acc[...], axis=0, keepdims=True)
    part_ref[:, pl.ds(own_at, half)] = totals[:, :half]
    part_ref[:, pl.ds(other_at, half)] = totals[:, half : 2 * half]
    part_ref[:, 2 * half :] = totals[:, 2 * half :]


def first_kernel(block, meta, y_ref, own_ref, other_ref, state_ref, part_ref, acc):
    row_pass(block, state_ref, meta, y_ref, own_ref, other_ref, acc, part_ref)


def advance(parts, state, kappa_ref, rate_ref):
    total = parts[0][...]
    for part in parts[1:]:
        total = total + part[...]
    width = state.shape[1]
    trace_val = jnp.sum(total[:, width:], axis=1, keepdims=True)
    lam_val = width / (2.0 * (width + trace_val))
    innovation = -lam_val * stencil(total[:, :width], kappa_ref, rate_ref)
    return stencil(state, kappa_ref, rate_ref) + innovation, innovation


def step_kernel(block, number, *refs):
    parts, rest = refs[:number], refs[number:]
    meta, y_ref, own_ref, other_ref, state_ref, kappa_ref, rate_ref = rest[:7]
    next_ref, innovation_ref, part_ref, acc = rest[7:]
    updated, innovation = advance(parts, state_ref[...], kappa_ref[...], rate_ref[...])
    next_ref[...] = updated
    innovation_ref[...] = innovation
    if block is None:
        block = meta[2 * y_ref.shape[0] + 1]
    row_pass(block, next_ref, meta, y_ref, own_ref, other_ref, acc, part_ref)


def last_kernel(number, *refs):
    parts, (state_ref, kappa_ref, rate_ref, next_ref, innovation_ref) = refs[:number], refs[number:]
    updated, innovation = advance(parts, state_ref[...], kappa_ref[...], rate_ref[...])
    next_ref[...] = updated
    innovation_ref[...] = innovation


def shards(rows_h, rows_y, tile_block, tile_count, kappa, rate, smooth_gain, start_state):
    tm_size, grp_size = lax.axis_size("tm"), lax.axis_size("grp")
    state_size = lax.axis_size("state")
    tm_index, grp_index, core = (lax.axis_index(name) for name in ("tm", "grp", "state"))
    tile_num, half = rows_h.shape[1], rows_h.shape[3]
    width = kappa.shape[2]
    own = rows_h[0]
    other = lax.ppermute(own, "state", [(i, (i + 1) % state_size) for i in range(state_size)])
    readings = rows_y[0].astype(jnp.float32)
    meta = jnp.concatenate([tile_block[0, :, 0], tile_count[0], core[None].astype(jnp.int32)])
    state = start_state.reshape(1, width)
    direct = tm_size <= DIRECT_TM and tm_size & (tm_size - 1) == 0

    def exchange(part):
        parts = [part]
        for flip in range(1, tm_size):
            parts.append(lax.ppermute(part, "tm", [(i, i ^ flip) for i in range(tm_size)]))
        return parts

    params = jnp.concatenate([kappa[0], rate[0], smooth_gain[0]], axis=0)
    if direct:
        pieces = jnp.stack(exchange(params))
        gathered = pieces[jnp.arange(tm_size) ^ tm_index]
    else:
        gathered = lax.all_gather(params, "tm")

    vector = jax.ShapeDtypeStruct((1, width), jnp.float32)
    partial = jax.ShapeDtypeStruct((1, width + LANES), jnp.float32)
    acc = pltpu.VMEM((GROUP_ROWS, width + LANES), jnp.float32)

    def first(block, state):
        return pl.pallas_call(
            functools.partial(first_kernel, block),
            out_shape=partial,
            in_specs=[SMEM] + [VMEM] * 4,
            out_specs=VMEM,
            scratch_shapes=[acc],
            compiler_params=KERNEL,
        )(meta, readings, own, other, state)

    def step(block, parts, state, coeff, decay, meta=meta):
        return pl.pallas_call(
            functools.partial(step_kernel, block, len(parts)),
            out_shape=(vector, vector, partial),
            in_specs=[VMEM] * len(parts) + [SMEM] + [VMEM] * 6,
            out_specs=(VMEM, VMEM, VMEM),
            scratch_shapes=[acc],
            compiler_params=KERNEL,
        )(*parts, meta, readings, own, other, state, coeff, decay)

    def last(parts, state, coeff, decay):
        return pl.pallas_call(
            functools.partial(last_kernel, len(parts)),
            out_shape=(vector, vector),
            in_specs=[VMEM] * (len(parts) + 3),
            out_specs=(VMEM, VMEM),
            compiler_params=KERNEL,
        )(*parts, state, coeff, decay)

    def coefficients(position):
        return gathered[position][0:1], gathered[position][1:2]

    def group_direct(state):
        states, innovations = [], []
        part = first(0, state)
        for block in range(tm_size):
            parts = exchange(part)
            if block < tm_size - 1:
                state, innovation, part = step(block + 1, parts, state, *coefficients(block))
            else:
                state, innovation = last(parts, state, *coefficients(block))
            states.append(state)
            innovations.append(innovation)
        return jnp.concatenate(states, 0), jnp.concatenate(innovations, 0)

    def group_loop(state):
        part = first(0, state)

        def lap(block, carry):
            state, part, states, innovations = carry
            here = lax.dynamic_index_in_dim(gathered, block, 0, False)
            own_meta = jnp.concatenate([meta, (block + 1)[None].astype(jnp.int32)])
            state, innovation, part = step(
                None, [lax.psum(part, "tm")], state, here[0:1], here[1:2], own_meta
            )
            states = lax.dynamic_update_slice_in_dim(states, state, block, 0)
            innovations = lax.dynamic_update_slice_in_dim(innovations, innovation, block, 0)
            return state, part, states, innovations

        empty = jnp.zeros((tm_size, width), jnp.float32)
        return lax.fori_loop(0, tm_size, lap, (state, part, empty, empty))[2:]

    states = innovations = jnp.zeros((tm_size, width), jnp.float32)
    for group in range(grp_size):
        new_states, new_innovations = (group_direct if direct else group_loop)(state)
        mine = grp_index == group
        states = jnp.where(mine, new_states, states)
        innovations = jnp.where(mine, new_innovations, innovations)
        if group < grp_size - 1:
            state = lax.ppermute(new_states[-1:], "grp", [(group, group + 1)])

    gains = gathered[:, 2]
    residual = jnp.zeros((1, width), jnp.float32)
    residuals = [None] * tm_size
    for group in reversed(range(grp_size)):
        running = residual
        for block in reversed(range(tm_size)):
            residuals[block] = running
            running = gains[block][None] * (running + innovations[block][None])
        if group > 0:
            arrived = lax.ppermute(running, "grp", [(group, group - 1)])
            residual = jnp.where(grp_index == group - 1, arrived, residual)
    smoothed = states + jnp.concatenate(residuals, 0)

    def out(values):
        piece = lax.dynamic_slice(values, (tm_index, core * half), (1, half))
        return piece.reshape(1, 1, half)

    return out(states), out(smoothed)


def solution(mesh):
    return jax.shard_map(
        shards,
        mesh=mesh,
        in_specs=(
            P(("runs", "grp"), "tm", None, "state"),
            P(("runs", "grp"), "tm", None),
            P(("runs", "grp"), "tm", None),
            P(("runs", "grp"), "tm"),
            P(("runs", "grp"), "tm", None),
            P(("runs", "grp"), "tm", None),
            P(("runs", "grp"), "tm", None),
            P("runs"),
        ),
        out_specs=(P(("runs", "grp"), "tm", "state"), P(("runs", "grp"), "tm", "state")),
        check_vma=False,
    )
```

```python
import functools

import jax
import jax.numpy as jnp
from jax import lax
from jax.experimental import pallas as pl
from jax.experimental.pallas import tpu as pltpu
from jax.sharding import PartitionSpec as P

STEPS = 4
LANES = 128
GROUP_ROWS = 16
DIRECT_TM = 4

VMEM = pl.BlockSpec(memory_space=pltpu.VMEM)
KERNEL = pltpu.CompilerParams(vmem_limit_bytes=16 * 2**20)
SMEM = pl.BlockSpec(memory_space=pltpu.SMEM)


def stencil(field, coeff, decay):
    width = field.shape[1]
    cell = lax.broadcasted_iota(jnp.int32, field.shape, 1)
    for _ in range(STEPS):
        upper_cell = jnp.where(cell == 0, 0.0, pltpu.roll(field, 1, 1))
        lower_cell = jnp.where(cell == width - 1, 0.0, pltpu.roll(field, width - 1, 1))
        field = field + coeff * (upper_cell + lower_cell - 2.0 * field) - decay * field
    return field


def row_pass(block, state, meta, y_ref, own_ref, other_ref, acc, part_ref):
    tile_num, row_num, half = own_ref.shape
    core = meta[2 * tile_num]
    own_at = pl.multiple_of(core * half, half)
    other_at = pl.multiple_of((1 - core) * half, half)
    state_own = state[:, pl.ds(own_at, half)]
    state_other = state[:, pl.ds(other_at, half)]
    lane = lax.broadcasted_iota(jnp.int32, (GROUP_ROWS, LANES), 1)
    row = lax.broadcasted_iota(jnp.int32, (GROUP_ROWS, LANES), 0)
    acc[...] = jnp.zeros_like(acc)

    def fold(values):
        total = values[:, :LANES]
        for start in range(LANES, half, LANES):
            total = total + values[:, start : start + LANES]
        return total

    def tile(index, carry):
        @pl.when(meta[index] == block)
        def _():
            live = meta[tile_num + index]
            readings = y_ref[pl.ds(index, 1), :]
            sum_own = jnp.zeros((GROUP_ROWS, half), jnp.float32)
            sum_other = jnp.zeros((GROUP_ROWS, half), jnp.float32)
            squares = jnp.zeros((GROUP_ROWS, LANES), jnp.float32)
            for start in range(0, row_num, GROUP_ROWS):
                own = own_ref[index, start : start + GROUP_ROWS, :].astype(jnp.float32)
                other = other_ref[index, start : start + GROUP_ROWS, :].astype(jnp.float32)
                valid = row + start < live
                product = fold(own * state_own) + fold(other * state_other)
                product = product - jnp.where(lane == row + start, readings, 0.0)
                weight = jnp.sum(product, axis=1, keepdims=True)
                weight = jnp.where(valid[:, :1], weight, 0.0)
                sum_own = sum_own + own * weight
                sum_other = sum_other + other * weight
                squares = squares + jnp.where(valid, fold(own * own) + fold(other * other), 0.0)
            acc[:, :half] += sum_own
            acc[:, half : 2 * half] += sum_other
            acc[:, 2 * half :] += squares

        return carry

    lax.fori_loop(0, tile_num, tile, 0)
    totals = jnp.sum(acc[...], axis=0, keepdims=True)
    part_ref[:, pl.ds(own_at, half)] = totals[:, :half]
    part_ref[:, pl.ds(other_at, half)] = totals[:, half : 2 * half]
    part_ref[:, 2 * half :] = totals[:, 2 * half :]


def first_kernel(block, meta, y_ref, own_ref, other_ref, state_ref, part_ref, acc):
    row_pass(block, state_ref, meta, y_ref, own_ref, other_ref, acc, part_ref)


def step_kernel(
    total_ref, meta, y_ref, own_ref, other_ref, state_ref, kappa_ref, rate_ref,
    next_ref, innovation_ref, part_ref, acc,
):
    width = state_ref.shape[1]
    trace_val = jnp.sum(total_ref[:, width:], axis=1, keepdims=True)
    lam_val = width / (2.0 * (width + trace_val))
    coeff, decay = kappa_ref[...], rate_ref[...]
    innovation = -lam_val * stencil(total_ref[:, :width], coeff, decay)
    next_ref[...] = stencil(state_ref[...], coeff, decay) + innovation
    innovation_ref[...] = innovation
    block = meta[2 * y_ref.shape[0] + 1]
    row_pass(block, next_ref, meta, y_ref, own_ref, other_ref, acc, part_ref)


def gram_kernel(meta, y_ref, own_ref, other_ref, params_ref, *refs):
    outs, side_ref, acc, vec = refs[:-3], refs[-3], refs[-2], refs[-1]
    tile_num, row_num, half = own_ref.shape
    block_num = len(outs)
    core, position = meta[2 * tile_num], meta[2 * tile_num + 1]
    acc[...] = jnp.zeros_like(acc)
    vec[...] = jnp.zeros_like(vec)
    row = lax.broadcasted_iota(jnp.int32, (row_num, half), 0)
    over_rows = (((0,), (0,)), ((), ()))

    def tile(index, carry):
        block = meta[index]
        live = meta[tile_num + index]
        rows = own_ref[index].astype(jnp.float32)
        rows = jnp.where(row < live, rows, 0.0).astype(jnp.bfloat16)
        readings = jnp.broadcast_to(y_ref[pl.ds(index, 1), :], (8, row_num)).astype(jnp.bfloat16)
        square = lax.dot_general(rows, rows, over_rows, preferred_element_type=jnp.float32)
        acc[block, 0:LANES] += square[:LANES, :LANES]
        acc[block, LANES : 2 * LANES] += square[:LANES, LANES:]
        acc[block, 2 * LANES : 3 * LANES] += square[LANES:, LANES:]
        for piece in range(2):
            at = pl.multiple_of((piece ^ core) * LANES, LANES)
            acc[block, (3 + piece) * LANES : (4 + piece) * LANES] += lax.dot_general(
                rows[:, piece * LANES : (piece + 1) * LANES],
                other_ref[index, :, pl.ds(at, LANES)],
                over_rows,
                preferred_element_type=jnp.float32,
            )
        vec[block] += jnp.dot(readings, rows, preferred_element_type=jnp.float32)
        return carry

    lax.fori_loop(0, tile_num, tile, 0, unroll=2)
    on_diagonal = lax.broadcasted_iota(jnp.int32, (LANES, LANES), 0) == lax.broadcasted_iota(
        jnp.int32, (LANES, LANES), 1
    )
    for flip, out_ref in enumerate(outs):
        block = position ^ flip
        for piece in range(5):
            values = acc[block, piece * LANES : (piece + 1) * LANES]
            if piece in (0, 2):
                side_ref[block, 0:1, (piece // 2) * LANES : (piece // 2 + 1) * LANES] = jnp.sum(
                    jnp.where(on_diagonal, values, 0.0), axis=0, keepdims=True
                )
                values = jnp.where(on_diagonal, 0.0, values)
            out_ref[piece * LANES : (piece + 1) * LANES] = values.astype(jnp.bfloat16)
    for block in range(block_num):
        side_ref[block, 1:2, :] = vec[block, 0:1, :]
    for which in range(3):
        for piece in range(2):
            side_ref[block_num + which, piece : piece + 1, :] = params_ref[
                which : which + 1, piece * half : (piece + 1) * half
            ]


def sum_kernel(*refs):
    total = refs[0][...].astype(jnp.float32)
    for part in refs[1:-1]:
        total = total + part[...].astype(jnp.float32)
    refs[-1][...] = total.astype(jnp.bfloat16)


def chain(grams, diag, info, kappa, rate, state, states_ref, innovations_ref):
    width = state.shape[1]
    line = lax.broadcasted_iota(jnp.int32, (16, width), 0)
    for block in range(grams.shape[0]):
        high = state.astype(jnp.bfloat16).astype(jnp.float32)
        middle = (state - high).astype(jnp.bfloat16).astype(jnp.float32)
        low = state - high - middle
        split = jnp.where(line == 0, high, jnp.where(line == 1, middle, jnp.where(line == 2, low, 0.0)))
        product = jnp.dot(
            split.astype(jnp.bfloat16), grams[block], preferred_element_type=jnp.float32
        )
        diagonal = diag[block : block + 1, :]
        product = jnp.sum(product, axis=0, keepdims=True) + diagonal * state
        trace_val = jnp.sum(diagonal, axis=1, keepdims=True)
        lam_val = width / (2.0 * (width + trace_val))
        coeff, decay = kappa[block : block + 1, :], rate[block : block + 1, :]
        innovation = -lam_val * stencil(product - info[block : block + 1, :], coeff, decay)
        state = stencil(state, coeff, decay) + innovation
        states_ref[block : block + 1, :] = state
        innovations_ref[block : block + 1, :] = innovation


def assemble_kernel(number, *refs):
    own, other, rest = refs[:number], refs[number : 2 * number], refs[2 * number :]
    where, diag, info, kappa, rate, state_ref, grams, states_ref, innovations_ref = rest
    core, position = where[0], where[1]
    half = 2 * LANES
    for flip in range(number):
        block = position ^ flip
        for pieces, side in ((own[flip], core), (other[flip], 1 - core)):
            def piece(index):
                return pieces[index * LANES : (index + 1) * LANES, :]

            def put(row, column, values):
                row, column = pl.multiple_of(row, LANES), pl.multiple_of(column, LANES)
                grams[block, pl.ds(row, LANES), pl.ds(column, LANES)] = values

            here, there = side * half, (1 - side) * half
            put(here, here, piece(0))
            put(here, here + LANES, piece(1))
            put(here + LANES, here, piece(1).T)
            put(here + LANES, here + LANES, piece(2))
            for index in range(2):
                across = there + (index ^ side) * LANES
                put(here + index * LANES, across, piece(3 + index))
                put(across, here + index * LANES, piece(3 + index).T)
    chain(grams, diag, info, kappa, rate, state_ref[...], states_ref, innovations_ref)


def chain_kernel(grams, diag, info, kappa, rate, state_ref, states_ref, innovations_ref):
    chain(grams, diag, info, kappa, rate, state_ref[...], states_ref, innovations_ref)


def shards(rows_h, rows_y, tile_block, tile_count, kappa, rate, smooth_gain, start_state):
    tm_size, grp_size = lax.axis_size("tm"), lax.axis_size("grp")
    state_size = lax.axis_size("state")
    tm_index, grp_index, core = (lax.axis_index(name) for name in ("tm", "grp", "state"))
    tile_num, half = rows_h.shape[1], rows_h.shape[3]
    width = kappa.shape[2]
    own = rows_h[0]
    other = lax.ppermute(own, "state", [(i, (i + 1) % state_size) for i in range(state_size)])
    readings = rows_y[0].astype(jnp.float32)
    state = start_state.reshape(1, width)
    meta = jnp.concatenate(
        [tile_block[0, :, 0], tile_count[0], jnp.stack([core, tm_index]).astype(jnp.int32)]
    )
    params = jnp.concatenate([kappa[0], rate[0], smooth_gain[0]], axis=0)
    direct = tm_size <= DIRECT_TM and tm_size & (tm_size - 1) == 0
    states_shape = jax.ShapeDtypeStruct((tm_size, width), jnp.float32)

    def flip_over(array, flip):
        return lax.ppermute(array, "tm", [(i, i ^ flip) for i in range(tm_size)])

    def across(array):
        return lax.ppermute(array, "state", [(i, (i + 1) % state_size) for i in range(state_size)])

    if direct:
        packed = jax.ShapeDtypeStruct((5 * LANES, LANES), jnp.bfloat16)
        *pieces, side = pl.pallas_call(
            gram_kernel,
            out_shape=[packed] * tm_size
            + [jax.ShapeDtypeStruct((tm_size + 3, 2, half), jnp.float32)],
            in_specs=[SMEM] + [VMEM] * 4,
            out_specs=[VMEM] * (tm_size + 1),
            scratch_shapes=[
                pltpu.VMEM((tm_size, 5 * LANES, LANES), jnp.float32),
                pltpu.VMEM((tm_size, 8, half), jnp.float32),
            ],
            compiler_params=KERNEL,
        )(meta, readings, own, other, params)
        parts = pieces[:1] + [flip_over(pieces[flip], flip) for flip in range(1, tm_size)]

        sides = [side] + [flip_over(side, flip) for flip in range(1, tm_size)]
        side_sum = sum(values[:tm_size] for values in sides)
        side_other = across(side_sum)
        low = jnp.where(core == 0, side_sum, side_other)
        high = jnp.where(core == 0, side_other, side_sum)
        vectors = jnp.concatenate([low, high], axis=2)
        diag, info = vectors[:, 0], vectors[:, 1]
        order = jnp.arange(tm_size) ^ tm_index
        gathered = jnp.stack([values[tm_size:].reshape(3, width) for values in sides])[order]

        own_sum = pl.pallas_call(
            sum_kernel,
            out_shape=packed,
            in_specs=[VMEM] * tm_size,
            out_specs=VMEM,
            compiler_params=KERNEL,
        )(*parts)
        own_sums = [own_sum] + [flip_over(own_sum, flip) for flip in range(1, tm_size)]
        other_sums = [across(values) for values in own_sums]
        coefficients = (diag, info, gathered[:, 0], gathered[:, 1])
        grams, new_states, new_innovations = pl.pallas_call(
            functools.partial(assemble_kernel, tm_size),
            out_shape=(
                jax.ShapeDtypeStruct((tm_size, width, width), jnp.bfloat16),
                states_shape,
                states_shape,
            ),
            in_specs=[VMEM] * (2 * tm_size) + [SMEM] + [VMEM] * 5,
            out_specs=(VMEM, VMEM, VMEM),
            compiler_params=KERNEL,
        )(*own_sums, *other_sums, meta[2 * tile_num :], *coefficients, state)

        def run_group(state, group):
            if group == 0:
                return new_states, new_innovations
            return pl.pallas_call(
                chain_kernel,
                out_shape=(states_shape, states_shape),
                in_specs=[VMEM] * 6,
                out_specs=(VMEM, VMEM),
                compiler_params=KERNEL,
            )(grams, *coefficients, state)
    else:
        gathered = lax.all_gather(params, "tm")
        vector = jax.ShapeDtypeStruct((1, width), jnp.float32)
        partial = jax.ShapeDtypeStruct((1, width + LANES), jnp.float32)
        acc = pltpu.VMEM((GROUP_ROWS, width + LANES), jnp.float32)

        def run_group(state, group):
            part = pl.pallas_call(
                functools.partial(first_kernel, 0),
                out_shape=partial,
                in_specs=[SMEM] + [VMEM] * 4,
                out_specs=VMEM,
                scratch_shapes=[acc],
                compiler_params=KERNEL,
            )(meta, readings, own, other, state)

            def lap(block, carry):
                state, part, states, innovations = carry
                here = lax.dynamic_index_in_dim(gathered, block, 0, False)
                own_meta = meta.at[2 * tile_num + 1].set((block + 1).astype(jnp.int32))
                state, innovation, part = pl.pallas_call(
                    step_kernel,
                    out_shape=(vector, vector, partial),
                    in_specs=[VMEM, SMEM] + [VMEM] * 6,
                    out_specs=(VMEM, VMEM, VMEM),
                    scratch_shapes=[acc],
                    compiler_params=KERNEL,
                )(lax.psum(part, "tm"), own_meta, readings, own, other, state, here[0:1], here[1:2])
                states = lax.dynamic_update_slice_in_dim(states, state, block, 0)
                innovations = lax.dynamic_update_slice_in_dim(innovations, innovation, block, 0)
                return state, part, states, innovations

            empty = jnp.zeros((tm_size, width), jnp.float32)
            return lax.fori_loop(0, tm_size, lap, (state, part, empty, empty))[2:]

    states = innovations = jnp.zeros((tm_size, width), jnp.float32)
    for group in range(grp_size):
        new_states, new_innovations = run_group(state, group)
        mine = grp_index == group
        states = jnp.where(mine, new_states, states)
        innovations = jnp.where(mine, new_innovations, innovations)
        if group < grp_size - 1:
            state = lax.ppermute(new_states[-1:], "grp", [(group, group + 1)])

    gains = gathered[:, 2]
    residual = jnp.zeros((1, width), jnp.float32)
    residuals = [None] * tm_size
    for group in reversed(range(grp_size)):
        running = residual
        for block in reversed(range(tm_size)):
            residuals[block] = running
            running = gains[block][None] * (running + innovations[block][None])
        if group > 0:
            arrived = lax.ppermute(running, "grp", [(group, group - 1)])
            residual = jnp.where(grp_index == group - 1, arrived, residual)
    smoothed = states + jnp.concatenate(residuals, 0)

    def out(values):
        piece = lax.dynamic_slice(values, (tm_index, core * half), (1, half))
        return piece.reshape(1, 1, half)

    return out(states), out(smoothed)


def solution(mesh):
    return jax.shard_map(
        shards,
        mesh=mesh,
        in_specs=(
            P(("runs", "grp"), "tm", None, "state"),
            P(("runs", "grp"), "tm", None),
            P(("runs", "grp"), "tm", None),
            P(("runs", "grp"), "tm"),
            P(("runs", "grp"), "tm", None),
            P(("runs", "grp"), "tm", None),
            P(("runs", "grp"), "tm", None),
            P("runs"),
        ),
        out_specs=(P(("runs", "grp"), "tm", "state"), P(("runs", "grp"), "tm", "state")),
        check_vma=False,
    )
```

```python
import functools

import jax
import jax.numpy as jnp
from jax import lax
from jax.experimental import pallas as pl
from jax.experimental.pallas import tpu as pltpu
from jax.sharding import PartitionSpec as P

STEPS = 4
LANES = 128
GROUP_ROWS = 16
VECTORS = 10
DIRECT_TM = 4

VMEM = pl.BlockSpec(memory_space=pltpu.VMEM)
KERNEL = pltpu.CompilerParams(vmem_limit_bytes=16 * 2**20)
SMEM = pl.BlockSpec(memory_space=pltpu.SMEM)


def stencil(field, coeff, decay):
    width = field.shape[1]
    cell = lax.broadcasted_iota(jnp.int32, field.shape, 1)
    for _ in range(STEPS):
        upper_cell = jnp.where(cell == 0, 0.0, pltpu.roll(field, 1, 1))
        lower_cell = jnp.where(cell == width - 1, 0.0, pltpu.roll(field, width - 1, 1))
        field = field + coeff * (upper_cell + lower_cell - 2.0 * field) - decay * field
    return field


def row_pass(block, state, meta, y_ref, own_ref, other_ref, acc, part_ref):
    tile_num, row_num, half = own_ref.shape
    core = meta[2 * tile_num]
    own_at = pl.multiple_of(core * half, half)
    other_at = pl.multiple_of((1 - core) * half, half)
    state_own = state[:, pl.ds(own_at, half)]
    state_other = state[:, pl.ds(other_at, half)]
    lane = lax.broadcasted_iota(jnp.int32, (GROUP_ROWS, LANES), 1)
    row = lax.broadcasted_iota(jnp.int32, (GROUP_ROWS, LANES), 0)
    acc[...] = jnp.zeros_like(acc)

    def fold(values):
        total = values[:, :LANES]
        for start in range(LANES, half, LANES):
            total = total + values[:, start : start + LANES]
        return total

    def tile(index, carry):
        @pl.when(meta[index] == block)
        def _():
            live = meta[tile_num + index]
            readings = y_ref[pl.ds(index, 1), :]
            sum_own = jnp.zeros((GROUP_ROWS, half), jnp.float32)
            sum_other = jnp.zeros((GROUP_ROWS, half), jnp.float32)
            squares = jnp.zeros((GROUP_ROWS, LANES), jnp.float32)
            for start in range(0, row_num, GROUP_ROWS):
                own = own_ref[index, start : start + GROUP_ROWS, :].astype(jnp.float32)
                other = other_ref[index, start : start + GROUP_ROWS, :].astype(jnp.float32)
                valid = row + start < live
                product = fold(own * state_own) + fold(other * state_other)
                product = product - jnp.where(lane == row + start, readings, 0.0)
                weight = jnp.sum(product, axis=1, keepdims=True)
                weight = jnp.where(valid[:, :1], weight, 0.0)
                sum_own = sum_own + own * weight
                sum_other = sum_other + other * weight
                squares = squares + jnp.where(valid, fold(own * own) + fold(other * other), 0.0)
            acc[:, :half] += sum_own
            acc[:, half : 2 * half] += sum_other
            acc[:, 2 * half :] += squares

        return carry

    lax.fori_loop(0, tile_num, tile, 0)
    totals = jnp.sum(acc[...], axis=0, keepdims=True)
    part_ref[:, pl.ds(own_at, half)] = totals[:, :half]
    part_ref[:, pl.ds(other_at, half)] = totals[:, half : 2 * half]
    part_ref[:, 2 * half :] = totals[:, 2 * half :]


def first_kernel(block, meta, y_ref, own_ref, other_ref, state_ref, part_ref, acc):
    row_pass(block, state_ref, meta, y_ref, own_ref, other_ref, acc, part_ref)


def step_kernel(
    total_ref, meta, y_ref, own_ref, other_ref, state_ref, kappa_ref, rate_ref,
    next_ref, innovation_ref, part_ref, acc,
):
    width = state_ref.shape[1]
    trace_val = jnp.sum(total_ref[:, width:], axis=1, keepdims=True)
    lam_val = width / (2.0 * (width + trace_val))
    coeff, decay = kappa_ref[...], rate_ref[...]
    innovation = -lam_val * stencil(total_ref[:, :width], coeff, decay)
    next_ref[...] = stencil(state_ref[...], coeff, decay) + innovation
    innovation_ref[...] = innovation
    block = meta[2 * y_ref.shape[0] + 1]
    row_pass(block, next_ref, meta, y_ref, own_ref, other_ref, acc, part_ref)


def pieces_of(values):
    high = values.astype(jnp.bfloat16).astype(jnp.float32)
    middle = (values - high).astype(jnp.bfloat16).astype(jnp.float32)
    return high, middle, values - high - middle


def gram_kernel(meta, y_ref, own_ref, other_ref, *refs):
    outs, acc, vec, side = refs[:-3], refs[-3], refs[-2], refs[-1]
    tile_num, row_num, half = own_ref.shape
    core, position = meta[2 * tile_num], meta[2 * tile_num + 1]
    acc[...] = jnp.zeros_like(acc)
    vec[...] = jnp.zeros_like(vec)
    side[...] = jnp.zeros_like(side)
    row = lax.broadcasted_iota(jnp.int32, (row_num, half), 0)
    over_rows = (((0,), (0,)), ((), ()))

    def tile(index, carry):
        block = meta[index]
        live = meta[tile_num + index]
        rows = own_ref[index].astype(jnp.float32)
        rows = jnp.where(row < live, rows, 0.0).astype(jnp.bfloat16)
        readings = jnp.broadcast_to(y_ref[pl.ds(index, 1), :], (8, row_num)).astype(jnp.bfloat16)
        square = lax.dot_general(rows, rows, over_rows, preferred_element_type=jnp.float32)
        acc[block, 0:LANES] += square[:LANES, :LANES]
        acc[block, LANES : 2 * LANES] += square[:LANES, LANES:]
        acc[block, 2 * LANES : 3 * LANES] += square[LANES:, LANES:]
        for piece in range(2):
            at = pl.multiple_of((piece ^ core) * LANES, LANES)
            acc[block, (3 + piece) * LANES : (4 + piece) * LANES] += lax.dot_general(
                rows[:, piece * LANES : (piece + 1) * LANES],
                other_ref[index, :, pl.ds(at, LANES)],
                over_rows,
                preferred_element_type=jnp.float32,
            )
        vec[block] += jnp.dot(readings, rows, preferred_element_type=jnp.float32)
        return carry

    lax.fori_loop(0, tile_num, tile, 0, unroll=2)
    line = lax.broadcasted_iota(jnp.int32, (LANES, LANES), 0)
    column = lax.broadcasted_iota(jnp.int32, (LANES, LANES), 1)
    for flip, out_ref in enumerate(outs):
        block = position ^ flip

        def take(piece):
            return acc[block, piece * LANES : (piece + 1) * LANES]

        packed = jnp.where(line < column, take(0), jnp.where(line > column, take(2), 0.0))
        out_ref[0:LANES] = packed.astype(jnp.bfloat16)
        for at, piece in ((1, 1), (2, 3), (3, 4)):
            out_ref[at * LANES : (at + 1) * LANES] = take(piece).astype(jnp.bfloat16)
        values = [vec[block, 0:1, :LANES], vec[block, 0:1, LANES:]]
        for piece in (0, 2):
            values.append(
                jnp.sum(jnp.where(line == column, take(piece), 0.0), axis=0, keepdims=True)
            )
        for at, value in enumerate(values):
            for which, part in enumerate(pieces_of(value)):
                side[which * 4 + at : which * 4 + at + 1, :] = part
        out_ref[4 * LANES :] = side[...].astype(jnp.bfloat16)


def sum_kernel(meta, params_ref, *refs):
    parts, out_ref, side = refs[:-2], refs[-2], refs[-1]
    core = meta[meta.shape[0] - 2]
    total = parts[0][...].astype(jnp.float32)
    for part in parts[1:]:
        total = total + part[...].astype(jnp.float32)
    out_ref[: 4 * LANES] = total[: 4 * LANES].astype(jnp.bfloat16)
    below = total[4 * LANES :]
    values = [below[at : at + 1] + below[at + 4 : at + 5] + below[at + 8 : at + 9] for at in range(4)]
    for which in range(3):
        for piece in range(2):
            at = pl.multiple_of((2 * core + piece) * LANES, LANES)
            values.append(params_ref[which : which + 1, pl.ds(at, LANES)])
    side[...] = jnp.zeros_like(side)
    for at, value in enumerate(values):
        for which, part in enumerate(pieces_of(value)):
            side[which * VECTORS + at : which * VECTORS + at + 1, :] = part
    out_ref[4 * LANES :] = side[...].astype(jnp.bfloat16)


def chain(grams, vectors, state, states_ref, innovations_ref):
    width = state.shape[1]
    line = lax.broadcasted_iota(jnp.int32, (16, width), 0)
    for block in range(grams.shape[0]):
        info, diagonal, coeff, decay = (vectors[block, which : which + 1, :] for which in range(4))
        high, middle, low = pieces_of(state)
        split = jnp.where(line == 0, high, jnp.where(line == 1, middle, jnp.where(line == 2, low, 0.0)))
        product = jnp.dot(
            split.astype(jnp.bfloat16), grams[block], preferred_element_type=jnp.float32
        )
        product = jnp.sum(product, axis=0, keepdims=True) + diagonal * state
        trace_val = jnp.sum(diagonal, axis=1, keepdims=True)
        lam_val = width / (2.0 * (width + trace_val))
        innovation = -lam_val * stencil(product - info, coeff, decay)
        state = stencil(state, coeff, decay) + innovation
        states_ref[block : block + 1, :] = state
        innovations_ref[block : block + 1, :] = innovation


def assemble_kernel(number, meta, *refs):
    own, other, rest = refs[:number], refs[number : 2 * number], refs[2 * number :]
    state_ref, grams, vectors, states_ref, innovations_ref = rest
    core, position = meta[meta.shape[0] - 2], meta[meta.shape[0] - 1]
    half = 2 * LANES
    line = lax.broadcasted_iota(jnp.int32, (LANES, LANES), 0)
    column = lax.broadcasted_iota(jnp.int32, (LANES, LANES), 1)
    for flip in range(number):
        block = position ^ flip
        for pieces, side in ((own[flip], core), (other[flip], 1 - core)):

            def piece(index):
                return pieces[index * LANES : (index + 1) * LANES, :]

            def put(row, column, values):
                row, column = pl.multiple_of(row, LANES), pl.multiple_of(column, LANES)
                grams[block, pl.ds(row, LANES), pl.ds(column, LANES)] = values.astype(jnp.bfloat16)

            here, there = side * half, (1 - side) * half
            packed = piece(0).astype(jnp.float32)
            turned = packed.T
            put(here, here, jnp.where(line < column, packed, turned))
            put(here + LANES, here + LANES, jnp.where(line > column, packed, turned))
            put(here, here + LANES, piece(1))
            put(here + LANES, here, piece(1).T)
            for index in range(2):
                beyond = there + (index ^ side) * LANES
                put(here + index * LANES, beyond, piece(2 + index))
                put(beyond, here + index * LANES, piece(2 + index).T)
            below = pieces[4 * LANES :, :].astype(jnp.float32)
            below = below[:VECTORS] + below[VECTORS : 2 * VECTORS] + below[2 * VECTORS : 3 * VECTORS]
            for at in range(VECTORS):
                lanes = pl.ds(pl.multiple_of(here + (at % 2) * LANES, LANES), LANES)
                vectors[block, at // 2 : at // 2 + 1, lanes] = below[at : at + 1]
    chain(grams, vectors, state_ref[...], states_ref, innovations_ref)


def chain_kernel(grams, vectors, state_ref, states_ref, innovations_ref):
    chain(grams, vectors, state_ref[...], states_ref, innovations_ref)


def shards(rows_h, rows_y, tile_block, tile_count, kappa, rate, smooth_gain, start_state):
    tm_size, grp_size = lax.axis_size("tm"), lax.axis_size("grp")
    state_size = lax.axis_size("state")
    tm_index, grp_index, core = (lax.axis_index(name) for name in ("tm", "grp", "state"))
    tile_num, half = rows_h.shape[1], rows_h.shape[3]
    width = kappa.shape[2]
    own = rows_h[0]
    other = lax.ppermute(own, "state", [(i, (i + 1) % state_size) for i in range(state_size)])
    readings = rows_y[0].astype(jnp.float32)
    state = start_state.reshape(1, width)
    meta = jnp.concatenate(
        [tile_block[0, :, 0], tile_count[0], jnp.stack([core, tm_index]).astype(jnp.int32)]
    )
    params = jnp.concatenate([kappa[0], rate[0], smooth_gain[0]], axis=0)
    direct = tm_size <= DIRECT_TM and tm_size & (tm_size - 1) == 0
    states_shape = jax.ShapeDtypeStruct((tm_size, width), jnp.float32)

    def flip_over(array, flip):
        return lax.ppermute(array, "tm", [(i, i ^ flip) for i in range(tm_size)])

    def across(array):
        return lax.ppermute(array, "state", [(i, (i + 1) % state_size) for i in range(state_size)])

    if direct:
        sent = jax.ShapeDtypeStruct((4 * LANES + 16, LANES), jnp.bfloat16)
        pieces = pl.pallas_call(
            gram_kernel,
            out_shape=[sent] * tm_size,
            in_specs=[SMEM] + [VMEM] * 3,
            out_specs=[VMEM] * tm_size,
            scratch_shapes=[
                pltpu.VMEM((tm_size, 5 * LANES, LANES), jnp.float32),
                pltpu.VMEM((tm_size, 8, half), jnp.float32),
                pltpu.VMEM((16, LANES), jnp.float32),
            ],
            compiler_params=KERNEL,
        )(meta, readings, own, other)
        parts = [pieces[0]] + [flip_over(pieces[flip], flip) for flip in range(1, tm_size)]
        own_sum = pl.pallas_call(
            sum_kernel,
            out_shape=jax.ShapeDtypeStruct((4 * LANES + 32, LANES), jnp.bfloat16),
            in_specs=[SMEM] + [VMEM] * (tm_size + 1),
            out_specs=VMEM,
            scratch_shapes=[pltpu.VMEM((32, LANES), jnp.float32)],
            compiler_params=KERNEL,
        )(meta, params, *parts)
        own_sums = [own_sum] + [flip_over(own_sum, flip) for flip in range(1, tm_size)]
        other_sums = [across(values) for values in own_sums]
        grams, vectors, new_states, new_innovations = pl.pallas_call(
            functools.partial(assemble_kernel, tm_size),
            out_shape=(
                jax.ShapeDtypeStruct((tm_size, width, width), jnp.bfloat16),
                jax.ShapeDtypeStruct((tm_size, VECTORS // 2, width), jnp.float32),
                states_shape,
                states_shape,
            ),
            in_specs=[SMEM] + [VMEM] * (2 * tm_size + 1),
            out_specs=[VMEM] * 4,
            compiler_params=KERNEL,
        )(meta, *own_sums, *other_sums, state)
        gains = vectors[:, 4]

        def run_group(state, group):
            if group == 0:
                return new_states, new_innovations
            return pl.pallas_call(
                chain_kernel,
                out_shape=(states_shape, states_shape),
                in_specs=[VMEM] * 3,
                out_specs=(VMEM, VMEM),
                compiler_params=KERNEL,
            )(grams, vectors, state)
    else:
        gathered = lax.all_gather(params, "tm")
        gains = gathered[:, 2]
        vector = jax.ShapeDtypeStruct((1, width), jnp.float32)
        partial = jax.ShapeDtypeStruct((1, width + LANES), jnp.float32)
        acc = pltpu.VMEM((GROUP_ROWS, width + LANES), jnp.float32)

        def run_group(state, group):
            part = pl.pallas_call(
                functools.partial(first_kernel, 0),
                out_shape=partial,
                in_specs=[SMEM] + [VMEM] * 4,
                out_specs=VMEM,
                scratch_shapes=[acc],
                compiler_params=KERNEL,
            )(meta, readings, own, other, state)

            def lap(block, carry):
                state, part, states, innovations = carry
                here = lax.dynamic_index_in_dim(gathered, block, 0, False)
                own_meta = meta.at[2 * tile_num + 1].set((block + 1).astype(jnp.int32))
                state, innovation, part = pl.pallas_call(
                    step_kernel,
                    out_shape=(vector, vector, partial),
                    in_specs=[VMEM, SMEM] + [VMEM] * 6,
                    out_specs=(VMEM, VMEM, VMEM),
                    scratch_shapes=[acc],
                    compiler_params=KERNEL,
                )(lax.psum(part, "tm"), own_meta, readings, own, other, state, here[0:1], here[1:2])
                states = lax.dynamic_update_slice_in_dim(states, state, block, 0)
                innovations = lax.dynamic_update_slice_in_dim(innovations, innovation, block, 0)
                return state, part, states, innovations

            empty = jnp.zeros((tm_size, width), jnp.float32)
            return lax.fori_loop(0, tm_size, lap, (state, part, empty, empty))[2:]

    states = innovations = jnp.zeros((tm_size, width), jnp.float32)
    for group in range(grp_size):
        new_states, new_innovations = run_group(state, group)
        mine = grp_index == group
        states = jnp.where(mine, new_states, states)
        innovations = jnp.where(mine, new_innovations, innovations)
        if group < grp_size - 1:
            state = lax.ppermute(new_states[-1:], "grp", [(group, group + 1)])

    residual = jnp.zeros((1, width), jnp.float32)
    residuals = [None] * tm_size
    for group in reversed(range(grp_size)):
        running = residual
        for block in reversed(range(tm_size)):
            residuals[block] = running
            running = gains[block][None] * (running + innovations[block][None])
        if group > 0:
            arrived = lax.ppermute(running, "grp", [(group, group - 1)])
            residual = jnp.where(grp_index == group - 1, arrived, residual)
    smoothed = states + jnp.concatenate(residuals, 0)

    def out(values):
        piece = lax.dynamic_slice(values, (tm_index, core * half), (1, half))
        return piece.reshape(1, 1, half)

    return out(states), out(smoothed)


def solution(mesh):
    return jax.shard_map(
        shards,
        mesh=mesh,
        in_specs=(
            P(("runs", "grp"), "tm", None, "state"),
            P(("runs", "grp"), "tm", None),
            P(("runs", "grp"), "tm", None),
            P(("runs", "grp"), "tm"),
            P(("runs", "grp"), "tm", None),
            P(("runs", "grp"), "tm", None),
            P(("runs", "grp"), "tm", None),
            P("runs"),
        ),
        out_specs=(P(("runs", "grp"), "tm", "state"), P(("runs", "grp"), "tm", "state")),
        check_vma=False,
    )
```

```python
import functools

import jax
import jax.numpy as jnp
from jax import lax
from jax.experimental import pallas as pl
from jax.experimental.pallas import tpu as pltpu
from jax.sharding import PartitionSpec as P

STEPS = 4
LANES = 128
GROUP_ROWS = 16
VECTORS = 10
DIRECT_TM = 4

VMEM = pl.BlockSpec(memory_space=pltpu.VMEM)
KERNEL = pltpu.CompilerParams(vmem_limit_bytes=16 * 2**20)
SMEM = pl.BlockSpec(memory_space=pltpu.SMEM)


def stencil(field, coeff, decay):
    width = field.shape[1]
    cell = lax.broadcasted_iota(jnp.int32, field.shape, 1)
    for _ in range(STEPS):
        upper_cell = jnp.where(cell == 0, 0.0, pltpu.roll(field, 1, 1))
        lower_cell = jnp.where(cell == width - 1, 0.0, pltpu.roll(field, width - 1, 1))
        field = field + coeff * (upper_cell + lower_cell - 2.0 * field) - decay * field
    return field


def row_pass(block, state, meta, y_ref, own_ref, other_ref, acc, part_ref):
    tile_num, row_num, half = own_ref.shape
    core = meta[2 * tile_num]
    own_at = pl.multiple_of(core * half, half)
    other_at = pl.multiple_of((1 - core) * half, half)
    state_own = state[:, pl.ds(own_at, half)]
    state_other = state[:, pl.ds(other_at, half)]
    lane = lax.broadcasted_iota(jnp.int32, (GROUP_ROWS, LANES), 1)
    row = lax.broadcasted_iota(jnp.int32, (GROUP_ROWS, LANES), 0)
    acc[...] = jnp.zeros_like(acc)

    def fold(values):
        total = values[:, :LANES]
        for start in range(LANES, half, LANES):
            total = total + values[:, start : start + LANES]
        return total

    def tile(index, carry):
        @pl.when(meta[index] == block)
        def _():
            live = meta[tile_num + index]
            readings = y_ref[pl.ds(index, 1), :]
            sum_own = jnp.zeros((GROUP_ROWS, half), jnp.float32)
            sum_other = jnp.zeros((GROUP_ROWS, half), jnp.float32)
            squares = jnp.zeros((GROUP_ROWS, LANES), jnp.float32)
            for start in range(0, row_num, GROUP_ROWS):
                own = own_ref[index, start : start + GROUP_ROWS, :].astype(jnp.float32)
                other = other_ref[index, start : start + GROUP_ROWS, :].astype(jnp.float32)
                valid = row + start < live
                product = fold(own * state_own) + fold(other * state_other)
                product = product - jnp.where(lane == row + start, readings, 0.0)
                weight = jnp.sum(product, axis=1, keepdims=True)
                weight = jnp.where(valid[:, :1], weight, 0.0)
                sum_own = sum_own + own * weight
                sum_other = sum_other + other * weight
                squares = squares + jnp.where(valid, fold(own * own) + fold(other * other), 0.0)
            acc[:, :half] += sum_own
            acc[:, half : 2 * half] += sum_other
            acc[:, 2 * half :] += squares

        return carry

    lax.fori_loop(0, tile_num, tile, 0)
    totals = jnp.sum(acc[...], axis=0, keepdims=True)
    part_ref[:, pl.ds(own_at, half)] = totals[:, :half]
    part_ref[:, pl.ds(other_at, half)] = totals[:, half : 2 * half]
    part_ref[:, 2 * half :] = totals[:, 2 * half :]


def first_kernel(block, meta, y_ref, own_ref, other_ref, state_ref, part_ref, acc):
    row_pass(block, state_ref, meta, y_ref, own_ref, other_ref, acc, part_ref)


def step_kernel(
    total_ref, meta, y_ref, own_ref, other_ref, state_ref, kappa_ref, rate_ref,
    next_ref, innovation_ref, part_ref, acc,
):
    width = state_ref.shape[1]
    trace_val = jnp.sum(total_ref[:, width:], axis=1, keepdims=True)
    lam_val = width / (2.0 * (width + trace_val))
    coeff, decay = kappa_ref[...], rate_ref[...]
    innovation = -lam_val * stencil(total_ref[:, :width], coeff, decay)
    next_ref[...] = stencil(state_ref[...], coeff, decay) + innovation
    innovation_ref[...] = innovation
    block = meta[2 * y_ref.shape[0] + 1]
    row_pass(block, next_ref, meta, y_ref, own_ref, other_ref, acc, part_ref)


def pieces_of(values):
    high = values.astype(jnp.bfloat16).astype(jnp.float32)
    middle = (values - high).astype(jnp.bfloat16).astype(jnp.float32)
    return high, middle, values - high - middle


OVER_ROWS = (((0,), (0,)), ((), ()))


def valid_rows(index, counts, own_ref):
    rows = own_ref[index].astype(jnp.float32)
    row = lax.broadcasted_iota(jnp.int32, rows.shape, 0)
    return jnp.where(row < counts[0, index], rows, 0.0).astype(jnp.bfloat16)


def half_kernel(blocks, counts, y_ref, own_ref, out_ref, acc, vec, side, readings):
    tile_num = own_ref.shape[0]
    readings[...] = y_ref[...].astype(jnp.float32)
    acc[...] = jnp.zeros_like(acc)
    vec[...] = jnp.zeros_like(vec)
    side[...] = jnp.zeros_like(side)

    def tile(index, carry):
        block = blocks[index, 0]
        rows = valid_rows(index, counts, own_ref)
        values = jnp.broadcast_to(readings[pl.ds(index, 1), :], (8, rows.shape[0]))
        square = lax.dot_general(rows, rows, OVER_ROWS, preferred_element_type=jnp.float32)
        acc[block, 0:LANES] += square[:LANES, :LANES]
        acc[block, LANES : 2 * LANES] += square[:LANES, LANES:]
        acc[block, 2 * LANES : 3 * LANES] += square[LANES:, LANES:]
        vec[block] += jnp.dot(
            values.astype(jnp.bfloat16), rows, preferred_element_type=jnp.float32
        )
        return carry

    lax.fori_loop(0, tile_num, tile, 0, unroll=2)
    line = lax.broadcasted_iota(jnp.int32, (LANES, LANES), 0)
    column = lax.broadcasted_iota(jnp.int32, (LANES, LANES), 1)
    for block in range(out_ref.shape[0]):
        first, between, second = (acc[block, at * LANES : (at + 1) * LANES] for at in range(3))
        packed = jnp.where(line < column, first, jnp.where(line > column, second, 0.0))
        out_ref[block, 0:LANES] = packed.astype(jnp.bfloat16)
        out_ref[block, LANES : 2 * LANES] = between.astype(jnp.bfloat16)
        values = [vec[block, 0:1, :LANES], vec[block, 0:1, LANES:]]
        for square in (first, second):
            values.append(jnp.sum(jnp.where(line == column, square, 0.0), axis=0, keepdims=True))
        for at, value in enumerate(values):
            for which, part in enumerate(pieces_of(value)):
                side[which * 4 + at : which * 4 + at + 1, :] = part
        out_ref[block, 2 * LANES :] = side[...].astype(jnp.bfloat16)


def cross_kernel(flips, blocks, counts, own_ref, other_ref, half_ref, *refs):
    outs, acc = refs[:-1], refs[-1]
    core, position = lax.axis_index("state"), lax.axis_index("tm")
    acc[...] = jnp.zeros_like(acc)

    def tile(index, carry):
        for slot, flip in enumerate(flips):

            @pl.when(blocks[index, 0] == position ^ flip)
            def _():
                rows = valid_rows(index, counts, own_ref)
                for piece in range(2):
                    at = pl.multiple_of((piece ^ core) * LANES, LANES)
                    acc[slot, piece * LANES : (piece + 1) * LANES] += lax.dot_general(
                        rows[:, piece * LANES : (piece + 1) * LANES],
                        other_ref[index, :, pl.ds(at, LANES)],
                        OVER_ROWS,
                        preferred_element_type=jnp.float32,
                    )

        return carry

    lax.fori_loop(0, own_ref.shape[0], tile, 0)
    for slot, flip in enumerate(flips):
        block = position ^ flip
        outs[slot][: 2 * LANES] = half_ref[block, : 2 * LANES]
        outs[slot][2 * LANES : 4 * LANES] = acc[slot].astype(jnp.bfloat16)
        outs[slot][4 * LANES :] = half_ref[block, 2 * LANES :]


def sum_kernel(kappa_ref, rate_ref, gain_ref, *refs):
    parts, out_ref, side = refs[:-2], refs[-2], refs[-1]
    core = lax.axis_index("state")
    total = parts[0][...].astype(jnp.float32)
    for part in parts[1:]:
        total = total + part[...].astype(jnp.float32)
    out_ref[: 4 * LANES] = total[: 4 * LANES].astype(jnp.bfloat16)
    below = total[4 * LANES :]
    values = [below[at : at + 1] + below[at + 4 : at + 5] + below[at + 8 : at + 9] for at in range(4)]
    for coefficient in (kappa_ref, rate_ref, gain_ref):
        for piece in range(2):
            at = pl.multiple_of((2 * core + piece) * LANES, LANES)
            values.append(coefficient[:, pl.ds(at, LANES)])
    side[...] = jnp.zeros_like(side)
    for at, value in enumerate(values):
        for which, part in enumerate(pieces_of(value)):
            side[which * VECTORS + at : which * VECTORS + at + 1, :] = part
    out_ref[4 * LANES :] = side[...].astype(jnp.bfloat16)


def chain(grams, vectors, state, states_ref, innovations_ref):
    width = state.shape[1]
    line = lax.broadcasted_iota(jnp.int32, (16, width), 0)
    for block in range(grams.shape[0]):
        info, diagonal, coeff, decay = (vectors[block, which : which + 1, :] for which in range(4))
        high, middle, low = pieces_of(state)
        split = jnp.where(line == 0, high, jnp.where(line == 1, middle, jnp.where(line == 2, low, 0.0)))
        product = jnp.dot(
            split.astype(jnp.bfloat16), grams[block], preferred_element_type=jnp.float32
        )
        product = jnp.sum(product, axis=0, keepdims=True) + diagonal * state
        trace_val = jnp.sum(diagonal, axis=1, keepdims=True)
        lam_val = width / (2.0 * (width + trace_val))
        innovation = -lam_val * stencil(product - info, coeff, decay)
        state = stencil(state, coeff, decay) + innovation
        states_ref[block : block + 1, :] = state
        innovations_ref[block : block + 1, :] = innovation


def assemble_kernel(number, *refs):
    own, other, rest = refs[:number], refs[number : 2 * number], refs[2 * number :]
    state_ref, grams, vectors, states_ref, innovations_ref = rest
    core, position = lax.axis_index("state"), lax.axis_index("tm")
    half = 2 * LANES
    line = lax.broadcasted_iota(jnp.int32, (LANES, LANES), 0)
    column = lax.broadcasted_iota(jnp.int32, (LANES, LANES), 1)
    for flip in range(number):
        block = position ^ flip
        for pieces, side in ((own[flip], core), (other[flip], 1 - core)):

            def piece(index):
                return pieces[index * LANES : (index + 1) * LANES, :]

            def put(row, column, values):
                row, column = pl.multiple_of(row, LANES), pl.multiple_of(column, LANES)
                grams[block, pl.ds(row, LANES), pl.ds(column, LANES)] = values.astype(jnp.bfloat16)

            here, there = side * half, (1 - side) * half
            packed = piece(0).astype(jnp.float32)
            turned = packed.T
            put(here, here, jnp.where(line < column, packed, turned))
            put(here + LANES, here + LANES, jnp.where(line > column, packed, turned))
            put(here, here + LANES, piece(1))
            put(here + LANES, here, piece(1).T)
            for index in range(2):
                beyond = there + (index ^ side) * LANES
                put(here + index * LANES, beyond, piece(2 + index))
                put(beyond, here + index * LANES, piece(2 + index).T)
            below = pieces[4 * LANES :, :].astype(jnp.float32)
            below = below[:VECTORS] + below[VECTORS : 2 * VECTORS] + below[2 * VECTORS : 3 * VECTORS]
            for at in range(VECTORS):
                lanes = pl.ds(pl.multiple_of(here + (at % 2) * LANES, LANES), LANES)
                vectors[block, at // 2 : at // 2 + 1, lanes] = below[at : at + 1]
    chain(grams, vectors, state_ref[...], states_ref, innovations_ref)


def chain_kernel(grams, vectors, state_ref, states_ref, innovations_ref):
    chain(grams, vectors, state_ref[...], states_ref, innovations_ref)


def shards(rows_h, rows_y, tile_block, tile_count, kappa, rate, smooth_gain, start_state):
    tm_size, grp_size = lax.axis_size("tm"), lax.axis_size("grp")
    state_size = lax.axis_size("state")
    tm_index, grp_index, core = (lax.axis_index(name) for name in ("tm", "grp", "state"))
    tile_num, half = rows_h.shape[1], rows_h.shape[3]
    width = kappa.shape[2]
    own = rows_h[0]
    other = lax.ppermute(own, "state", [(i, (i + 1) % state_size) for i in range(state_size)])
    state = start_state.reshape(1, width)
    direct = tm_size <= DIRECT_TM and tm_size & (tm_size - 1) == 0
    states_shape = jax.ShapeDtypeStruct((tm_size, width), jnp.float32)

    def flip_over(array, flip):
        return lax.ppermute(array, "tm", [(i, i ^ flip) for i in range(tm_size)])

    def ring(array, step):
        return lax.ppermute(array, "grp", [(i, (i + step) % grp_size) for i in range(grp_size)])

    def across(array):
        return lax.ppermute(array, "state", [(i, (i + 1) % state_size) for i in range(state_size)])

    if direct:
        blocks = tile_block[0]
        part_of = pl.pallas_call(
            half_kernel,
            out_shape=jax.ShapeDtypeStruct((tm_size, 2 * LANES + 16, LANES), jnp.bfloat16),
            in_specs=[SMEM, SMEM, VMEM, VMEM],
            out_specs=VMEM,
            scratch_shapes=[
                pltpu.VMEM((tm_size, 3 * LANES, LANES), jnp.float32),
                pltpu.VMEM((tm_size, 8, half), jnp.float32),
                pltpu.VMEM((16, LANES), jnp.float32),
                pltpu.VMEM(rows_y.shape[1:], jnp.float32),
            ],
            compiler_params=KERNEL,
        )(blocks, tile_count, rows_y[0], own)

        def cross(flips):
            return pl.pallas_call(
                functools.partial(cross_kernel, flips),
                out_shape=[jax.ShapeDtypeStruct((4 * LANES + 16, LANES), jnp.bfloat16)] * len(flips),
                in_specs=[SMEM, SMEM] + [VMEM] * 3,
                out_specs=[VMEM] * len(flips),
                scratch_shapes=[pltpu.VMEM((len(flips), 2 * LANES, LANES), jnp.float32)],
                compiler_params=KERNEL,
            )(blocks, tile_count, own, other, part_of)

        order = list(reversed(range(tm_size)))
        parts = []
        for flips in (order[: tm_size // 2], order[tm_size // 2 :]):
            for flip, piece in zip(flips, cross(flips)):
                parts.append(piece if flip == 0 else flip_over(piece, flip))
        own_sum = pl.pallas_call(
            sum_kernel,
            out_shape=jax.ShapeDtypeStruct((4 * LANES + 32, LANES), jnp.bfloat16),
            in_specs=[VMEM] * (tm_size + 3),
            out_specs=VMEM,
            scratch_shapes=[pltpu.VMEM((32, LANES), jnp.float32)],
            compiler_params=KERNEL,
        )(kappa[0], rate[0], smooth_gain[0], *parts)
        own_sums = [own_sum] + [flip_over(own_sum, flip) for flip in range(1, tm_size)]
        other_sums = [across(values) for values in own_sums]
        grams, vectors, new_states, new_innovations = pl.pallas_call(
            functools.partial(assemble_kernel, tm_size),
            out_shape=(
                jax.ShapeDtypeStruct((tm_size, width, width), jnp.bfloat16),
                jax.ShapeDtypeStruct((tm_size, VECTORS // 2, width), jnp.float32),
                states_shape,
                states_shape,
            ),
            in_specs=[VMEM] * (2 * tm_size + 1),
            out_specs=[VMEM] * 4,
            compiler_params=KERNEL,
        )(*own_sums, *other_sums, state)
        gains = vectors[:, 4]

        def run_group(state, group):
            if group == 0:
                return new_states, new_innovations
            return pl.pallas_call(
                chain_kernel,
                out_shape=(states_shape, states_shape),
                in_specs=[VMEM] * 3,
                out_specs=(VMEM, VMEM),
                compiler_params=KERNEL,
            )(grams, vectors, state)
    else:
        readings = rows_y[0].astype(jnp.float32)
        meta = jnp.concatenate(
            [tile_block[0, :, 0], tile_count[0], jnp.stack([core, tm_index]).astype(jnp.int32)]
        )
        params = jnp.concatenate([kappa[0], rate[0], smooth_gain[0]], axis=0)
        gathered = lax.all_gather(params, "tm")
        gains = gathered[:, 2]
        vector = jax.ShapeDtypeStruct((1, width), jnp.float32)
        partial = jax.ShapeDtypeStruct((1, width + LANES), jnp.float32)
        acc = pltpu.VMEM((GROUP_ROWS, width + LANES), jnp.float32)

        def run_group(state, group):
            part = pl.pallas_call(
                functools.partial(first_kernel, 0),
                out_shape=partial,
                in_specs=[SMEM] + [VMEM] * 4,
                out_specs=VMEM,
                scratch_shapes=[acc],
                compiler_params=KERNEL,
            )(meta, readings, own, other, state)

            def lap(block, carry):
                state, part, states, innovations = carry
                here = lax.dynamic_index_in_dim(gathered, block, 0, False)
                own_meta = meta.at[2 * tile_num + 1].set((block + 1).astype(jnp.int32))
                state, innovation, part = pl.pallas_call(
                    step_kernel,
                    out_shape=(vector, vector, partial),
                    in_specs=[VMEM, SMEM] + [VMEM] * 6,
                    out_specs=(VMEM, VMEM, VMEM),
                    scratch_shapes=[acc],
                    compiler_params=KERNEL,
                )(lax.psum(part, "tm"), own_meta, readings, own, other, state, here[0:1], here[1:2])
                states = lax.dynamic_update_slice_in_dim(states, state, block, 0)
                innovations = lax.dynamic_update_slice_in_dim(innovations, innovation, block, 0)
                return state, part, states, innovations

            empty = jnp.zeros((tm_size, width), jnp.float32)
            return lax.fori_loop(0, tm_size, lap, (state, part, empty, empty))[2:]

    states = innovations = jnp.zeros((tm_size, width), jnp.float32)
    for group in range(grp_size):
        new_states, new_innovations = run_group(state, group)
        mine = grp_index == group
        states = jnp.where(mine, new_states, states)
        innovations = jnp.where(mine, new_innovations, innovations)
        if group < grp_size - 1:
            state = ring(new_states[-1:], 1)

    residual = jnp.zeros((1, width), jnp.float32)
    residuals = [None] * tm_size
    for group in reversed(range(grp_size)):
        running = residual
        for block in reversed(range(tm_size)):
            residuals[block] = running
            running = gains[block][None] * (running + innovations[block][None])
        if group > 0:
            arrived = ring(running, -1)
            residual = jnp.where(grp_index == group - 1, arrived, residual)
    smoothed = states + jnp.concatenate(residuals, 0)

    def out(values):
        piece = lax.dynamic_slice(values, (tm_index, core * half), (1, half))
        return piece.reshape(1, 1, half)

    return out(states), out(smoothed)


def solution(mesh):
    return jax.shard_map(
        shards,
        mesh=mesh,
        in_specs=(
            P(("runs", "grp"), "tm", None, "state"),
            P(("runs", "grp"), "tm", None),
            P(("runs", "grp"), "tm", None),
            P(("runs", "grp"), "tm"),
            P(("runs", "grp"), "tm", None),
            P(("runs", "grp"), "tm", None),
            P(("runs", "grp"), "tm", None),
            P("runs"),
        ),
        out_specs=(P(("runs", "grp"), "tm", "state"), P(("runs", "grp"), "tm", "state")),
        check_vma=False,
    )
```

```python
import functools

import jax
import jax.numpy as jnp
from jax import lax
from jax.experimental import pallas as pl
from jax.experimental.pallas import tpu as pltpu
from jax.sharding import PartitionSpec as P

STEPS = 4
LANES = 128
GROUP_ROWS = 16
VECTORS = 10
DIRECT_TM = 4

VMEM = pl.BlockSpec(memory_space=pltpu.VMEM)
KERNEL = pltpu.CompilerParams(vmem_limit_bytes=16 * 2**20)
HBM = pl.BlockSpec(memory_space=pltpu.HBM)
SMEM = pl.BlockSpec(memory_space=pltpu.SMEM)


def stencil(field, coeff, decay):
    width = field.shape[1]
    cell = lax.broadcasted_iota(jnp.int32, field.shape, 1)
    for _ in range(STEPS):
        upper_cell = jnp.where(cell == 0, 0.0, pltpu.roll(field, 1, 1))
        lower_cell = jnp.where(cell == width - 1, 0.0, pltpu.roll(field, width - 1, 1))
        field = field + coeff * (upper_cell + lower_cell - 2.0 * field) - decay * field
    return field


def row_pass(block, state, meta, y_ref, own_ref, other_ref, acc, part_ref):
    tile_num, row_num, half = own_ref.shape
    core = meta[2 * tile_num]
    own_at = pl.multiple_of(core * half, half)
    other_at = pl.multiple_of((1 - core) * half, half)
    state_own = state[:, pl.ds(own_at, half)]
    state_other = state[:, pl.ds(other_at, half)]
    lane = lax.broadcasted_iota(jnp.int32, (GROUP_ROWS, LANES), 1)
    row = lax.broadcasted_iota(jnp.int32, (GROUP_ROWS, LANES), 0)
    acc[...] = jnp.zeros_like(acc)

    def fold(values):
        total = values[:, :LANES]
        for start in range(LANES, half, LANES):
            total = total + values[:, start : start + LANES]
        return total

    def tile(index, carry):
        @pl.when(meta[index] == block)
        def _():
            live = meta[tile_num + index]
            readings = y_ref[pl.ds(index, 1), :]
            sum_own = jnp.zeros((GROUP_ROWS, half), jnp.float32)
            sum_other = jnp.zeros((GROUP_ROWS, half), jnp.float32)
            squares = jnp.zeros((GROUP_ROWS, LANES), jnp.float32)
            for start in range(0, row_num, GROUP_ROWS):
                own = own_ref[index, start : start + GROUP_ROWS, :].astype(jnp.float32)
                other = other_ref[index, start : start + GROUP_ROWS, :].astype(jnp.float32)
                valid = row + start < live
                product = fold(own * state_own) + fold(other * state_other)
                product = product - jnp.where(lane == row + start, readings, 0.0)
                weight = jnp.sum(product, axis=1, keepdims=True)
                weight = jnp.where(valid[:, :1], weight, 0.0)
                sum_own = sum_own + own * weight
                sum_other = sum_other + other * weight
                squares = squares + jnp.where(valid, fold(own * own) + fold(other * other), 0.0)
            acc[:, :half] += sum_own
            acc[:, half : 2 * half] += sum_other
            acc[:, 2 * half :] += squares

        return carry

    lax.fori_loop(0, tile_num, tile, 0)
    totals = jnp.sum(acc[...], axis=0, keepdims=True)
    part_ref[:, pl.ds(own_at, half)] = totals[:, :half]
    part_ref[:, pl.ds(other_at, half)] = totals[:, half : 2 * half]
    part_ref[:, 2 * half :] = totals[:, 2 * half :]


def first_kernel(block, meta, y_ref, own_ref, other_ref, state_ref, part_ref, acc):
    row_pass(block, state_ref, meta, y_ref, own_ref, other_ref, acc, part_ref)


def step_kernel(
    total_ref, meta, y_ref, own_ref, other_ref, state_ref, kappa_ref, rate_ref,
    next_ref, innovation_ref, part_ref, acc,
):
    width = state_ref.shape[1]
    trace_val = jnp.sum(total_ref[:, width:], axis=1, keepdims=True)
    lam_val = width / (2.0 * (width + trace_val))
    coeff, decay = kappa_ref[...], rate_ref[...]
    innovation = -lam_val * stencil(total_ref[:, :width], coeff, decay)
    next_ref[...] = stencil(state_ref[...], coeff, decay) + innovation
    innovation_ref[...] = innovation
    block = meta[2 * y_ref.shape[0] + 1]
    row_pass(block, next_ref, meta, y_ref, own_ref, other_ref, acc, part_ref)


def pieces_of(values):
    high = values.astype(jnp.bfloat16).astype(jnp.float32)
    middle = (values - high).astype(jnp.bfloat16).astype(jnp.float32)
    return high, middle, values - high - middle


OVER_ROWS = (((0,), (0,)), ((), ()))


def flip_of(turn, number, core):
    flips = list(reversed(range(1, number)))
    return flips[(turn + core) % len(flips)]


def flip_here(turn, number, beside=0):
    if turn == number - 1:
        return 0
    on_core = [flip_of(turn, number, core) for core in range(2)]
    return jnp.where(lax.axis_index("state") == beside, on_core[0], on_core[1])


def half_kernel(
    blocks_hbm, counts_hbm, y_hbm, own_hbm, out_ref, turned_ref,
    blocks, counts, y_ref, own_ref, acc, vec, side, readings, small_sems, tile_sems,
):
    tile_num, row_num, half = own_ref.shape
    small = [
        pltpu.make_async_copy(source, target, small_sems.at[at])
        for at, (source, target) in enumerate(
            ((blocks_hbm, blocks), (counts_hbm, counts), (y_hbm, y_ref))
        )
    ]
    tiles = [
        pltpu.make_async_copy(own_hbm.at[index], own_ref.at[index], tile_sems.at[index])
        for index in range(tile_num)
    ]
    for copy in small + tiles:
        copy.start()
    acc[...] = jnp.zeros_like(acc)
    vec[...] = jnp.zeros_like(vec)
    side[...] = jnp.zeros_like(side)
    for copy in small:
        copy.wait()
    readings[...] = y_ref[...].astype(jnp.float32)
    row = lax.broadcasted_iota(jnp.int32, (row_num, half), 0)
    for index in range(tile_num):
        tiles[index].wait()
        block = blocks[0, index]
        rows = jnp.where(row < counts[0, index], own_ref[index].astype(jnp.float32), 0.0)
        rows = rows.astype(jnp.bfloat16)
        turned = rows.T
        turned_ref[index] = turned
        square = jnp.dot(turned, rows, preferred_element_type=jnp.float32)
        acc[block, 0:LANES] += square[:LANES, :LANES]
        acc[block, LANES : 2 * LANES] += square[:LANES, LANES:]
        acc[block, 2 * LANES : 3 * LANES] += square[LANES:, LANES:]
        values = jnp.broadcast_to(readings[index : index + 1, :], (8, row_num))
        vec[block] += jnp.dot(
            values.astype(jnp.bfloat16), rows, preferred_element_type=jnp.float32
        )
    line = lax.broadcasted_iota(jnp.int32, (LANES, LANES), 0)
    column = lax.broadcasted_iota(jnp.int32, (LANES, LANES), 1)
    for block in range(out_ref.shape[0]):
        first, between, second = (acc[block, at * LANES : (at + 1) * LANES] for at in range(3))
        packed = jnp.where(line < column, first, jnp.where(line > column, second, 0.0))
        out_ref[block, 0:LANES] = packed.astype(jnp.bfloat16)
        out_ref[block, LANES : 2 * LANES] = between.astype(jnp.bfloat16)
        values = [vec[block, 0:1, :LANES], vec[block, 0:1, LANES:]]
        for square in (first, second):
            values.append(jnp.sum(jnp.where(line == column, square, 0.0), axis=0, keepdims=True))
        for at, value in enumerate(values):
            for which, part in enumerate(pieces_of(value)):
                side[which * 4 + at : which * 4 + at + 1, :] = part
        out_ref[block, 2 * LANES :] = side[...].astype(jnp.bfloat16)


def cross_kernel(blocks_hbm, other_hbm, turned_ref, half_ref, *refs):
    outs, (blocks, other_ref, acc, small_sem, tile_sems) = refs[:-5], refs[-5:]
    tile_num = other_ref.shape[0]
    number = len(outs)
    core, position = lax.axis_index("state"), lax.axis_index("tm")
    small = pltpu.make_async_copy(blocks_hbm, blocks, small_sem)
    tiles = [
        pltpu.make_async_copy(other_hbm.at[index], other_ref.at[index], tile_sems.at[index])
        for index in range(tile_num)
    ]
    for copy in [small] + tiles:
        copy.start()
    acc[...] = jnp.zeros_like(acc)
    small.wait()
    for index in range(tile_num):
        tiles[index].wait()
        block = blocks[0, index]
        for piece in range(2):
            at = pl.multiple_of((piece ^ core) * LANES, LANES)
            acc[block, piece * LANES : (piece + 1) * LANES] += jnp.dot(
                turned_ref[index, piece * LANES : (piece + 1) * LANES, :],
                other_ref[index, :, pl.ds(at, LANES)],
                preferred_element_type=jnp.float32,
            )
    for turn, out_ref in enumerate(outs):
        block = position ^ flip_here(turn, number)
        out_ref[: 2 * LANES] = half_ref[block, : 2 * LANES]
        out_ref[2 * LANES : 4 * LANES] = acc[block].astype(jnp.bfloat16)
        out_ref[4 * LANES :] = half_ref[block, 2 * LANES :]


def sum_kernel(kappa_ref, rate_ref, gain_ref, *refs):
    parts, out_ref, side = refs[:-2], refs[-2], refs[-1]
    core = lax.axis_index("state")
    total = parts[0][...].astype(jnp.float32)
    for part in parts[1:]:
        total = total + part[...].astype(jnp.float32)
    out_ref[: 4 * LANES] = total[: 4 * LANES].astype(jnp.bfloat16)
    below = total[4 * LANES :]
    values = [below[at : at + 1] + below[at + 4 : at + 5] + below[at + 8 : at + 9] for at in range(4)]
    for coefficient in (kappa_ref, rate_ref, gain_ref):
        for piece in range(2):
            at = pl.multiple_of((2 * core + piece) * LANES, LANES)
            values.append(coefficient[:, pl.ds(at, LANES)])
    side[...] = jnp.zeros_like(side)
    for at, value in enumerate(values):
        for which, part in enumerate(pieces_of(value)):
            side[which * VECTORS + at : which * VECTORS + at + 1, :] = part
    out_ref[4 * LANES :] = side[...].astype(jnp.bfloat16)


def chain(grams, vectors, state, states_ref, innovations_ref):
    width = state.shape[1]
    line = lax.broadcasted_iota(jnp.int32, (16, width), 0)
    for block in range(grams.shape[0]):
        info, diagonal, coeff, decay = (vectors[block, which : which + 1, :] for which in range(4))
        high, middle, low = pieces_of(state)
        split = jnp.where(line == 0, high, jnp.where(line == 1, middle, jnp.where(line == 2, low, 0.0)))
        product = jnp.dot(
            split.astype(jnp.bfloat16), grams[block], preferred_element_type=jnp.float32
        )
        product = jnp.sum(product, axis=0, keepdims=True) + diagonal * state
        trace_val = jnp.sum(diagonal, axis=1, keepdims=True)
        lam_val = width / (2.0 * (width + trace_val))
        innovation = -lam_val * stencil(product - info, coeff, decay)
        state = stencil(state, coeff, decay) + innovation
        states_ref[block : block + 1, :] = state
        innovations_ref[block : block + 1, :] = innovation


def assemble_kernel(number, *refs):
    own, other, rest = refs[:number], refs[number : 2 * number], refs[2 * number :]
    state_ref, grams, vectors, states_ref, innovations_ref = rest
    core, position = lax.axis_index("state"), lax.axis_index("tm")
    half = 2 * LANES
    line = lax.broadcasted_iota(jnp.int32, (LANES, LANES), 0)
    column = lax.broadcasted_iota(jnp.int32, (LANES, LANES), 1)
    for turn in range(number):
        flip, flip_other = flip_here(turn, number), flip_here(turn, number, 1)
        for pieces, side, block in (
            (own[turn], core, position ^ flip),
            (other[turn], 1 - core, position ^ flip_other),
        ):

            def piece(index):
                return pieces[index * LANES : (index + 1) * LANES, :]

            def put(row, column, values):
                row, column = pl.multiple_of(row, LANES), pl.multiple_of(column, LANES)
                grams[block, pl.ds(row, LANES), pl.ds(column, LANES)] = values.astype(jnp.bfloat16)

            here, there = side * half, (1 - side) * half
            packed = piece(0).astype(jnp.float32)
            turned = packed.T
            put(here, here, jnp.where(line < column, packed, turned))
            put(here + LANES, here + LANES, jnp.where(line > column, packed, turned))
            put(here, here + LANES, piece(1))
            put(here + LANES, here, piece(1).T)
            for index in range(2):
                beyond = there + (index ^ side) * LANES
                put(here + index * LANES, beyond, piece(2 + index))
                put(beyond, here + index * LANES, piece(2 + index).T)
            below = pieces[4 * LANES :, :].astype(jnp.float32)
            below = below[:VECTORS] + below[VECTORS : 2 * VECTORS] + below[2 * VECTORS : 3 * VECTORS]
            for at in range(VECTORS):
                lanes = pl.ds(pl.multiple_of(here + (at % 2) * LANES, LANES), LANES)
                vectors[block, at // 2 : at // 2 + 1, lanes] = below[at : at + 1]
    chain(grams, vectors, state_ref[...], states_ref, innovations_ref)


def chain_kernel(grams, vectors, state_ref, states_ref, innovations_ref):
    chain(grams, vectors, state_ref[...], states_ref, innovations_ref)


def shards(rows_h, rows_y, tile_block, tile_count, kappa, rate, smooth_gain, start_state):
    tm_size, grp_size = lax.axis_size("tm"), lax.axis_size("grp")
    state_size = lax.axis_size("state")
    tm_index, grp_index, core = (lax.axis_index(name) for name in ("tm", "grp", "state"))
    tile_num, row_num, half = rows_h.shape[1:]
    width = kappa.shape[2]
    own = rows_h[0]
    other = lax.ppermute(own, "state", [(i, (i + 1) % state_size) for i in range(state_size)])
    state = start_state.reshape(1, width)
    direct = tm_size <= DIRECT_TM and tm_size & (tm_size - 1) == 0
    states_shape = jax.ShapeDtypeStruct((tm_size, width), jnp.float32)

    def flip_over(array, turn):
        pairs = [
            (i * state_size + j, (i ^ flip_of(turn, tm_size, j)) * state_size + j)
            for i in range(tm_size)
            for j in range(state_size)
        ]
        return lax.ppermute(array, ("tm", "state"), pairs)

    def ring(array, step):
        return lax.ppermute(array, "grp", [(i, (i + step) % grp_size) for i in range(grp_size)])

    def across(array):
        return lax.ppermute(array, "state", [(i, (i + 1) % state_size) for i in range(state_size)])

    if direct:
        blocks = tile_block[0, :, 0][None]
        part_of, turned = pl.pallas_call(
            half_kernel,
            out_shape=(
                jax.ShapeDtypeStruct((tm_size, 2 * LANES + 16, LANES), jnp.bfloat16),
                jax.ShapeDtypeStruct((tile_num, half, row_num), jnp.bfloat16),
            ),
            in_specs=[HBM] * 4,
            out_specs=(VMEM, VMEM),
            scratch_shapes=[
                pltpu.SMEM((1, tile_num), jnp.int32),
                pltpu.SMEM((1, tile_num), jnp.int32),
                pltpu.VMEM((tile_num, row_num), jnp.bfloat16),
                pltpu.VMEM((tile_num, row_num, half), jnp.bfloat16),
                pltpu.VMEM((tm_size, 3 * LANES, LANES), jnp.float32),
                pltpu.VMEM((tm_size, 8, half), jnp.float32),
                pltpu.VMEM((16, LANES), jnp.float32),
                pltpu.VMEM((tile_num, row_num), jnp.float32),
                pltpu.SemaphoreType.DMA((3,)),
                pltpu.SemaphoreType.DMA((tile_num,)),
            ],
            compiler_params=KERNEL,
        )(blocks, tile_count, rows_y[0], own)
        pieces = pl.pallas_call(
            cross_kernel,
            out_shape=[jax.ShapeDtypeStruct((4 * LANES + 16, LANES), jnp.bfloat16)] * tm_size,
            in_specs=[HBM, HBM, VMEM, VMEM],
            out_specs=[VMEM] * tm_size,
            scratch_shapes=[
                pltpu.SMEM((1, tile_num), jnp.int32),
                pltpu.VMEM((tile_num, row_num, half), jnp.bfloat16),
                pltpu.VMEM((tm_size, 2 * LANES, LANES), jnp.float32),
                pltpu.SemaphoreType.DMA(()),
                pltpu.SemaphoreType.DMA((tile_num,)),
            ],
            compiler_params=KERNEL,
        )(blocks, other, turned, part_of)
        turns = range(tm_size - 1)
        parts = [flip_over(pieces[turn], turn) for turn in turns] + [pieces[-1]]
        own_sum = pl.pallas_call(
            sum_kernel,
            out_shape=jax.ShapeDtypeStruct((4 * LANES + 32, LANES), jnp.bfloat16),
            in_specs=[VMEM] * (tm_size + 3),
            out_specs=VMEM,
            scratch_shapes=[pltpu.VMEM((32, LANES), jnp.float32)],
            compiler_params=KERNEL,
        )(kappa[0], rate[0], smooth_gain[0], *parts)
        own_sums = [flip_over(own_sum, turn) for turn in turns] + [own_sum]
        other_sums = [across(values) for values in own_sums]
        grams, vectors, new_states, new_innovations = pl.pallas_call(
            functools.partial(assemble_kernel, tm_size),
            out_shape=(
                jax.ShapeDtypeStruct((tm_size, width, width), jnp.bfloat16),
                jax.ShapeDtypeStruct((tm_size, VECTORS // 2, width), jnp.float32),
                states_shape,
                states_shape,
            ),
            in_specs=[VMEM] * (2 * tm_size + 1),
            out_specs=[VMEM] * 4,
            compiler_params=KERNEL,
        )(*own_sums, *other_sums, state)
        gains = vectors[:, 4]

        def run_group(state, group):
            if group == 0:
                return new_states, new_innovations
            return pl.pallas_call(
                chain_kernel,
                out_shape=(states_shape, states_shape),
                in_specs=[VMEM] * 3,
                out_specs=(VMEM, VMEM),
                compiler_params=KERNEL,
            )(grams, vectors, state)
    else:
        readings = rows_y[0].astype(jnp.float32)
        meta = jnp.concatenate(
            [tile_block[0, :, 0], tile_count[0], jnp.stack([core, tm_index]).astype(jnp.int32)]
        )
        params = jnp.concatenate([kappa[0], rate[0], smooth_gain[0]], axis=0)
        gathered = lax.all_gather(params, "tm")
        gains = gathered[:, 2]
        vector = jax.ShapeDtypeStruct((1, width), jnp.float32)
        partial = jax.ShapeDtypeStruct((1, width + LANES), jnp.float32)
        acc = pltpu.VMEM((GROUP_ROWS, width + LANES), jnp.float32)

        def run_group(state, group):
            part = pl.pallas_call(
                functools.partial(first_kernel, 0),
                out_shape=partial,
                in_specs=[SMEM] + [VMEM] * 4,
                out_specs=VMEM,
                scratch_shapes=[acc],
                compiler_params=KERNEL,
            )(meta, readings, own, other, state)

            def lap(block, carry):
                state, part, states, innovations = carry
                here = lax.dynamic_index_in_dim(gathered, block, 0, False)
                own_meta = meta.at[2 * tile_num + 1].set((block + 1).astype(jnp.int32))
                state, innovation, part = pl.pallas_call(
                    step_kernel,
                    out_shape=(vector, vector, partial),
                    in_specs=[VMEM, SMEM] + [VMEM] * 6,
                    out_specs=(VMEM, VMEM, VMEM),
                    scratch_shapes=[acc],
                    compiler_params=KERNEL,
                )(lax.psum(part, "tm"), own_meta, readings, own, other, state, here[0:1], here[1:2])
                states = lax.dynamic_update_slice_in_dim(states, state, block, 0)
                innovations = lax.dynamic_update_slice_in_dim(innovations, innovation, block, 0)
                return state, part, states, innovations

            empty = jnp.zeros((tm_size, width), jnp.float32)
            return lax.fori_loop(0, tm_size, lap, (state, part, empty, empty))[2:]

    states = innovations = jnp.zeros((tm_size, width), jnp.float32)
    for group in range(grp_size):
        new_states, new_innovations = run_group(state, group)
        mine = grp_index == group
        states = jnp.where(mine, new_states, states)
        innovations = jnp.where(mine, new_innovations, innovations)
        if group < grp_size - 1:
            state = ring(new_states[-1:], 1)

    residual = jnp.zeros((1, width), jnp.float32)
    residuals = [None] * tm_size
    for group in reversed(range(grp_size)):
        running = residual
        for block in reversed(range(tm_size)):
            residuals[block] = running
            running = gains[block][None] * (running + innovations[block][None])
        if group > 0:
            arrived = ring(running, -1)
            residual = jnp.where(grp_index == group - 1, arrived, residual)
    smoothed = states + jnp.concatenate(residuals, 0)

    def out(values):
        piece = lax.dynamic_slice(values, (tm_index, core * half), (1, half))
        return piece.reshape(1, 1, half)

    return out(states), out(smoothed)


def solution(mesh):
    return jax.shard_map(
        shards,
        mesh=mesh,
        in_specs=(
            P(("runs", "grp"), "tm", None, "state"),
            P(("runs", "grp"), "tm", None),
            P(("runs", "grp"), "tm", None),
            P(("runs", "grp"), "tm"),
            P(("runs", "grp"), "tm", None),
            P(("runs", "grp"), "tm", None),
            P(("runs", "grp"), "tm", None),
            P("runs"),
        ),
        out_specs=(P(("runs", "grp"), "tm", "state"), P(("runs", "grp"), "tm", "state")),
        check_vma=False,
    )
```

```python
import functools

import jax
import jax.numpy as jnp
from jax import lax
from jax.experimental import pallas as pl
from jax.experimental.pallas import tpu as pltpu
from jax.sharding import PartitionSpec as P

STEPS = 4
LANES = 128
GROUP_ROWS = 16
VECTORS = 10
DIRECT_TM = 4

VMEM = pl.BlockSpec(memory_space=pltpu.VMEM)
KERNEL = pltpu.CompilerParams(vmem_limit_bytes=16 * 2**20)
SMEM = pl.BlockSpec(memory_space=pltpu.SMEM)


def stencil(field, coeff, decay):
    width = field.shape[1]
    cell = lax.broadcasted_iota(jnp.int32, field.shape, 1)
    for _ in range(STEPS):
        upper_cell = jnp.where(cell == 0, 0.0, pltpu.roll(field, 1, 1))
        lower_cell = jnp.where(cell == width - 1, 0.0, pltpu.roll(field, width - 1, 1))
        field = field + coeff * (upper_cell + lower_cell - 2.0 * field) - decay * field
    return field


def row_pass(block, state, meta, y_ref, own_ref, other_ref, acc, part_ref):
    tile_num, row_num, half = own_ref.shape
    core = meta[2 * tile_num]
    own_at = pl.multiple_of(core * half, half)
    other_at = pl.multiple_of((1 - core) * half, half)
    state_own = state[:, pl.ds(own_at, half)]
    state_other = state[:, pl.ds(other_at, half)]
    lane = lax.broadcasted_iota(jnp.int32, (GROUP_ROWS, LANES), 1)
    row = lax.broadcasted_iota(jnp.int32, (GROUP_ROWS, LANES), 0)
    acc[...] = jnp.zeros_like(acc)

    def fold(values):
        total = values[:, :LANES]
        for start in range(LANES, half, LANES):
            total = total + values[:, start : start + LANES]
        return total

    def tile(index, carry):
        @pl.when(meta[index] == block)
        def _():
            live = meta[tile_num + index]
            readings = y_ref[pl.ds(index, 1), :]
            sum_own = jnp.zeros((GROUP_ROWS, half), jnp.float32)
            sum_other = jnp.zeros((GROUP_ROWS, half), jnp.float32)
            squares = jnp.zeros((GROUP_ROWS, LANES), jnp.float32)
            for start in range(0, row_num, GROUP_ROWS):
                own = own_ref[index, start : start + GROUP_ROWS, :].astype(jnp.float32)
                other = other_ref[index, start : start + GROUP_ROWS, :].astype(jnp.float32)
                valid = row + start < live
                product = fold(own * state_own) + fold(other * state_other)
                product = product - jnp.where(lane == row + start, readings, 0.0)
                weight = jnp.sum(product, axis=1, keepdims=True)
                weight = jnp.where(valid[:, :1], weight, 0.0)
                sum_own = sum_own + own * weight
                sum_other = sum_other + other * weight
                squares = squares + jnp.where(valid, fold(own * own) + fold(other * other), 0.0)
            acc[:, :half] += sum_own
            acc[:, half : 2 * half] += sum_other
            acc[:, 2 * half :] += squares

        return carry

    lax.fori_loop(0, tile_num, tile, 0)
    totals = jnp.sum(acc[...], axis=0, keepdims=True)
    part_ref[:, pl.ds(own_at, half)] = totals[:, :half]
    part_ref[:, pl.ds(other_at, half)] = totals[:, half : 2 * half]
    part_ref[:, 2 * half :] = totals[:, 2 * half :]


def first_kernel(block, meta, y_ref, own_ref, other_ref, state_ref, part_ref, acc):
    row_pass(block, state_ref, meta, y_ref, own_ref, other_ref, acc, part_ref)


def step_kernel(
    total_ref, meta, y_ref, own_ref, other_ref, state_ref, kappa_ref, rate_ref,
    next_ref, innovation_ref, part_ref, acc,
):
    width = state_ref.shape[1]
    trace_val = jnp.sum(total_ref[:, width:], axis=1, keepdims=True)
    lam_val = width / (2.0 * (width + trace_val))
    coeff, decay = kappa_ref[...], rate_ref[...]
    innovation = -lam_val * stencil(total_ref[:, :width], coeff, decay)
    next_ref[...] = stencil(state_ref[...], coeff, decay) + innovation
    innovation_ref[...] = innovation
    block = meta[2 * y_ref.shape[0] + 1]
    row_pass(block, next_ref, meta, y_ref, own_ref, other_ref, acc, part_ref)


def pieces_of(values):
    high = values.astype(jnp.bfloat16).astype(jnp.float32)
    middle = (values - high).astype(jnp.bfloat16).astype(jnp.float32)
    return high, middle, values - high - middle


def flip_of(turn, number, core):
    flips = list(reversed(range(1, number)))
    return flips[(turn + core) % len(flips)]


def flip_here(turn, number, beside=0):
    if turn == number - 1:
        return 0
    on_core = [flip_of(turn, number, core) for core in range(2)]
    return jnp.where(lax.axis_index("state") == beside, on_core[0], on_core[1])


def gram_kernel(blocks, y_ref, own_ref, other_ref, *refs):
    outs, (acc, vec, side, readings) = refs[:-4], refs[-4:]
    tile_num, row_num, _ = own_ref.shape
    number = len(outs)
    core, position = lax.axis_index("state"), lax.axis_index("tm")
    acc[...] = jnp.zeros_like(acc)
    vec[...] = jnp.zeros_like(vec)
    side[...] = jnp.zeros_like(side)
    readings[...] = y_ref[...].astype(jnp.float32)
    for index in range(tile_num):
        block = blocks[index]
        rows = own_ref[index]
        turned = rows.T
        square = jnp.dot(turned, rows, preferred_element_type=jnp.float32)
        acc[block, 0:LANES] += square[:LANES, :LANES]
        acc[block, LANES : 2 * LANES] += square[:LANES, LANES:]
        acc[block, 2 * LANES : 3 * LANES] += square[LANES:, LANES:]
        for piece in range(2):
            at = pl.multiple_of((piece ^ core) * LANES, LANES)
            acc[block, (3 + piece) * LANES : (4 + piece) * LANES] += jnp.dot(
                turned[piece * LANES : (piece + 1) * LANES, :],
                other_ref[index, :, pl.ds(at, LANES)],
                preferred_element_type=jnp.float32,
            )
        values = jnp.broadcast_to(readings[index : index + 1, :], (8, row_num))
        vec[block] += jnp.dot(
            values.astype(jnp.bfloat16), rows, preferred_element_type=jnp.float32
        )
    line = lax.broadcasted_iota(jnp.int32, (LANES, LANES), 0)
    column = lax.broadcasted_iota(jnp.int32, (LANES, LANES), 1)
    for turn, out_ref in enumerate(outs):
        block = position ^ flip_here(turn, number)

        def take(piece):
            return acc[block, piece * LANES : (piece + 1) * LANES]

        packed = jnp.where(line < column, take(0), jnp.where(line > column, take(2), 0.0))
        out_ref[0:LANES] = packed.astype(jnp.bfloat16)
        for at, piece in ((1, 1), (2, 3), (3, 4)):
            out_ref[at * LANES : (at + 1) * LANES] = take(piece).astype(jnp.bfloat16)
        values = [vec[block, 0:1, :LANES], vec[block, 0:1, LANES:]]
        for piece in (0, 2):
            values.append(
                jnp.sum(jnp.where(line == column, take(piece), 0.0), axis=0, keepdims=True)
            )
        for at, value in enumerate(values):
            for which, part in enumerate(pieces_of(value)):
                side[which * 4 + at : which * 4 + at + 1, :] = part
        out_ref[4 * LANES :] = side[...].astype(jnp.bfloat16)


def sum_kernel(kappa_ref, rate_ref, gain_ref, *refs):
    parts, out_ref, side = refs[:-2], refs[-2], refs[-1]
    core = lax.axis_index("state")
    total = parts[0][...].astype(jnp.float32)
    for part in parts[1:]:
        total = total + part[...].astype(jnp.float32)
    out_ref[: 4 * LANES] = total[: 4 * LANES].astype(jnp.bfloat16)
    below = total[4 * LANES :]
    values = [below[at : at + 1] + below[at + 4 : at + 5] + below[at + 8 : at + 9] for at in range(4)]
    for coefficient in (kappa_ref, rate_ref, gain_ref):
        for piece in range(2):
            at = pl.multiple_of((2 * core + piece) * LANES, LANES)
            values.append(coefficient[:, pl.ds(at, LANES)])
    side[...] = jnp.zeros_like(side)
    for at, value in enumerate(values):
        for which, part in enumerate(pieces_of(value)):
            side[which * VECTORS + at : which * VECTORS + at + 1, :] = part
    out_ref[4 * LANES :] = side[...].astype(jnp.bfloat16)


def chain(grams, vectors, state, states_ref, innovations_ref):
    width = state.shape[1]
    line = lax.broadcasted_iota(jnp.int32, (16, width), 0)
    for block in range(grams.shape[0]):
        info, diagonal, coeff, decay = (vectors[block, which : which + 1, :] for which in range(4))
        high, middle, low = pieces_of(state)
        split = jnp.where(line == 0, high, jnp.where(line == 1, middle, jnp.where(line == 2, low, 0.0)))
        product = jnp.dot(
            split.astype(jnp.bfloat16), grams[block], preferred_element_type=jnp.float32
        )
        product = jnp.sum(product, axis=0, keepdims=True) + diagonal * state
        trace_val = jnp.sum(diagonal, axis=1, keepdims=True)
        lam_val = width / (2.0 * (width + trace_val))
        innovation = -lam_val * stencil(product - info, coeff, decay)
        state = stencil(state, coeff, decay) + innovation
        states_ref[block : block + 1, :] = state
        innovations_ref[block : block + 1, :] = innovation


def assemble_kernel(number, *refs):
    own, other, rest = refs[:number], refs[number : 2 * number], refs[2 * number :]
    state_ref, grams, vectors, states_ref, innovations_ref = rest
    core, position = lax.axis_index("state"), lax.axis_index("tm")
    half = 2 * LANES
    line = lax.broadcasted_iota(jnp.int32, (LANES, LANES), 0)
    column = lax.broadcasted_iota(jnp.int32, (LANES, LANES), 1)
    for turn in range(number):
        flip, flip_other = flip_here(turn, number), flip_here(turn, number, 1)
        for pieces, side, block in (
            (own[turn], core, position ^ flip),
            (other[turn], 1 - core, position ^ flip_other),
        ):

            def piece(index):
                return pieces[index * LANES : (index + 1) * LANES, :]

            def put(row, column, values):
                row, column = pl.multiple_of(row, LANES), pl.multiple_of(column, LANES)
                grams[block, pl.ds(row, LANES), pl.ds(column, LANES)] = values.astype(jnp.bfloat16)

            here, there = side * half, (1 - side) * half
            packed = piece(0).astype(jnp.float32)
            turned = packed.T
            put(here, here, jnp.where(line < column, packed, turned))
            put(here + LANES, here + LANES, jnp.where(line > column, packed, turned))
            put(here, here + LANES, piece(1))
            put(here + LANES, here, piece(1).T)
            for index in range(2):
                beyond = there + (index ^ side) * LANES
                put(here + index * LANES, beyond, piece(2 + index))
                put(beyond, here + index * LANES, piece(2 + index).T)
            below = pieces[4 * LANES :, :].astype(jnp.float32)
            below = below[:VECTORS] + below[VECTORS : 2 * VECTORS] + below[2 * VECTORS : 3 * VECTORS]
            for at in range(VECTORS):
                lanes = pl.ds(pl.multiple_of(here + (at % 2) * LANES, LANES), LANES)
                vectors[block, at // 2 : at // 2 + 1, lanes] = below[at : at + 1]
    chain(grams, vectors, state_ref[...], states_ref, innovations_ref)


def chain_kernel(grams, vectors, state_ref, states_ref, innovations_ref):
    chain(grams, vectors, state_ref[...], states_ref, innovations_ref)


def shards(rows_h, rows_y, tile_block, tile_count, kappa, rate, smooth_gain, start_state):
    tm_size, grp_size = lax.axis_size("tm"), lax.axis_size("grp")
    state_size = lax.axis_size("state")
    tm_index, grp_index, core = (lax.axis_index(name) for name in ("tm", "grp", "state"))
    tile_num, row_num, half = rows_h.shape[1:]
    width = kappa.shape[2]
    own = rows_h[0]
    other = lax.ppermute(own, "state", [(i, (i + 1) % state_size) for i in range(state_size)])
    state = start_state.reshape(1, width)
    direct = tm_size <= DIRECT_TM and tm_size & (tm_size - 1) == 0
    states_shape = jax.ShapeDtypeStruct((tm_size, width), jnp.float32)

    def flip_over(array, turn):
        pairs = [
            (i * state_size + j, (i ^ flip_of(turn, tm_size, j)) * state_size + j)
            for i in range(tm_size)
            for j in range(state_size)
        ]
        return lax.ppermute(array, ("tm", "state"), pairs)

    def ring(array, step):
        return lax.ppermute(array, "grp", [(i, (i + step) % grp_size) for i in range(grp_size)])

    def across(array):
        return lax.ppermute(array, "state", [(i, (i + 1) % state_size) for i in range(state_size)])

    if direct:
        live = jnp.arange(row_num, dtype=jnp.int32)[None, :] < tile_count[0][:, None]
        valid = jnp.where(live[:, :, None], own, jnp.zeros((), own.dtype))
        pieces = pl.pallas_call(
            gram_kernel,
            out_shape=[jax.ShapeDtypeStruct((4 * LANES + 16, LANES), jnp.bfloat16)] * tm_size,
            in_specs=[SMEM] + [VMEM] * 3,
            out_specs=[VMEM] * tm_size,
            scratch_shapes=[
                pltpu.VMEM((tm_size, 5 * LANES, LANES), jnp.float32),
                pltpu.VMEM((tm_size, 8, half), jnp.float32),
                pltpu.VMEM((16, LANES), jnp.float32),
                pltpu.VMEM((tile_num, row_num), jnp.float32),
            ],
            compiler_params=KERNEL,
        )(tile_block[0, :, 0], rows_y[0], valid, other)
        turns = range(tm_size - 1)
        parts = [flip_over(pieces[turn], turn) for turn in turns] + [pieces[-1]]
        own_sum = pl.pallas_call(
            sum_kernel,
            out_shape=jax.ShapeDtypeStruct((4 * LANES + 32, LANES), jnp.bfloat16),
            in_specs=[VMEM] * (tm_size + 3),
            out_specs=VMEM,
            scratch_shapes=[pltpu.VMEM((32, LANES), jnp.float32)],
            compiler_params=KERNEL,
        )(kappa[0], rate[0], smooth_gain[0], *parts)
        own_sums = [flip_over(own_sum, turn) for turn in turns] + [own_sum]
        other_sums = [across(values) for values in own_sums]
        grams, vectors, new_states, new_innovations = pl.pallas_call(
            functools.partial(assemble_kernel, tm_size),
            out_shape=(
                jax.ShapeDtypeStruct((tm_size, width, width), jnp.bfloat16),
                jax.ShapeDtypeStruct((tm_size, VECTORS // 2, width), jnp.float32),
                states_shape,
                states_shape,
            ),
            in_specs=[VMEM] * (2 * tm_size + 1),
            out_specs=[VMEM] * 4,
            compiler_params=KERNEL,
        )(*own_sums, *other_sums, state)
        gains = vectors[:, 4]

        def run_group(state, group):
            if group == 0:
                return new_states, new_innovations
            return pl.pallas_call(
                chain_kernel,
                out_shape=(states_shape, states_shape),
                in_specs=[VMEM] * 3,
                out_specs=(VMEM, VMEM),
                compiler_params=KERNEL,
            )(grams, vectors, state)
    else:
        readings = rows_y[0].astype(jnp.float32)
        meta = jnp.concatenate(
            [tile_block[0, :, 0], tile_count[0], jnp.stack([core, tm_index]).astype(jnp.int32)]
        )
        params = jnp.concatenate([kappa[0], rate[0], smooth_gain[0]], axis=0)
        gathered = lax.all_gather(params, "tm")
        gains = gathered[:, 2]
        vector = jax.ShapeDtypeStruct((1, width), jnp.float32)
        partial = jax.ShapeDtypeStruct((1, width + LANES), jnp.float32)
        acc = pltpu.VMEM((GROUP_ROWS, width + LANES), jnp.float32)

        def run_group(state, group):
            part = pl.pallas_call(
                functools.partial(first_kernel, 0),
                out_shape=partial,
                in_specs=[SMEM] + [VMEM] * 4,
                out_specs=VMEM,
                scratch_shapes=[acc],
                compiler_params=KERNEL,
            )(meta, readings, own, other, state)

            def lap(block, carry):
                state, part, states, innovations = carry
                here = lax.dynamic_index_in_dim(gathered, block, 0, False)
                own_meta = meta.at[2 * tile_num + 1].set((block + 1).astype(jnp.int32))
                state, innovation, part = pl.pallas_call(
                    step_kernel,
                    out_shape=(vector, vector, partial),
                    in_specs=[VMEM, SMEM] + [VMEM] * 6,
                    out_specs=(VMEM, VMEM, VMEM),
                    scratch_shapes=[acc],
                    compiler_params=KERNEL,
                )(lax.psum(part, "tm"), own_meta, readings, own, other, state, here[0:1], here[1:2])
                states = lax.dynamic_update_slice_in_dim(states, state, block, 0)
                innovations = lax.dynamic_update_slice_in_dim(innovations, innovation, block, 0)
                return state, part, states, innovations

            empty = jnp.zeros((tm_size, width), jnp.float32)
            return lax.fori_loop(0, tm_size, lap, (state, part, empty, empty))[2:]

    states = innovations = jnp.zeros((tm_size, width), jnp.float32)
    for group in range(grp_size):
        new_states, new_innovations = run_group(state, group)
        mine = grp_index == group
        states = jnp.where(mine, new_states, states)
        innovations = jnp.where(mine, new_innovations, innovations)
        if group < grp_size - 1:
            state = ring(new_states[-1:], 1)

    residual = jnp.zeros((1, width), jnp.float32)
    residuals = [None] * tm_size
    for group in reversed(range(grp_size)):
        running = residual
        for block in reversed(range(tm_size)):
            residuals[block] = running
            running = gains[block][None] * (running + innovations[block][None])
        if group > 0:
            arrived = ring(running, -1)
            residual = jnp.where(grp_index == group - 1, arrived, residual)
    smoothed = states + jnp.concatenate(residuals, 0)

    def out(values):
        piece = lax.dynamic_slice(values, (tm_index, core * half), (1, half))
        return piece.reshape(1, 1, half)

    return out(states), out(smoothed)


def solution(mesh):
    return jax.shard_map(
        shards,
        mesh=mesh,
        in_specs=(
            P(("runs", "grp"), "tm", None, "state"),
            P(("runs", "grp"), "tm", None),
            P(("runs", "grp"), "tm", None),
            P(("runs", "grp"), "tm"),
            P(("runs", "grp"), "tm", None),
            P(("runs", "grp"), "tm", None),
            P(("runs", "grp"), "tm", None),
            P("runs"),
        ),
        out_specs=(P(("runs", "grp"), "tm", "state"), P(("runs", "grp"), "tm", "state")),
        check_vma=False,
    )
```

```python
import functools

import jax
import jax.numpy as jnp
from jax import lax
from jax.experimental import pallas as pl
from jax.experimental.pallas import tpu as pltpu
from jax.sharding import PartitionSpec as P

STEPS = 4
LANES = 128
GROUP_ROWS = 16
VECTORS = 10
DIRECT_TM = 4

VMEM = pl.BlockSpec(memory_space=pltpu.VMEM)
KERNEL = pltpu.CompilerParams(vmem_limit_bytes=16 * 2**20)
SMEM = pl.BlockSpec(memory_space=pltpu.SMEM)


def stencil(field, coeff, decay):
    width = field.shape[1]
    cell = lax.broadcasted_iota(jnp.int32, field.shape, 1)
    for _ in range(STEPS):
        upper_cell = jnp.where(cell == 0, 0.0, pltpu.roll(field, 1, 1))
        lower_cell = jnp.where(cell == width - 1, 0.0, pltpu.roll(field, width - 1, 1))
        field = field + coeff * (upper_cell + lower_cell - 2.0 * field) - decay * field
    return field


def band_of(coeff, decay):
    width = coeff.shape[1]
    cell = lax.broadcasted_iota(jnp.int32, coeff.shape, 1)
    from_upper = jnp.where(cell == 0, 0.0, coeff)
    from_lower = jnp.where(cell == width - 1, 0.0, coeff)
    stay = 1.0 - 2.0 * coeff - decay
    band = {-1: from_upper, 0: stay, 1: from_lower}
    for _ in range(STEPS - 1):
        longer = {}
        for offset, values in band.items():
            for step, weight, turned in (
                (-1, from_upper, lambda: pltpu.roll(values, 1, 1)),
                (0, stay, lambda: values),
                (1, from_lower, lambda: pltpu.roll(values, width - 1, 1)),
            ):
                term = weight * turned()
                longer[offset + step] = longer[offset + step] + term if offset + step in longer else term
        band = longer
    return [band[offset] for offset in range(-STEPS, STEPS + 1)]


def apply_band(field, band):
    width = field.shape[1]
    total = band[STEPS : STEPS + 1] * field
    for offset in range(1, STEPS + 1):
        total = total + (
            band[STEPS - offset : STEPS - offset + 1] * pltpu.roll(field, offset, 1)
            + band[STEPS + offset : STEPS + offset + 1] * pltpu.roll(field, width - offset, 1)
        )
    return total


def row_pass(block, state, meta, y_ref, own_ref, other_ref, acc, part_ref):
    tile_num, row_num, half = own_ref.shape
    core = meta[2 * tile_num]
    own_at = pl.multiple_of(core * half, half)
    other_at = pl.multiple_of((1 - core) * half, half)
    state_own = state[:, pl.ds(own_at, half)]
    state_other = state[:, pl.ds(other_at, half)]
    lane = lax.broadcasted_iota(jnp.int32, (GROUP_ROWS, LANES), 1)
    row = lax.broadcasted_iota(jnp.int32, (GROUP_ROWS, LANES), 0)
    acc[...] = jnp.zeros_like(acc)

    def fold(values):
        total = values[:, :LANES]
        for start in range(LANES, half, LANES):
            total = total + values[:, start : start + LANES]
        return total

    def tile(index, carry):
        @pl.when(meta[index] == block)
        def _():
            live = meta[tile_num + index]
            readings = y_ref[pl.ds(index, 1), :]
            sum_own = jnp.zeros((GROUP_ROWS, half), jnp.float32)
            sum_other = jnp.zeros((GROUP_ROWS, half), jnp.float32)
            squares = jnp.zeros((GROUP_ROWS, LANES), jnp.float32)
            for start in range(0, row_num, GROUP_ROWS):
                own = own_ref[index, start : start + GROUP_ROWS, :].astype(jnp.float32)
                other = other_ref[index, start : start + GROUP_ROWS, :].astype(jnp.float32)
                valid = row + start < live
                product = fold(own * state_own) + fold(other * state_other)
                product = product - jnp.where(lane == row + start, readings, 0.0)
                weight = jnp.sum(product, axis=1, keepdims=True)
                weight = jnp.where(valid[:, :1], weight, 0.0)
                sum_own = sum_own + own * weight
                sum_other = sum_other + other * weight
                squares = squares + jnp.where(valid, fold(own * own) + fold(other * other), 0.0)
            acc[:, :half] += sum_own
            acc[:, half : 2 * half] += sum_other
            acc[:, 2 * half :] += squares

        return carry

    lax.fori_loop(0, tile_num, tile, 0)
    totals = jnp.sum(acc[...], axis=0, keepdims=True)
    part_ref[:, pl.ds(own_at, half)] = totals[:, :half]
    part_ref[:, pl.ds(other_at, half)] = totals[:, half : 2 * half]
    part_ref[:, 2 * half :] = totals[:, 2 * half :]


def first_kernel(block, meta, y_ref, own_ref, other_ref, state_ref, part_ref, acc):
    row_pass(block, state_ref, meta, y_ref, own_ref, other_ref, acc, part_ref)


def step_kernel(
    total_ref, meta, y_ref, own_ref, other_ref, state_ref, kappa_ref, rate_ref,
    next_ref, innovation_ref, part_ref, acc,
):
    width = state_ref.shape[1]
    trace_val = jnp.sum(total_ref[:, width:], axis=1, keepdims=True)
    lam_val = width / (2.0 * (width + trace_val))
    coeff, decay = kappa_ref[...], rate_ref[...]
    innovation = -lam_val * stencil(total_ref[:, :width], coeff, decay)
    next_ref[...] = stencil(state_ref[...], coeff, decay) + innovation
    innovation_ref[...] = innovation
    block = meta[2 * y_ref.shape[0] + 1]
    row_pass(block, next_ref, meta, y_ref, own_ref, other_ref, acc, part_ref)


def pieces_of(values):
    high = values.astype(jnp.bfloat16).astype(jnp.float32)
    middle = (values - high).astype(jnp.bfloat16).astype(jnp.float32)
    return high, middle, values - high - middle


def flip_of(turn, number, core):
    flips = list(reversed(range(1, number)))
    return flips[(turn + core) % len(flips)]


def flip_here(turn, number, beside=0):
    if turn == number - 1:
        return 0
    on_core = [flip_of(turn, number, core) for core in range(2)]
    return jnp.where(lax.axis_index("state") == beside, on_core[0], on_core[1])


def gram_kernel(blocks, y_ref, own_ref, other_ref, kappa_ref, rate_ref, gain_ref, *refs):
    outs, (acc, vec, side, readings) = refs[:-4], refs[-4:]
    tile_num, row_num, _ = own_ref.shape
    number = len(outs)
    core, position = lax.axis_index("state"), lax.axis_index("tm")
    acc[...] = jnp.zeros_like(acc)
    vec[...] = jnp.zeros_like(vec)
    side[...] = jnp.zeros_like(side)
    readings[...] = y_ref[...].astype(jnp.float32)
    for index in range(tile_num):
        block = blocks[index]
        rows = own_ref[index]
        turned = rows.T
        square = jnp.dot(turned, rows, preferred_element_type=jnp.float32)
        acc[block, 0:LANES] += square[:LANES, :LANES]
        acc[block, LANES : 2 * LANES] += square[:LANES, LANES:]
        acc[block, 2 * LANES : 3 * LANES] += square[LANES:, LANES:]
        for piece in range(2):
            at = pl.multiple_of((piece ^ core) * LANES, LANES)
            acc[block, (3 + piece) * LANES : (4 + piece) * LANES] += jnp.dot(
                turned[piece * LANES : (piece + 1) * LANES, :],
                other_ref[index, :, pl.ds(at, LANES)],
                preferred_element_type=jnp.float32,
            )
        values = jnp.broadcast_to(readings[index : index + 1, :], (8, row_num))
        vec[block] += jnp.dot(
            values.astype(jnp.bfloat16), rows, preferred_element_type=jnp.float32
        )
    line = lax.broadcasted_iota(jnp.int32, (LANES, LANES), 0)
    column = lax.broadcasted_iota(jnp.int32, (LANES, LANES), 1)
    for turn, out_ref in enumerate(outs):
        block = position ^ flip_here(turn, number)

        def take(piece):
            return acc[block, piece * LANES : (piece + 1) * LANES]

        packed = jnp.where(line < column, take(0), jnp.where(line > column, take(2), 0.0))
        out_ref[0:LANES] = packed.astype(jnp.bfloat16)
        for at, piece in ((1, 1), (2, 3), (3, 4)):
            out_ref[at * LANES : (at + 1) * LANES] = take(piece).astype(jnp.bfloat16)
        values = [vec[block, 0:1, :LANES], vec[block, 0:1, LANES:]]
        for piece in (0, 2):
            values.append(
                jnp.sum(jnp.where(line == column, take(piece), 0.0), axis=0, keepdims=True)
            )
        for coefficient in (kappa_ref, rate_ref, gain_ref):
            for piece in range(2):
                at = pl.multiple_of((2 * core + piece) * LANES, LANES)
                values.append(coefficient[:, pl.ds(at, LANES)])
        for at, value in enumerate(values):
            for which, part in enumerate(pieces_of(value)):
                side[which * VECTORS + at : which * VECTORS + at + 1, :] = part
        out_ref[4 * LANES :] = side[...].astype(jnp.bfloat16)


def sum_kernel(*refs):
    parts, (out_ref, coefficients, side) = refs[:-3], refs[-3:]
    number = len(parts)
    position = lax.axis_index("tm")
    total = parts[0][: 4 * LANES].astype(jnp.float32)
    for part in parts[1:]:
        total = total + part[: 4 * LANES].astype(jnp.float32)
    out_ref[: 4 * LANES] = total.astype(jnp.bfloat16)
    values = None
    for turn, part in enumerate(parts):
        below = part[4 * LANES :].astype(jnp.float32)
        below = below[:VECTORS] + below[VECTORS : 2 * VECTORS] + below[2 * VECTORS : 3 * VECTORS]
        coefficients[position ^ flip_here(turn, number), 0 : VECTORS - 4] = below[4:]
        values = below[:4] if values is None else values + below[:4]
    side[...] = jnp.zeros_like(side)
    for which, part in enumerate(pieces_of(values)):
        side[which * 4 : which * 4 + 4, :] = part
    out_ref[4 * LANES :] = side[...].astype(jnp.bfloat16)


def band_kernel(here_ref, there_ref, band_ref, whole):
    core = lax.axis_index("state")
    block_num = here_ref.shape[0]
    for source, side in ((here_ref, core), (there_ref, 1 - core)):
        for block in range(block_num):
            for at in range(VECTORS - 4):
                lanes = pl.ds(pl.multiple_of((2 * side + at % 2) * LANES, LANES), LANES)
                whole[at // 2, block : block + 1, lanes] = source[block, at : at + 1]
    band = band_of(whole[0], whole[1]) + [whole[2]]
    for at, values in enumerate(band):
        for block in range(block_num):
            band_ref[block, at : at + 1, :] = values[block : block + 1]


def chain(grams, vectors, bands, state, states_ref, innovations_ref):
    width = state.shape[1]
    line = lax.broadcasted_iota(jnp.int32, (16, width), 0)
    for block in range(grams.shape[0]):
        info, diagonal = vectors[block, 0:1, :], vectors[block, 1:2, :]
        band = bands[block, : 2 * STEPS + 1, :]
        high, middle, low = pieces_of(state)
        split = jnp.where(line == 0, high, jnp.where(line == 1, middle, jnp.where(line == 2, low, 0.0)))
        product = jnp.dot(
            split.astype(jnp.bfloat16), grams[block], preferred_element_type=jnp.float32
        )
        product = jnp.sum(product, axis=0, keepdims=True) + diagonal * state
        trace_val = jnp.sum(diagonal, axis=1, keepdims=True)
        lam_val = width / (2.0 * (width + trace_val))
        innovation = -lam_val * apply_band(product - info, band)
        state = apply_band(state, band) + innovation
        states_ref[block : block + 1, :] = state
        innovations_ref[block : block + 1, :] = innovation


def assemble_kernel(number, *refs):
    own, other, rest = refs[:number], refs[number : 2 * number], refs[2 * number :]
    bands, state_ref, grams, vectors, states_ref, innovations_ref = rest
    core, position = lax.axis_index("state"), lax.axis_index("tm")
    half = 2 * LANES
    line = lax.broadcasted_iota(jnp.int32, (LANES, LANES), 0)
    column = lax.broadcasted_iota(jnp.int32, (LANES, LANES), 1)
    for turn in range(number):
        flip, flip_other = flip_here(turn, number), flip_here(turn, number, 1)
        for pieces, side, block in (
            (own[turn], core, position ^ flip),
            (other[turn], 1 - core, position ^ flip_other),
        ):

            def piece(index):
                return pieces[index * LANES : (index + 1) * LANES, :]

            def put(row, column, values):
                row, column = pl.multiple_of(row, LANES), pl.multiple_of(column, LANES)
                grams[block, pl.ds(row, LANES), pl.ds(column, LANES)] = values.astype(jnp.bfloat16)

            here, there = side * half, (1 - side) * half
            packed = piece(0).astype(jnp.float32)
            turned = packed.T
            put(here, here, jnp.where(line < column, packed, turned))
            put(here + LANES, here + LANES, jnp.where(line > column, packed, turned))
            put(here, here + LANES, piece(1))
            put(here + LANES, here, piece(1).T)
            for index in range(2):
                beyond = there + (index ^ side) * LANES
                put(here + index * LANES, beyond, piece(2 + index))
                put(beyond, here + index * LANES, piece(2 + index).T)
            below = pieces[4 * LANES :, :].astype(jnp.float32)
            below = below[:4] + below[4:8] + below[8:12]
            for at in range(4):
                lanes = pl.ds(pl.multiple_of(here + (at % 2) * LANES, LANES), LANES)
                vectors[block, at // 2 : at // 2 + 1, lanes] = below[at : at + 1]
    chain(grams, vectors, bands, state_ref[...], states_ref, innovations_ref)


def chain_kernel(grams, vectors, bands, state_ref, states_ref, innovations_ref):
    chain(grams, vectors, bands, state_ref[...], states_ref, innovations_ref)


def shards(rows_h, rows_y, tile_block, tile_count, kappa, rate, smooth_gain, start_state):
    tm_size, grp_size = lax.axis_size("tm"), lax.axis_size("grp")
    state_size = lax.axis_size("state")
    tm_index, grp_index, core = (lax.axis_index(name) for name in ("tm", "grp", "state"))
    tile_num, row_num, half = rows_h.shape[1:]
    width = kappa.shape[2]
    own = rows_h[0]
    other = lax.ppermute(own, "state", [(i, (i + 1) % state_size) for i in range(state_size)])
    state = start_state.reshape(1, width)
    direct = tm_size <= DIRECT_TM and tm_size & (tm_size - 1) == 0
    states_shape = jax.ShapeDtypeStruct((tm_size, width), jnp.float32)

    def flip_over(array, turn):
        pairs = [
            (i * state_size + j, (i ^ flip_of(turn, tm_size, j)) * state_size + j)
            for i in range(tm_size)
            for j in range(state_size)
        ]
        return lax.ppermute(array, ("tm", "state"), pairs)

    def ring(array, step):
        return lax.ppermute(array, "grp", [(i, (i + step) % grp_size) for i in range(grp_size)])

    def across(array):
        return lax.ppermute(array, "state", [(i, (i + 1) % state_size) for i in range(state_size)])

    if direct:
        live = jnp.arange(row_num, dtype=jnp.int32)[None, :] < tile_count[0][:, None]
        valid = jnp.where(live[:, :, None], own, jnp.zeros((), own.dtype))
        pieces = pl.pallas_call(
            gram_kernel,
            out_shape=[jax.ShapeDtypeStruct((4 * LANES + 32, LANES), jnp.bfloat16)] * tm_size,
            in_specs=[SMEM] + [VMEM] * 6,
            out_specs=[VMEM] * tm_size,
            scratch_shapes=[
                pltpu.VMEM((tm_size, 5 * LANES, LANES), jnp.float32),
                pltpu.VMEM((tm_size, 8, half), jnp.float32),
                pltpu.VMEM((32, LANES), jnp.float32),
                pltpu.VMEM((tile_num, row_num), jnp.float32),
            ],
            compiler_params=KERNEL,
        )(tile_block[0, :, 0], rows_y[0], valid, other, kappa[0], rate[0], smooth_gain[0])
        turns = range(tm_size - 1)
        parts = [flip_over(pieces[turn], turn) for turn in turns] + [pieces[-1]]
        half_coefficients = jax.ShapeDtypeStruct((tm_size, 8, LANES), jnp.float32)
        own_sum, here = pl.pallas_call(
            sum_kernel,
            out_shape=(jax.ShapeDtypeStruct((4 * LANES + 16, LANES), jnp.bfloat16), half_coefficients),
            in_specs=[VMEM] * tm_size,
            out_specs=(VMEM, VMEM),
            scratch_shapes=[pltpu.VMEM((16, LANES), jnp.float32)],
            compiler_params=KERNEL,
        )(*parts)
        own_sums = [flip_over(own_sum, turn) for turn in turns] + [own_sum]
        here, own_sums[0] = lax.optimization_barrier((here, own_sums[0]))
        bands = pl.pallas_call(
            band_kernel,
            out_shape=jax.ShapeDtypeStruct((tm_size, 16, width), jnp.float32),
            in_specs=[VMEM, VMEM],
            out_specs=VMEM,
            scratch_shapes=[pltpu.VMEM((3, tm_size, width), jnp.float32)],
            compiler_params=KERNEL,
        )(here, across(here))
        other_sums = [across(values) for values in own_sums]
        grams, vectors, new_states, new_innovations = pl.pallas_call(
            functools.partial(assemble_kernel, tm_size),
            out_shape=(
                jax.ShapeDtypeStruct((tm_size, width, width), jnp.bfloat16),
                jax.ShapeDtypeStruct((tm_size, 8, width), jnp.float32),
                states_shape,
                states_shape,
            ),
            in_specs=[VMEM] * (2 * tm_size + 2),
            out_specs=[VMEM] * 4,
            compiler_params=KERNEL,
        )(*own_sums, *other_sums, bands, state)
        gains = bands[:, 2 * STEPS + 1]

        def run_group(state, group):
            if group == 0:
                return new_states, new_innovations
            return pl.pallas_call(
                chain_kernel,
                out_shape=(states_shape, states_shape),
                in_specs=[VMEM] * 4,
                out_specs=(VMEM, VMEM),
                compiler_params=KERNEL,
            )(grams, vectors, bands, state)
    else:
        readings = rows_y[0].astype(jnp.float32)
        meta = jnp.concatenate(
            [tile_block[0, :, 0], tile_count[0], jnp.stack([core, tm_index]).astype(jnp.int32)]
        )
        params = jnp.concatenate([kappa[0], rate[0], smooth_gain[0]], axis=0)
        gathered = lax.all_gather(params, "tm")
        gains = gathered[:, 2]
        vector = jax.ShapeDtypeStruct((1, width), jnp.float32)
        partial = jax.ShapeDtypeStruct((1, width + LANES), jnp.float32)
        acc = pltpu.VMEM((GROUP_ROWS, width + LANES), jnp.float32)

        def run_group(state, group):
            part = pl.pallas_call(
                functools.partial(first_kernel, 0),
                out_shape=partial,
                in_specs=[SMEM] + [VMEM] * 4,
                out_specs=VMEM,
                scratch_shapes=[acc],
                compiler_params=KERNEL,
            )(meta, readings, own, other, state)

            def lap(block, carry):
                state, part, states, innovations = carry
                here = lax.dynamic_index_in_dim(gathered, block, 0, False)
                own_meta = meta.at[2 * tile_num + 1].set((block + 1).astype(jnp.int32))
                state, innovation, part = pl.pallas_call(
                    step_kernel,
                    out_shape=(vector, vector, partial),
                    in_specs=[VMEM, SMEM] + [VMEM] * 6,
                    out_specs=(VMEM, VMEM, VMEM),
                    scratch_shapes=[acc],
                    compiler_params=KERNEL,
                )(lax.psum(part, "tm"), own_meta, readings, own, other, state, here[0:1], here[1:2])
                states = lax.dynamic_update_slice_in_dim(states, state, block, 0)
                innovations = lax.dynamic_update_slice_in_dim(innovations, innovation, block, 0)
                return state, part, states, innovations

            empty = jnp.zeros((tm_size, width), jnp.float32)
            return lax.fori_loop(0, tm_size, lap, (state, part, empty, empty))[2:]

    states = innovations = jnp.zeros((tm_size, width), jnp.float32)
    for group in range(grp_size):
        new_states, new_innovations = run_group(state, group)
        mine = grp_index == group
        states = jnp.where(mine, new_states, states)
        innovations = jnp.where(mine, new_innovations, innovations)
        if group < grp_size - 1:
            state = ring(new_states[-1:], 1)

    residual = jnp.zeros((1, width), jnp.float32)
    residuals = [None] * tm_size
    for group in reversed(range(grp_size)):
        running = residual
        for block in reversed(range(tm_size)):
            residuals[block] = running
            running = gains[block][None] * (running + innovations[block][None])
        if group > 0:
            arrived = ring(running, -1)
            residual = jnp.where(grp_index == group - 1, arrived, residual)
    smoothed = states + jnp.concatenate(residuals, 0)

    def out(values):
        piece = lax.dynamic_slice(values, (tm_index, core * half), (1, half))
        return piece.reshape(1, 1, half)

    return out(states), out(smoothed)


def solution(mesh):
    return jax.shard_map(
        shards,
        mesh=mesh,
        in_specs=(
            P(("runs", "grp"), "tm", None, "state"),
            P(("runs", "grp"), "tm", None),
            P(("runs", "grp"), "tm", None),
            P(("runs", "grp"), "tm"),
            P(("runs", "grp"), "tm", None),
            P(("runs", "grp"), "tm", None),
            P(("runs", "grp"), "tm", None),
            P("runs"),
        ),
        out_specs=(P(("runs", "grp"), "tm", "state"), P(("runs", "grp"), "tm", "state")),
        check_vma=False,
    )
```

```python
import functools

import jax
import jax.numpy as jnp
from jax import lax
from jax.experimental import pallas as pl
from jax.experimental.pallas import tpu as pltpu
from jax.sharding import PartitionSpec as P

STEPS = 4
LANES = 128
GROUP_ROWS = 16
VECTORS = 10
DIRECT_TM = 4

VMEM = pl.BlockSpec(memory_space=pltpu.VMEM)
KERNEL = pltpu.CompilerParams(vmem_limit_bytes=16 * 2**20)
SMEM = pl.BlockSpec(memory_space=pltpu.SMEM)


def stencil(field, coeff, decay):
    width = field.shape[1]
    cell = lax.broadcasted_iota(jnp.int32, field.shape, 1)
    for _ in range(STEPS):
        upper_cell = jnp.where(cell == 0, 0.0, pltpu.roll(field, 1, 1))
        lower_cell = jnp.where(cell == width - 1, 0.0, pltpu.roll(field, width - 1, 1))
        field = field + coeff * (upper_cell + lower_cell - 2.0 * field) - decay * field
    return field


def band_of(coeff, decay):
    width = coeff.shape[1]
    cell = lax.broadcasted_iota(jnp.int32, coeff.shape, 1)
    from_upper = jnp.where(cell == 0, 0.0, coeff)
    from_lower = jnp.where(cell == width - 1, 0.0, coeff)
    stay = 1.0 - 2.0 * coeff - decay
    band = {-1: from_upper, 0: stay, 1: from_lower}
    for _ in range(STEPS - 1):
        longer = {}
        for offset, values in band.items():
            for step, weight, turned in (
                (-1, from_upper, lambda: pltpu.roll(values, 1, 1)),
                (0, stay, lambda: values),
                (1, from_lower, lambda: pltpu.roll(values, width - 1, 1)),
            ):
                term = weight * turned()
                longer[offset + step] = longer[offset + step] + term if offset + step in longer else term
        band = longer
    return [band[offset] for offset in range(-STEPS, STEPS + 1)]


def apply_band(field, band):
    width = field.shape[1]
    total = band[STEPS : STEPS + 1] * field
    for offset in range(1, STEPS + 1):
        total = total + (
            band[STEPS - offset : STEPS - offset + 1] * pltpu.roll(field, offset, 1)
            + band[STEPS + offset : STEPS + offset + 1] * pltpu.roll(field, width - offset, 1)
        )
    return total


def row_pass(block, state, meta, y_ref, own_ref, other_ref, acc, part_ref):
    tile_num, row_num, half = own_ref.shape
    core = meta[2 * tile_num]
    own_at = pl.multiple_of(core * half, half)
    other_at = pl.multiple_of((1 - core) * half, half)
    state_own = state[:, pl.ds(own_at, half)]
    state_other = state[:, pl.ds(other_at, half)]
    lane = lax.broadcasted_iota(jnp.int32, (GROUP_ROWS, LANES), 1)
    row = lax.broadcasted_iota(jnp.int32, (GROUP_ROWS, LANES), 0)
    acc[...] = jnp.zeros_like(acc)

    def fold(values):
        total = values[:, :LANES]
        for start in range(LANES, half, LANES):
            total = total + values[:, start : start + LANES]
        return total

    def tile(index, carry):
        @pl.when(meta[index] == block)
        def _():
            live = meta[tile_num + index]
            readings = y_ref[pl.ds(index, 1), :]
            sum_own = jnp.zeros((GROUP_ROWS, half), jnp.float32)
            sum_other = jnp.zeros((GROUP_ROWS, half), jnp.float32)
            squares = jnp.zeros((GROUP_ROWS, LANES), jnp.float32)
            for start in range(0, row_num, GROUP_ROWS):
                own = own_ref[index, start : start + GROUP_ROWS, :].astype(jnp.float32)
                other = other_ref[index, start : start + GROUP_ROWS, :].astype(jnp.float32)
                valid = row + start < live
                product = fold(own * state_own) + fold(other * state_other)
                product = product - jnp.where(lane == row + start, readings, 0.0)
                weight = jnp.sum(product, axis=1, keepdims=True)
                weight = jnp.where(valid[:, :1], weight, 0.0)
                sum_own = sum_own + own * weight
                sum_other = sum_other + other * weight
                squares = squares + jnp.where(valid, fold(own * own) + fold(other * other), 0.0)
            acc[:, :half] += sum_own
            acc[:, half : 2 * half] += sum_other
            acc[:, 2 * half :] += squares

        return carry

    lax.fori_loop(0, tile_num, tile, 0)
    totals = jnp.sum(acc[...], axis=0, keepdims=True)
    part_ref[:, pl.ds(own_at, half)] = totals[:, :half]
    part_ref[:, pl.ds(other_at, half)] = totals[:, half : 2 * half]
    part_ref[:, 2 * half :] = totals[:, 2 * half :]


def first_kernel(block, meta, y_ref, own_ref, other_ref, state_ref, part_ref, acc):
    row_pass(block, state_ref, meta, y_ref, own_ref, other_ref, acc, part_ref)


def step_kernel(
    total_ref, meta, y_ref, own_ref, other_ref, state_ref, kappa_ref, rate_ref,
    next_ref, innovation_ref, part_ref, acc,
):
    width = state_ref.shape[1]
    trace_val = jnp.sum(total_ref[:, width:], axis=1, keepdims=True)
    lam_val = width / (2.0 * (width + trace_val))
    coeff, decay = kappa_ref[...], rate_ref[...]
    innovation = -lam_val * stencil(total_ref[:, :width], coeff, decay)
    next_ref[...] = stencil(state_ref[...], coeff, decay) + innovation
    innovation_ref[...] = innovation
    block = meta[2 * y_ref.shape[0] + 1]
    row_pass(block, next_ref, meta, y_ref, own_ref, other_ref, acc, part_ref)


def pieces_of(values):
    high = values.astype(jnp.bfloat16).astype(jnp.float32)
    middle = (values - high).astype(jnp.bfloat16).astype(jnp.float32)
    return high, middle, values - high - middle


def flip_of(turn, number, core):
    flips = list(reversed(range(1, number)))
    return flips[(turn + core) % len(flips)]


def flip_here(turn, number, beside=0):
    if turn == number - 1:
        return 0
    on_core = [flip_of(turn, number, core) for core in range(2)]
    return jnp.where(lax.axis_index("state") == beside, on_core[0], on_core[1])


def half_kernel(blocks, y_ref, own_ref, kappa_ref, rate_ref, gain_ref, *refs):
    outs, (turned_ref, acc, vec, side, readings) = refs[:-5], refs[-5:]
    tile_num, row_num, _ = own_ref.shape
    number = len(outs)
    core, position = lax.axis_index("state"), lax.axis_index("tm")
    acc[...] = jnp.zeros_like(acc)
    vec[...] = jnp.zeros_like(vec)
    side[...] = jnp.zeros_like(side)
    readings[...] = y_ref[...].astype(jnp.float32)
    for index in range(tile_num):
        block = blocks[index]
        rows = own_ref[index]
        turned = rows.T
        turned_ref[index] = turned
        square = jnp.dot(turned, rows, preferred_element_type=jnp.float32)
        acc[block, 0:LANES] += square[:LANES, :LANES]
        acc[block, LANES : 2 * LANES] += square[:LANES, LANES:]
        acc[block, 2 * LANES : 3 * LANES] += square[LANES:, LANES:]
        values = jnp.broadcast_to(readings[index : index + 1, :], (8, row_num))
        vec[block] += jnp.dot(
            values.astype(jnp.bfloat16), rows, preferred_element_type=jnp.float32
        )
    line = lax.broadcasted_iota(jnp.int32, (LANES, LANES), 0)
    column = lax.broadcasted_iota(jnp.int32, (LANES, LANES), 1)
    for turn, out_ref in enumerate(outs):
        block = position ^ flip_here(turn, number)
        first, between, second = (acc[block, at * LANES : (at + 1) * LANES] for at in range(3))
        packed = jnp.where(line < column, first, jnp.where(line > column, second, 0.0))
        out_ref[0:LANES] = packed.astype(jnp.bfloat16)
        out_ref[LANES : 2 * LANES] = between.astype(jnp.bfloat16)
        values = [vec[block, 0:1, :LANES], vec[block, 0:1, LANES:]]
        for square in (first, second):
            values.append(jnp.sum(jnp.where(line == column, square, 0.0), axis=0, keepdims=True))
        for coefficient in (kappa_ref, rate_ref, gain_ref):
            for piece in range(2):
                at = pl.multiple_of((2 * core + piece) * LANES, LANES)
                values.append(coefficient[:, pl.ds(at, LANES)])
        for at, value in enumerate(values):
            for which, part in enumerate(pieces_of(value)):
                side[which * VECTORS + at : which * VECTORS + at + 1, :] = part
        out_ref[2 * LANES :] = side[...].astype(jnp.bfloat16)


def cross_kernel(blocks, turned_ref, other_ref, *refs):
    outs, acc = refs[:-1], refs[-1]
    number = len(outs)
    core, position = lax.axis_index("state"), lax.axis_index("tm")
    acc[...] = jnp.zeros_like(acc)
    for index in range(other_ref.shape[0]):
        block = blocks[index]
        for piece in range(2):
            at = pl.multiple_of((piece ^ core) * LANES, LANES)
            acc[block, piece * LANES : (piece + 1) * LANES] += jnp.dot(
                turned_ref[index, piece * LANES : (piece + 1) * LANES, :],
                other_ref[index, :, pl.ds(at, LANES)],
                preferred_element_type=jnp.float32,
            )
    for turn, out_ref in enumerate(outs):
        out_ref[...] = acc[position ^ flip_here(turn, number)].astype(jnp.bfloat16)


def sum_kernel(*refs):
    parts, (out_ref, coefficients, side) = refs[:-3], refs[-3:]
    number = len(parts) // 2
    position = lax.axis_index("tm")
    for at, some in enumerate((parts[:number], parts[number:])):
        total = some[0][: 2 * LANES].astype(jnp.float32)
        for part in some[1:]:
            total = total + part[: 2 * LANES].astype(jnp.float32)
        out_ref[2 * at * LANES : 2 * (at + 1) * LANES] = total.astype(jnp.bfloat16)
    values = None
    for turn, part in enumerate(parts[:number]):
        below = part[2 * LANES :].astype(jnp.float32)
        below = below[:VECTORS] + below[VECTORS : 2 * VECTORS] + below[2 * VECTORS : 3 * VECTORS]
        coefficients[position ^ flip_here(turn, number), 0 : VECTORS - 4] = below[4:]
        values = below[:4] if values is None else values + below[:4]
    side[...] = jnp.zeros_like(side)
    for which, part in enumerate(pieces_of(values)):
        side[which * 4 : which * 4 + 4, :] = part
    out_ref[4 * LANES :] = side[...].astype(jnp.bfloat16)


def band_kernel(here_ref, there_ref, band_ref, whole):
    core = lax.axis_index("state")
    block_num = here_ref.shape[0]
    for source, side in ((here_ref, core), (there_ref, 1 - core)):
        for block in range(block_num):
            for at in range(VECTORS - 4):
                lanes = pl.ds(pl.multiple_of((2 * side + at % 2) * LANES, LANES), LANES)
                whole[at // 2, block : block + 1, lanes] = source[block, at : at + 1]
    band = band_of(whole[0], whole[1]) + [whole[2]]
    for at, values in enumerate(band):
        for block in range(block_num):
            band_ref[block, at : at + 1, :] = values[block : block + 1]


def chain(grams, vectors, bands, state, states_ref, innovations_ref):
    width = state.shape[1]
    line = lax.broadcasted_iota(jnp.int32, (16, width), 0)
    for block in range(grams.shape[0]):
        info, diagonal = vectors[block, 0:1, :], vectors[block, 1:2, :]
        band = bands[block, : 2 * STEPS + 1, :]
        high, middle, low = pieces_of(state)
        split = jnp.where(line == 0, high, jnp.where(line == 1, middle, jnp.where(line == 2, low, 0.0)))
        product = jnp.dot(
            split.astype(jnp.bfloat16), grams[block], preferred_element_type=jnp.float32
        )
        product = jnp.sum(product, axis=0, keepdims=True) + diagonal * state
        trace_val = jnp.sum(diagonal, axis=1, keepdims=True)
        lam_val = width / (2.0 * (width + trace_val))
        innovation = -lam_val * apply_band(product - info, band)
        state = apply_band(state, band) + innovation
        states_ref[block : block + 1, :] = state
        innovations_ref[block : block + 1, :] = innovation


def assemble_kernel(number, *refs):
    own, other, rest = refs[:number], refs[number : 2 * number], refs[2 * number :]
    bands, state_ref, grams, vectors, states_ref, innovations_ref = rest
    core, position = lax.axis_index("state"), lax.axis_index("tm")
    half = 2 * LANES
    line = lax.broadcasted_iota(jnp.int32, (LANES, LANES), 0)
    column = lax.broadcasted_iota(jnp.int32, (LANES, LANES), 1)
    for turn in range(number):
        flip, flip_other = flip_here(turn, number), flip_here(turn, number, 1)
        for pieces, side, block in (
            (own[turn], core, position ^ flip),
            (other[turn], 1 - core, position ^ flip_other),
        ):

            def piece(index):
                return pieces[index * LANES : (index + 1) * LANES, :]

            def put(row, column, values):
                row, column = pl.multiple_of(row, LANES), pl.multiple_of(column, LANES)
                grams[block, pl.ds(row, LANES), pl.ds(column, LANES)] = values.astype(jnp.bfloat16)

            here, there = side * half, (1 - side) * half
            packed = piece(0).astype(jnp.float32)
            turned = packed.T
            put(here, here, jnp.where(line < column, packed, turned))
            put(here + LANES, here + LANES, jnp.where(line > column, packed, turned))
            put(here, here + LANES, piece(1))
            put(here + LANES, here, piece(1).T)
            for index in range(2):
                beyond = there + (index ^ side) * LANES
                put(here + index * LANES, beyond, piece(2 + index))
                put(beyond, here + index * LANES, piece(2 + index).T)
            below = pieces[4 * LANES :, :].astype(jnp.float32)
            below = below[:4] + below[4:8] + below[8:12]
            for at in range(4):
                lanes = pl.ds(pl.multiple_of(here + (at % 2) * LANES, LANES), LANES)
                vectors[block, at // 2 : at // 2 + 1, lanes] = below[at : at + 1]
    chain(grams, vectors, bands, state_ref[...], states_ref, innovations_ref)


def chain_kernel(grams, vectors, bands, state_ref, states_ref, innovations_ref):
    chain(grams, vectors, bands, state_ref[...], states_ref, innovations_ref)


def shards(rows_h, rows_y, tile_block, tile_count, kappa, rate, smooth_gain, start_state):
    tm_size, grp_size = lax.axis_size("tm"), lax.axis_size("grp")
    state_size = lax.axis_size("state")
    tm_index, grp_index, core = (lax.axis_index(name) for name in ("tm", "grp", "state"))
    tile_num, row_num, half = rows_h.shape[1:]
    width = kappa.shape[2]
    own = rows_h[0]
    other = lax.ppermute(own, "state", [(i, (i + 1) % state_size) for i in range(state_size)])
    state = start_state.reshape(1, width)
    direct = tm_size <= DIRECT_TM and tm_size & (tm_size - 1) == 0
    states_shape = jax.ShapeDtypeStruct((tm_size, width), jnp.float32)

    def flip_over(array, turn):
        pairs = [
            (i * state_size + j, (i ^ flip_of(turn, tm_size, j)) * state_size + j)
            for i in range(tm_size)
            for j in range(state_size)
        ]
        return lax.ppermute(array, ("tm", "state"), pairs)

    def ring(array, step):
        return lax.ppermute(array, "grp", [(i, (i + step) % grp_size) for i in range(grp_size)])

    def across(array):
        return lax.ppermute(array, "state", [(i, (i + 1) % state_size) for i in range(state_size)])

    if direct:
        live = jnp.arange(row_num, dtype=jnp.int32)[None, :] < tile_count[0][:, None]
        valid = jnp.where(live[:, :, None], own, jnp.zeros((), own.dtype))
        second_half = jax.ShapeDtypeStruct((2 * LANES, LANES), jnp.bfloat16)
        blocks = tile_block[0, :, 0]
        *pieces, turned = pl.pallas_call(
            half_kernel,
            out_shape=[jax.ShapeDtypeStruct((2 * LANES + 32, LANES), jnp.bfloat16)] * tm_size
            + [jax.ShapeDtypeStruct((tile_num, half, row_num), jnp.bfloat16)],
            in_specs=[SMEM] + [VMEM] * 5,
            out_specs=[VMEM] * (tm_size + 1),
            scratch_shapes=[
                pltpu.VMEM((tm_size, 3 * LANES, LANES), jnp.float32),
                pltpu.VMEM((tm_size, 8, half), jnp.float32),
                pltpu.VMEM((32, LANES), jnp.float32),
                pltpu.VMEM((tile_num, row_num), jnp.float32),
            ],
            compiler_params=KERNEL,
        )(blocks, rows_y[0], valid, kappa[0], rate[0], smooth_gain[0])
        turns = range(tm_size - 1)
        parts = [flip_over(pieces[turn], turn) for turn in turns] + [pieces[-1]]
        pieces2 = pl.pallas_call(
            cross_kernel,
            out_shape=[second_half] * tm_size,
            in_specs=[SMEM] + [VMEM] * 2,
            out_specs=[VMEM] * tm_size,
            scratch_shapes=[pltpu.VMEM((tm_size, 2 * LANES, LANES), jnp.float32)],
            compiler_params=KERNEL,
        )(blocks, turned, other)
        parts2 = [flip_over(pieces2[turn], turn) for turn in turns] + [pieces2[-1]]
        half_coefficients = jax.ShapeDtypeStruct((tm_size, 8, LANES), jnp.float32)
        own_sum, here = pl.pallas_call(
            sum_kernel,
            out_shape=(jax.ShapeDtypeStruct((4 * LANES + 16, LANES), jnp.bfloat16), half_coefficients),
            in_specs=[VMEM] * (2 * tm_size),
            out_specs=(VMEM, VMEM),
            scratch_shapes=[pltpu.VMEM((16, LANES), jnp.float32)],
            compiler_params=KERNEL,
        )(*parts, *parts2)
        own_sums = [flip_over(own_sum, turn) for turn in turns] + [own_sum]
        here, own_sums[0] = lax.optimization_barrier((here, own_sums[0]))
        bands = pl.pallas_call(
            band_kernel,
            out_shape=jax.ShapeDtypeStruct((tm_size, 16, width), jnp.float32),
            in_specs=[VMEM, VMEM],
            out_specs=VMEM,
            scratch_shapes=[pltpu.VMEM((3, tm_size, width), jnp.float32)],
            compiler_params=KERNEL,
        )(here, across(here))
        other_sums = [across(values) for values in own_sums]
        grams, vectors, new_states, new_innovations = pl.pallas_call(
            functools.partial(assemble_kernel, tm_size),
            out_shape=(
                jax.ShapeDtypeStruct((tm_size, width, width), jnp.bfloat16),
                jax.ShapeDtypeStruct((tm_size, 8, width), jnp.float32),
                states_shape,
                states_shape,
            ),
            in_specs=[VMEM] * (2 * tm_size + 2),
            out_specs=[VMEM] * 4,
            compiler_params=KERNEL,
        )(*own_sums, *other_sums, bands, state)
        gains = bands[:, 2 * STEPS + 1]

        def run_group(state, group):
            if group == 0:
                return new_states, new_innovations
            return pl.pallas_call(
                chain_kernel,
                out_shape=(states_shape, states_shape),
                in_specs=[VMEM] * 4,
                out_specs=(VMEM, VMEM),
                compiler_params=KERNEL,
            )(grams, vectors, bands, state)
    else:
        readings = rows_y[0].astype(jnp.float32)
        meta = jnp.concatenate(
            [tile_block[0, :, 0], tile_count[0], jnp.stack([core, tm_index]).astype(jnp.int32)]
        )
        params = jnp.concatenate([kappa[0], rate[0], smooth_gain[0]], axis=0)
        gathered = lax.all_gather(params, "tm")
        gains = gathered[:, 2]
        vector = jax.ShapeDtypeStruct((1, width), jnp.float32)
        partial = jax.ShapeDtypeStruct((1, width + LANES), jnp.float32)
        acc = pltpu.VMEM((GROUP_ROWS, width + LANES), jnp.float32)

        def run_group(state, group):
            part = pl.pallas_call(
                functools.partial(first_kernel, 0),
                out_shape=partial,
                in_specs=[SMEM] + [VMEM] * 4,
                out_specs=VMEM,
                scratch_shapes=[acc],
                compiler_params=KERNEL,
            )(meta, readings, own, other, state)

            def lap(block, carry):
                state, part, states, innovations = carry
                here = lax.dynamic_index_in_dim(gathered, block, 0, False)
                own_meta = meta.at[2 * tile_num + 1].set((block + 1).astype(jnp.int32))
                state, innovation, part = pl.pallas_call(
                    step_kernel,
                    out_shape=(vector, vector, partial),
                    in_specs=[VMEM, SMEM] + [VMEM] * 6,
                    out_specs=(VMEM, VMEM, VMEM),
                    scratch_shapes=[acc],
                    compiler_params=KERNEL,
                )(lax.psum(part, "tm"), own_meta, readings, own, other, state, here[0:1], here[1:2])
                states = lax.dynamic_update_slice_in_dim(states, state, block, 0)
                innovations = lax.dynamic_update_slice_in_dim(innovations, innovation, block, 0)
                return state, part, states, innovations

            empty = jnp.zeros((tm_size, width), jnp.float32)
            return lax.fori_loop(0, tm_size, lap, (state, part, empty, empty))[2:]

    states = innovations = jnp.zeros((tm_size, width), jnp.float32)
    for group in range(grp_size):
        new_states, new_innovations = run_group(state, group)
        mine = grp_index == group
        states = jnp.where(mine, new_states, states)
        innovations = jnp.where(mine, new_innovations, innovations)
        if group < grp_size - 1:
            state = ring(new_states[-1:], 1)

    residual = jnp.zeros((1, width), jnp.float32)
    residuals = [None] * tm_size
    for group in reversed(range(grp_size)):
        running = residual
        for block in reversed(range(tm_size)):
            residuals[block] = running
            running = gains[block][None] * (running + innovations[block][None])
        if group > 0:
            arrived = ring(running, -1)
            residual = jnp.where(grp_index == group - 1, arrived, residual)
    smoothed = states + jnp.concatenate(residuals, 0)

    def out(values):
        piece = lax.dynamic_slice(values, (tm_index, core * half), (1, half))
        return piece.reshape(1, 1, half)

    return out(states), out(smoothed)


def solution(mesh):
    return jax.shard_map(
        shards,
        mesh=mesh,
        in_specs=(
            P(("runs", "grp"), "tm", None, "state"),
            P(("runs", "grp"), "tm", None),
            P(("runs", "grp"), "tm", None),
            P(("runs", "grp"), "tm"),
            P(("runs", "grp"), "tm", None),
            P(("runs", "grp"), "tm", None),
            P(("runs", "grp"), "tm", None),
            P("runs"),
        ),
        out_specs=(P(("runs", "grp"), "tm", "state"), P(("runs", "grp"), "tm", "state")),
        check_vma=False,
    )
```

```python
import functools

import jax
import jax.numpy as jnp
from jax import lax
from jax.experimental import pallas as pl
from jax.experimental.pallas import tpu as pltpu
from jax.sharding import PartitionSpec as P

STEPS = 4
LANES = 128
GROUP_ROWS = 16
VECTORS = 10
FLIPS = {1: (), 2: (1,), 4: (2, 1, 3)}

VMEM = pl.BlockSpec(memory_space=pltpu.VMEM)
KERNEL = pltpu.CompilerParams(vmem_limit_bytes=16 * 2**20)
SMEM = pl.BlockSpec(memory_space=pltpu.SMEM)


def stencil(field, coeff, decay):
    width = field.shape[1]
    cell = lax.broadcasted_iota(jnp.int32, field.shape, 1)
    for _ in range(STEPS):
        upper_cell = jnp.where(cell == 0, 0.0, pltpu.roll(field, 1, 1))
        lower_cell = jnp.where(cell == width - 1, 0.0, pltpu.roll(field, width - 1, 1))
        field = field + coeff * (upper_cell + lower_cell - 2.0 * field) - decay * field
    return field


def band_of(coeff, decay):
    width = coeff.shape[1]
    cell = lax.broadcasted_iota(jnp.int32, coeff.shape, 1)
    from_upper = jnp.where(cell == 0, 0.0, coeff)
    from_lower = jnp.where(cell == width - 1, 0.0, coeff)
    stay = 1.0 - 2.0 * coeff - decay
    band = {-1: from_upper, 0: stay, 1: from_lower}
    for _ in range(STEPS - 1):
        longer = {}
        for offset, values in band.items():
            for step, weight, turned in (
                (-1, from_upper, lambda: pltpu.roll(values, 1, 1)),
                (0, stay, lambda: values),
                (1, from_lower, lambda: pltpu.roll(values, width - 1, 1)),
            ):
                term = weight * turned()
                longer[offset + step] = longer[offset + step] + term if offset + step in longer else term
        band = longer
    return [band[offset] for offset in range(-STEPS, STEPS + 1)]


def apply_band(field, band):
    width = field.shape[1]
    total = band[STEPS : STEPS + 1] * field
    for offset in range(1, STEPS + 1):
        total = total + (
            band[STEPS - offset : STEPS - offset + 1] * pltpu.roll(field, offset, 1)
            + band[STEPS + offset : STEPS + offset + 1] * pltpu.roll(field, width - offset, 1)
        )
    return total


def row_pass(block, state, meta, y_ref, own_ref, other_ref, acc, part_ref):
    tile_num, row_num, half = own_ref.shape
    core = meta[2 * tile_num]
    own_at = pl.multiple_of(core * half, half)
    other_at = pl.multiple_of((1 - core) * half, half)
    state_own = state[:, pl.ds(own_at, half)]
    state_other = state[:, pl.ds(other_at, half)]
    lane = lax.broadcasted_iota(jnp.int32, (GROUP_ROWS, LANES), 1)
    row = lax.broadcasted_iota(jnp.int32, (GROUP_ROWS, LANES), 0)
    acc[...] = jnp.zeros_like(acc)

    def fold(values):
        total = values[:, :LANES]
        for start in range(LANES, half, LANES):
            total = total + values[:, start : start + LANES]
        return total

    def tile(index, carry):
        @pl.when(meta[index] == block)
        def _():
            live = meta[tile_num + index]
            readings = y_ref[pl.ds(index, 1), :]
            sum_own = jnp.zeros((GROUP_ROWS, half), jnp.float32)
            sum_other = jnp.zeros((GROUP_ROWS, half), jnp.float32)
            squares = jnp.zeros((GROUP_ROWS, LANES), jnp.float32)
            for start in range(0, row_num, GROUP_ROWS):
                own = own_ref[index, start : start + GROUP_ROWS, :].astype(jnp.float32)
                other = other_ref[index, start : start + GROUP_ROWS, :].astype(jnp.float32)
                valid = row + start < live
                product = fold(own * state_own) + fold(other * state_other)
                product = product - jnp.where(lane == row + start, readings, 0.0)
                weight = jnp.sum(product, axis=1, keepdims=True)
                weight = jnp.where(valid[:, :1], weight, 0.0)
                sum_own = sum_own + own * weight
                sum_other = sum_other + other * weight
                squares = squares + jnp.where(valid, fold(own * own) + fold(other * other), 0.0)
            acc[:, :half] += sum_own
            acc[:, half : 2 * half] += sum_other
            acc[:, 2 * half :] += squares

        return carry

    lax.fori_loop(0, tile_num, tile, 0)
    totals = jnp.sum(acc[...], axis=0, keepdims=True)
    part_ref[:, pl.ds(own_at, half)] = totals[:, :half]
    part_ref[:, pl.ds(other_at, half)] = totals[:, half : 2 * half]
    part_ref[:, 2 * half :] = totals[:, 2 * half :]


def first_kernel(block, meta, y_ref, own_ref, other_ref, state_ref, part_ref, acc):
    row_pass(block, state_ref, meta, y_ref, own_ref, other_ref, acc, part_ref)


def step_kernel(
    total_ref, meta, y_ref, own_ref, other_ref, state_ref, kappa_ref, rate_ref,
    next_ref, innovation_ref, part_ref, acc,
):
    width = state_ref.shape[1]
    trace_val = jnp.sum(total_ref[:, width:], axis=1, keepdims=True)
    lam_val = width / (2.0 * (width + trace_val))
    coeff, decay = kappa_ref[...], rate_ref[...]
    innovation = -lam_val * stencil(total_ref[:, :width], coeff, decay)
    next_ref[...] = stencil(state_ref[...], coeff, decay) + innovation
    innovation_ref[...] = innovation
    block = meta[2 * y_ref.shape[0] + 1]
    row_pass(block, next_ref, meta, y_ref, own_ref, other_ref, acc, part_ref)


def pieces_of(values):
    high = values.astype(jnp.bfloat16).astype(jnp.float32)
    middle = (values - high).astype(jnp.bfloat16).astype(jnp.float32)
    return high, middle, values - high - middle


def flip_of(turn, number, core):
    return FLIPS[number][:: 1 - 2 * core][turn]


def flip_here(turn, number, beside=0):
    if turn == number - 1:
        return 0
    on_core = [flip_of(turn, number, core) for core in range(2)]
    return jnp.where(lax.axis_index("state") == beside, on_core[0], on_core[1])


def half_kernel(blocks, y_ref, own_ref, kappa_ref, rate_ref, gain_ref, *refs):
    outs, (turned_ref, acc, vec, side, readings) = refs[:-5], refs[-5:]
    tile_num, row_num, _ = own_ref.shape
    number = len(outs)
    core, position = lax.axis_index("state"), lax.axis_index("tm")
    acc[...] = jnp.zeros_like(acc)
    vec[...] = jnp.zeros_like(vec)
    side[...] = jnp.zeros_like(side)
    readings[...] = y_ref[...].astype(jnp.float32)
    for index in range(tile_num):
        block = blocks[index]
        rows = own_ref[index]
        turned = rows.T
        turned_ref[index] = turned
        square = jnp.dot(turned, rows, preferred_element_type=jnp.float32)
        acc[block, 0:LANES] += square[:LANES, :LANES]
        acc[block, LANES : 2 * LANES] += square[:LANES, LANES:]
        acc[block, 2 * LANES : 3 * LANES] += square[LANES:, LANES:]
        values = jnp.broadcast_to(readings[index : index + 1, :], (8, row_num))
        vec[block] += jnp.dot(
            values.astype(jnp.bfloat16), rows, preferred_element_type=jnp.float32
        )
    line = lax.broadcasted_iota(jnp.int32, (LANES, LANES), 0)
    column = lax.broadcasted_iota(jnp.int32, (LANES, LANES), 1)
    for turn, out_ref in enumerate(outs):
        block = position ^ flip_here(turn, number)
        first, between, second = (acc[block, at * LANES : (at + 1) * LANES] for at in range(3))
        packed = jnp.where(line < column, first, jnp.where(line > column, second, 0.0))
        out_ref[0:LANES] = packed.astype(jnp.bfloat16)
        out_ref[LANES : 2 * LANES] = between.astype(jnp.bfloat16)
        values = [vec[block, 0:1, :LANES], vec[block, 0:1, LANES:]]
        for square in (first, second):
            values.append(jnp.sum(jnp.where(line == column, square, 0.0), axis=0, keepdims=True))
        for coefficient in (kappa_ref, rate_ref, gain_ref):
            for piece in range(2):
                at = pl.multiple_of((2 * core + piece) * LANES, LANES)
                values.append(coefficient[:, pl.ds(at, LANES)])
        for at, value in enumerate(values):
            for which, part in enumerate(pieces_of(value)):
                side[which * VECTORS + at : which * VECTORS + at + 1, :] = part
        out_ref[2 * LANES :] = side[...].astype(jnp.bfloat16)


def cross_kernel(blocks, turned_ref, other_ref, *refs):
    outs, acc = refs[:-1], refs[-1]
    number = len(outs)
    core, position = lax.axis_index("state"), lax.axis_index("tm")
    acc[...] = jnp.zeros_like(acc)
    for index in range(other_ref.shape[0]):
        block = blocks[index]
        for piece in range(2):
            at = pl.multiple_of((piece ^ core) * LANES, LANES)
            acc[block, piece * LANES : (piece + 1) * LANES] += jnp.dot(
                turned_ref[index, piece * LANES : (piece + 1) * LANES, :],
                other_ref[index, :, pl.ds(at, LANES)],
                preferred_element_type=jnp.float32,
            )
    for turn, out_ref in enumerate(outs):
        out_ref[...] = acc[position ^ flip_here(turn, number)].astype(jnp.bfloat16)


def sum_kernel(*refs):
    parts, (out_ref, coefficients, side) = refs[:-3], refs[-3:]
    number = len(parts) // 2
    position = lax.axis_index("tm")
    for at, some in enumerate((parts[:number], parts[number:])):
        total = some[0][: 2 * LANES].astype(jnp.float32)
        for part in some[1:]:
            total = total + part[: 2 * LANES].astype(jnp.float32)
        out_ref[2 * at * LANES : 2 * (at + 1) * LANES] = total.astype(jnp.bfloat16)
    values = None
    for turn, part in enumerate(parts[:number]):
        below = part[2 * LANES :].astype(jnp.float32)
        below = below[:VECTORS] + below[VECTORS : 2 * VECTORS] + below[2 * VECTORS : 3 * VECTORS]
        coefficients[position ^ flip_here(turn, number), 0 : VECTORS - 4] = below[4:]
        values = below[:4] if values is None else values + below[:4]
    side[...] = jnp.zeros_like(side)
    for which, part in enumerate(pieces_of(values)):
        side[which * 4 : which * 4 + 4, :] = part
    out_ref[4 * LANES :] = side[...].astype(jnp.bfloat16)


def band_kernel(here_ref, there_ref, band_ref, whole):
    core = lax.axis_index("state")
    block_num = here_ref.shape[0]
    for source, side in ((here_ref, core), (there_ref, 1 - core)):
        for block in range(block_num):
            for at in range(VECTORS - 4):
                lanes = pl.ds(pl.multiple_of((2 * side + at % 2) * LANES, LANES), LANES)
                whole[at // 2, block : block + 1, lanes] = source[block, at : at + 1]
    band = band_of(whole[0], whole[1]) + [whole[2]]
    for at, values in enumerate(band):
        for block in range(block_num):
            band_ref[block, at : at + 1, :] = values[block : block + 1]


def chain(grams, vectors, bands, state, states_ref, innovations_ref):
    width = state.shape[1]
    line = lax.broadcasted_iota(jnp.int32, (16, width), 0)
    for block in range(grams.shape[0]):
        info, diagonal = vectors[block, 0:1, :], vectors[block, 1:2, :]
        band = bands[block, : 2 * STEPS + 1, :]
        high, middle, low = pieces_of(state)
        split = jnp.where(line == 0, high, jnp.where(line == 1, middle, jnp.where(line == 2, low, 0.0)))
        product = jnp.dot(
            split.astype(jnp.bfloat16), grams[block], preferred_element_type=jnp.float32
        )
        product = jnp.sum(product, axis=0, keepdims=True) + diagonal * state
        trace_val = jnp.sum(diagonal, axis=1, keepdims=True)
        lam_val = width / (2.0 * (width + trace_val))
        innovation = -lam_val * apply_band(product - info, band)
        state = apply_band(state, band) + innovation
        states_ref[block : block + 1, :] = state
        innovations_ref[block : block + 1, :] = innovation


def assemble_kernel(number, *refs):
    own, other, rest = refs[:number], refs[number : 2 * number], refs[2 * number :]
    bands, state_ref, grams, vectors, states_ref, innovations_ref = rest
    core, position = lax.axis_index("state"), lax.axis_index("tm")
    half = 2 * LANES
    line = lax.broadcasted_iota(jnp.int32, (LANES, LANES), 0)
    column = lax.broadcasted_iota(jnp.int32, (LANES, LANES), 1)
    for turn in range(number):
        flip, flip_other = flip_here(turn, number), flip_here(turn, number, 1)
        for pieces, side, block in (
            (own[turn], core, position ^ flip),
            (other[turn], 1 - core, position ^ flip_other),
        ):

            def piece(index):
                return pieces[index * LANES : (index + 1) * LANES, :]

            def put(row, column, values):
                row, column = pl.multiple_of(row, LANES), pl.multiple_of(column, LANES)
                grams[block, pl.ds(row, LANES), pl.ds(column, LANES)] = values.astype(jnp.bfloat16)

            here, there = side * half, (1 - side) * half
            packed = piece(0).astype(jnp.float32)
            turned = packed.T
            put(here, here, jnp.where(line < column, packed, turned))
            put(here + LANES, here + LANES, jnp.where(line > column, packed, turned))
            put(here, here + LANES, piece(1))
            put(here + LANES, here, piece(1).T)
            for index in range(2):
                beyond = there + (index ^ side) * LANES
                put(here + index * LANES, beyond, piece(2 + index))
                put(beyond, here + index * LANES, piece(2 + index).T)
            below = pieces[4 * LANES :, :].astype(jnp.float32)
            below = below[:4] + below[4:8] + below[8:12]
            for at in range(4):
                lanes = pl.ds(pl.multiple_of(here + (at % 2) * LANES, LANES), LANES)
                vectors[block, at // 2 : at // 2 + 1, lanes] = below[at : at + 1]
    chain(grams, vectors, bands, state_ref[...], states_ref, innovations_ref)


def chain_kernel(grams, vectors, bands, state_ref, states_ref, innovations_ref):
    chain(grams, vectors, bands, state_ref[...], states_ref, innovations_ref)


def shards(rows_h, rows_y, tile_block, tile_count, kappa, rate, smooth_gain, start_state):
    tm_size, grp_size = lax.axis_size("tm"), lax.axis_size("grp")
    state_size = lax.axis_size("state")
    tm_index, grp_index, core = (lax.axis_index(name) for name in ("tm", "grp", "state"))
    tile_num, row_num, half = rows_h.shape[1:]
    width = kappa.shape[2]
    own = rows_h[0]
    other = lax.ppermute(own, "state", [(i, (i + 1) % state_size) for i in range(state_size)])
    state = start_state.reshape(1, width)
    direct = tm_size in FLIPS
    states_shape = jax.ShapeDtypeStruct((tm_size, width), jnp.float32)

    def flip_over(array, turn):
        pairs = [
            (i * state_size + j, (i ^ flip_of(turn, tm_size, j)) * state_size + j)
            for i in range(tm_size)
            for j in range(state_size)
        ]
        return lax.ppermute(array, ("tm", "state"), pairs)

    def ring(array, step):
        return lax.ppermute(array, "grp", [(i, (i + step) % grp_size) for i in range(grp_size)])

    def across(array):
        return lax.ppermute(array, "state", [(i, (i + 1) % state_size) for i in range(state_size)])

    if direct:
        row = lax.broadcasted_iota(jnp.int32, own.shape, 1)
        valid = jnp.where(row < tile_count[0][:, None, None], own, jnp.zeros((), own.dtype))
        second_half = jax.ShapeDtypeStruct((2 * LANES, LANES), jnp.bfloat16)
        blocks = tile_block[0, :, 0]
        *pieces, turned = pl.pallas_call(
            half_kernel,
            out_shape=[jax.ShapeDtypeStruct((2 * LANES + 32, LANES), jnp.bfloat16)] * tm_size
            + [jax.ShapeDtypeStruct((tile_num, half, row_num), jnp.bfloat16)],
            in_specs=[SMEM] + [VMEM] * 5,
            out_specs=[VMEM] * (tm_size + 1),
            scratch_shapes=[
                pltpu.VMEM((tm_size, 3 * LANES, LANES), jnp.float32),
                pltpu.VMEM((tm_size, 8, half), jnp.float32),
                pltpu.VMEM((32, LANES), jnp.float32),
                pltpu.VMEM((tile_num, row_num), jnp.float32),
            ],
            compiler_params=KERNEL,
        )(blocks, rows_y[0], valid, kappa[0], rate[0], smooth_gain[0])
        turns = range(tm_size - 1)
        parts = [flip_over(pieces[turn], turn) for turn in turns] + [pieces[-1]]
        pieces2 = pl.pallas_call(
            cross_kernel,
            out_shape=[second_half] * tm_size,
            in_specs=[SMEM] + [VMEM] * 2,
            out_specs=[VMEM] * tm_size,
            scratch_shapes=[pltpu.VMEM((tm_size, 2 * LANES, LANES), jnp.float32)],
            compiler_params=KERNEL,
        )(blocks, turned, other)
        parts2 = [flip_over(pieces2[turn], turn) for turn in turns] + [pieces2[-1]]
        half_coefficients = jax.ShapeDtypeStruct((tm_size, 8, LANES), jnp.float32)
        own_sum, here = pl.pallas_call(
            sum_kernel,
            out_shape=(jax.ShapeDtypeStruct((4 * LANES + 16, LANES), jnp.bfloat16), half_coefficients),
            in_specs=[VMEM] * (2 * tm_size),
            out_specs=(VMEM, VMEM),
            scratch_shapes=[pltpu.VMEM((16, LANES), jnp.float32)],
            compiler_params=KERNEL,
        )(*parts, *parts2)
        own_sums = [flip_over(own_sum, turn) for turn in turns] + [own_sum]
        bands = pl.pallas_call(
            band_kernel,
            out_shape=jax.ShapeDtypeStruct((tm_size, 16, width), jnp.float32),
            in_specs=[VMEM, VMEM],
            out_specs=VMEM,
            scratch_shapes=[pltpu.VMEM((3, tm_size, width), jnp.float32)],
            compiler_params=KERNEL,
        )(here, across(here))
        bands, own_sums[0] = lax.optimization_barrier((bands, own_sums[0]))
        other_sums = [across(values) for values in own_sums]
        grams, vectors, new_states, new_innovations = pl.pallas_call(
            functools.partial(assemble_kernel, tm_size),
            out_shape=(
                jax.ShapeDtypeStruct((tm_size, width, width), jnp.bfloat16),
                jax.ShapeDtypeStruct((tm_size, 8, width), jnp.float32),
                states_shape,
                states_shape,
            ),
            in_specs=[VMEM] * (2 * tm_size + 2),
            out_specs=[VMEM] * 4,
            compiler_params=KERNEL,
        )(*own_sums, *other_sums, bands, state)
        gains = bands[:, 2 * STEPS + 1]

        def run_group(state, group):
            if group == 0:
                return new_states, new_innovations
            return pl.pallas_call(
                chain_kernel,
                out_shape=(states_shape, states_shape),
                in_specs=[VMEM] * 4,
                out_specs=(VMEM, VMEM),
                compiler_params=KERNEL,
            )(grams, vectors, bands, state)
    else:
        readings = rows_y[0].astype(jnp.float32)
        meta = jnp.concatenate(
            [tile_block[0, :, 0], tile_count[0], jnp.stack([core, tm_index]).astype(jnp.int32)]
        )
        params = jnp.concatenate([kappa[0], rate[0], smooth_gain[0]], axis=0)
        gathered = lax.all_gather(params, "tm")
        gains = gathered[:, 2]
        vector = jax.ShapeDtypeStruct((1, width), jnp.float32)
        partial = jax.ShapeDtypeStruct((1, width + LANES), jnp.float32)
        acc = pltpu.VMEM((GROUP_ROWS, width + LANES), jnp.float32)

        def run_group(state, group):
            part = pl.pallas_call(
                functools.partial(first_kernel, 0),
                out_shape=partial,
                in_specs=[SMEM] + [VMEM] * 4,
                out_specs=VMEM,
                scratch_shapes=[acc],
                compiler_params=KERNEL,
            )(meta, readings, own, other, state)

            def lap(block, carry):
                state, part, states, innovations = carry
                here = lax.dynamic_index_in_dim(gathered, block, 0, False)
                own_meta = meta.at[2 * tile_num + 1].set((block + 1).astype(jnp.int32))
                state, innovation, part = pl.pallas_call(
                    step_kernel,
                    out_shape=(vector, vector, partial),
                    in_specs=[VMEM, SMEM] + [VMEM] * 6,
                    out_specs=(VMEM, VMEM, VMEM),
                    scratch_shapes=[acc],
                    compiler_params=KERNEL,
                )(lax.psum(part, "tm"), own_meta, readings, own, other, state, here[0:1], here[1:2])
                states = lax.dynamic_update_slice_in_dim(states, state, block, 0)
                innovations = lax.dynamic_update_slice_in_dim(innovations, innovation, block, 0)
                return state, part, states, innovations

            empty = jnp.zeros((tm_size, width), jnp.float32)
            return lax.fori_loop(0, tm_size, lap, (state, part, empty, empty))[2:]

    states = innovations = jnp.zeros((tm_size, width), jnp.float32)
    for group in range(grp_size):
        new_states, new_innovations = run_group(state, group)
        mine = grp_index == group
        states = jnp.where(mine, new_states, states)
        innovations = jnp.where(mine, new_innovations, innovations)
        if group < grp_size - 1:
            state = ring(new_states[-1:], 1)

    residual = jnp.zeros((1, width), jnp.float32)
    residuals = [None] * tm_size
    for group in reversed(range(grp_size)):
        running = residual
        for block in reversed(range(tm_size)):
            residuals[block] = running
            running = gains[block][None] * (running + innovations[block][None])
        if group > 0:
            arrived = ring(running, -1)
            residual = jnp.where(grp_index == group - 1, arrived, residual)
    smoothed = states + jnp.concatenate(residuals, 0)

    def out(values):
        piece = lax.dynamic_slice(values, (tm_index, core * half), (1, half))
        return piece.reshape(1, 1, half)

    return out(states), out(smoothed)


def solution(mesh):
    return jax.shard_map(
        shards,
        mesh=mesh,
        in_specs=(
            P(("runs", "grp"), "tm", None, "state"),
            P(("runs", "grp"), "tm", None),
            P(("runs", "grp"), "tm", None),
            P(("runs", "grp"), "tm"),
            P(("runs", "grp"), "tm", None),
            P(("runs", "grp"), "tm", None),
            P(("runs", "grp"), "tm", None),
            P("runs"),
        ),
        out_specs=(P(("runs", "grp"), "tm", "state"), P(("runs", "grp"), "tm", "state")),
        check_vma=False,
    )
```

```python
import functools

import jax
import jax.numpy as jnp
from jax import lax
from jax.experimental import pallas as pl
from jax.experimental.pallas import tpu as pltpu
from jax.sharding import PartitionSpec as P

STEPS = 4
LANES = 128
GROUP_ROWS = 16
VECTORS = 10
FLIPS = {1: (), 2: (1,), 4: (2, 1, 3)}

VMEM = pl.BlockSpec(memory_space=pltpu.VMEM)
KERNEL = pltpu.CompilerParams(vmem_limit_bytes=16 * 2**20)
SMEM = pl.BlockSpec(memory_space=pltpu.SMEM)


def stencil(field, coeff, decay):
    width = field.shape[1]
    cell = lax.broadcasted_iota(jnp.int32, field.shape, 1)
    for _ in range(STEPS):
        upper_cell = jnp.where(cell == 0, 0.0, pltpu.roll(field, 1, 1))
        lower_cell = jnp.where(cell == width - 1, 0.0, pltpu.roll(field, width - 1, 1))
        field = field + coeff * (upper_cell + lower_cell - 2.0 * field) - decay * field
    return field


def band_of(coeff, decay):
    width = coeff.shape[1]
    cell = lax.broadcasted_iota(jnp.int32, coeff.shape, 1)
    from_upper = jnp.where(cell == 0, 0.0, coeff)
    from_lower = jnp.where(cell == width - 1, 0.0, coeff)
    stay = 1.0 - 2.0 * coeff - decay
    band = {-1: from_upper, 0: stay, 1: from_lower}
    for _ in range(STEPS - 1):
        longer = {}
        for offset, values in band.items():
            for step, weight, turned in (
                (-1, from_upper, lambda: pltpu.roll(values, 1, 1)),
                (0, stay, lambda: values),
                (1, from_lower, lambda: pltpu.roll(values, width - 1, 1)),
            ):
                term = weight * turned()
                longer[offset + step] = longer[offset + step] + term if offset + step in longer else term
        band = longer
    return [band[offset] for offset in range(-STEPS, STEPS + 1)]


def apply_band(field, band):
    width = field.shape[1]
    total = band[STEPS : STEPS + 1] * field
    for offset in range(1, STEPS + 1):
        total = total + (
            band[STEPS - offset : STEPS - offset + 1] * pltpu.roll(field, offset, 1)
            + band[STEPS + offset : STEPS + offset + 1] * pltpu.roll(field, width - offset, 1)
        )
    return total


def row_pass(block, state, meta, y_ref, own_ref, other_ref, acc, part_ref):
    tile_num, row_num, half = own_ref.shape
    core = meta[2 * tile_num]
    own_at = pl.multiple_of(core * half, half)
    other_at = pl.multiple_of((1 - core) * half, half)
    state_own = state[:, pl.ds(own_at, half)]
    state_other = state[:, pl.ds(other_at, half)]
    lane = lax.broadcasted_iota(jnp.int32, (GROUP_ROWS, LANES), 1)
    row = lax.broadcasted_iota(jnp.int32, (GROUP_ROWS, LANES), 0)
    acc[...] = jnp.zeros_like(acc)

    def fold(values):
        total = values[:, :LANES]
        for start in range(LANES, half, LANES):
            total = total + values[:, start : start + LANES]
        return total

    def tile(index, carry):
        @pl.when(meta[index] == block)
        def _():
            live = meta[tile_num + index]
            readings = y_ref[pl.ds(index, 1), :]
            sum_own = jnp.zeros((GROUP_ROWS, half), jnp.float32)
            sum_other = jnp.zeros((GROUP_ROWS, half), jnp.float32)
            squares = jnp.zeros((GROUP_ROWS, LANES), jnp.float32)
            for start in range(0, row_num, GROUP_ROWS):
                own = own_ref[index, start : start + GROUP_ROWS, :].astype(jnp.float32)
                other = other_ref[index, start : start + GROUP_ROWS, :].astype(jnp.float32)
                valid = row + start < live
                product = fold(own * state_own) + fold(other * state_other)
                product = product - jnp.where(lane == row + start, readings, 0.0)
                weight = jnp.sum(product, axis=1, keepdims=True)
                weight = jnp.where(valid[:, :1], weight, 0.0)
                sum_own = sum_own + own * weight
                sum_other = sum_other + other * weight
                squares = squares + jnp.where(valid, fold(own * own) + fold(other * other), 0.0)
            acc[:, :half] += sum_own
            acc[:, half : 2 * half] += sum_other
            acc[:, 2 * half :] += squares

        return carry

    lax.fori_loop(0, tile_num, tile, 0)
    totals = jnp.sum(acc[...], axis=0, keepdims=True)
    part_ref[:, pl.ds(own_at, half)] = totals[:, :half]
    part_ref[:, pl.ds(other_at, half)] = totals[:, half : 2 * half]
    part_ref[:, 2 * half :] = totals[:, 2 * half :]


def first_kernel(block, meta, y_ref, own_ref, other_ref, state_ref, part_ref, acc):
    row_pass(block, state_ref, meta, y_ref, own_ref, other_ref, acc, part_ref)


def step_kernel(
    total_ref, meta, y_ref, own_ref, other_ref, state_ref, kappa_ref, rate_ref,
    next_ref, innovation_ref, part_ref, acc,
):
    width = state_ref.shape[1]
    trace_val = jnp.sum(total_ref[:, width:], axis=1, keepdims=True)
    lam_val = width / (2.0 * (width + trace_val))
    coeff, decay = kappa_ref[...], rate_ref[...]
    innovation = -lam_val * stencil(total_ref[:, :width], coeff, decay)
    next_ref[...] = stencil(state_ref[...], coeff, decay) + innovation
    innovation_ref[...] = innovation
    block = meta[2 * y_ref.shape[0] + 1]
    row_pass(block, next_ref, meta, y_ref, own_ref, other_ref, acc, part_ref)


def pieces_of(values):
    high = values.astype(jnp.bfloat16).astype(jnp.float32)
    middle = (values - high).astype(jnp.bfloat16).astype(jnp.float32)
    return high, middle, values - high - middle


def flip_of(turn, number, core):
    return FLIPS[number][:: 1 - 2 * core][turn]


def flip_here(turn, number, beside=0):
    if turn == number - 1:
        return 0
    on_core = [flip_of(turn, number, core) for core in range(2)]
    return jnp.where(lax.axis_index("state") == beside, on_core[0], on_core[1])


def half_kernel(blocks, y_ref, own_ref, kappa_ref, rate_ref, gain_ref, *refs):
    outs, (turned_ref, acc, vec, side, readings) = refs[:-5], refs[-5:]
    tile_num, row_num, _ = own_ref.shape
    number = len(outs)
    core, position = lax.axis_index("state"), lax.axis_index("tm")
    acc[...] = jnp.zeros_like(acc)
    vec[...] = jnp.zeros_like(vec)
    side[...] = jnp.zeros_like(side)
    readings[...] = y_ref[...].astype(jnp.float32)
    for index in range(tile_num):
        block = blocks[index]
        rows = own_ref[index]
        turned = rows.T
        turned_ref[index] = turned
        square = jnp.dot(turned, rows, preferred_element_type=jnp.float32)
        acc[block, 0:LANES] += square[:LANES, :LANES]
        acc[block, LANES : 2 * LANES] += square[:LANES, LANES:]
        acc[block, 2 * LANES : 3 * LANES] += square[LANES:, LANES:]
        values = jnp.broadcast_to(readings[index : index + 1, :], (8, row_num))
        vec[block] += jnp.dot(
            values.astype(jnp.bfloat16), rows, preferred_element_type=jnp.float32
        )
    line = lax.broadcasted_iota(jnp.int32, (LANES, LANES), 0)
    column = lax.broadcasted_iota(jnp.int32, (LANES, LANES), 1)
    for turn, out_ref in enumerate(outs):
        block = position ^ flip_here(turn, number)
        first, between, second = (acc[block, at * LANES : (at + 1) * LANES] for at in range(3))
        packed = jnp.where(line < column, first, jnp.where(line > column, second, 0.0))
        out_ref[0:LANES] = packed.astype(jnp.bfloat16)
        out_ref[LANES : 2 * LANES] = between.astype(jnp.bfloat16)
        values = [vec[block, 0:1, :LANES], vec[block, 0:1, LANES:]]
        for square in (first, second):
            values.append(jnp.sum(jnp.where(line == column, square, 0.0), axis=0, keepdims=True))
        for coefficient in (kappa_ref, rate_ref, gain_ref):
            for piece in range(2):
                at = pl.multiple_of((2 * core + piece) * LANES, LANES)
                values.append(coefficient[:, pl.ds(at, LANES)])
        for at, value in enumerate(values):
            for which, part in enumerate(pieces_of(value)):
                side[which * VECTORS + at : which * VECTORS + at + 1, :] = part
        out_ref[2 * LANES :] = side[...].astype(jnp.bfloat16)


def cross_kernel(blocks, turned_ref, other_ref, *refs):
    outs, acc = refs[:-1], refs[-1]
    number = len(outs)
    core, position = lax.axis_index("state"), lax.axis_index("tm")
    acc[...] = jnp.zeros_like(acc)
    for index in range(other_ref.shape[0]):
        block = blocks[index]
        for piece in range(2):
            at = pl.multiple_of((piece ^ core) * LANES, LANES)
            acc[block, piece * LANES : (piece + 1) * LANES] += jnp.dot(
                turned_ref[index, piece * LANES : (piece + 1) * LANES, :],
                other_ref[index, :, pl.ds(at, LANES)],
                preferred_element_type=jnp.float32,
            )
    for turn, out_ref in enumerate(outs):
        out_ref[...] = acc[position ^ flip_here(turn, number)].astype(jnp.bfloat16)


def sum_kernel(*refs):
    parts, (out_ref, coefficients, side) = refs[:-3], refs[-3:]
    number = len(parts) // 2
    position = lax.axis_index("tm")
    for at, some in enumerate((parts[:number], parts[number:])):
        total = some[0][: 2 * LANES].astype(jnp.float32)
        for part in some[1:]:
            total = total + part[: 2 * LANES].astype(jnp.float32)
        out_ref[2 * at * LANES : 2 * (at + 1) * LANES] = total.astype(jnp.bfloat16)
    values = None
    for turn, part in enumerate(parts[:number]):
        below = part[2 * LANES :].astype(jnp.float32)
        below = below[:VECTORS] + below[VECTORS : 2 * VECTORS] + below[2 * VECTORS : 3 * VECTORS]
        coefficients[position ^ flip_here(turn, number), 0 : VECTORS - 4] = below[4:]
        values = below[:4] if values is None else values + below[:4]
    side[...] = jnp.zeros_like(side)
    for which, part in enumerate(pieces_of(values)):
        side[which * 4 : which * 4 + 4, :] = part
    out_ref[4 * LANES :] = side[...].astype(jnp.bfloat16)


def band_kernel(here_ref, there_ref, band_ref, whole):
    core = lax.axis_index("state")
    block_num = here_ref.shape[0]
    for source, side in ((here_ref, core), (there_ref, 1 - core)):
        for block in range(block_num):
            for at in range(VECTORS - 4):
                lanes = pl.ds(pl.multiple_of((2 * side + at % 2) * LANES, LANES), LANES)
                whole[at // 2, block : block + 1, lanes] = source[block, at : at + 1]
    band = band_of(whole[0], whole[1]) + [whole[2]]
    for at, values in enumerate(band):
        for block in range(block_num):
            band_ref[block, at : at + 1, :] = values[block : block + 1]


def chain(grams, vectors, bands, state, states_ref, innovations_ref):
    width = state.shape[1]
    line = lax.broadcasted_iota(jnp.int32, (16, width), 0)
    for block in range(grams.shape[0]):
        info, diagonal = vectors[block, 0:1, :], vectors[block, 1:2, :]
        band = bands[block, : 2 * STEPS + 1, :]
        high, middle, low = pieces_of(state)
        split = jnp.where(line == 0, high, jnp.where(line == 1, middle, jnp.where(line == 2, low, 0.0)))
        product = jnp.dot(
            split.astype(jnp.bfloat16), grams[block], preferred_element_type=jnp.float32
        )
        product = jnp.sum(product, axis=0, keepdims=True) + diagonal * state
        trace_val = jnp.sum(diagonal, axis=1, keepdims=True)
        lam_val = width / (2.0 * (width + trace_val))
        innovation = -lam_val * apply_band(product - info, band)
        state = apply_band(state, band) + innovation
        states_ref[block : block + 1, :] = state
        innovations_ref[block : block + 1, :] = innovation


def put_grams(number, turns, own, other, grams, vectors):
    core, position = lax.axis_index("state"), lax.axis_index("tm")
    half = 2 * LANES
    line = lax.broadcasted_iota(jnp.int32, (LANES, LANES), 0)
    column = lax.broadcasted_iota(jnp.int32, (LANES, LANES), 1)
    for at, turn in enumerate(turns):
        flip, flip_other = flip_here(turn, number), flip_here(turn, number, 1)
        for pieces, side, block in (
            (own[at], core, position ^ flip),
            (other[at], 1 - core, position ^ flip_other),
        ):

            def piece(index):
                return pieces[index * LANES : (index + 1) * LANES, :]

            def put(row, column, values):
                row, column = pl.multiple_of(row, LANES), pl.multiple_of(column, LANES)
                grams[block, pl.ds(row, LANES), pl.ds(column, LANES)] = values.astype(jnp.bfloat16)

            here, there = side * half, (1 - side) * half
            packed = piece(0).astype(jnp.float32)
            turned = packed.T
            put(here, here, jnp.where(line < column, packed, turned))
            put(here + LANES, here + LANES, jnp.where(line > column, packed, turned))
            put(here, here + LANES, piece(1))
            put(here + LANES, here, piece(1).T)
            for index in range(2):
                beyond = there + (index ^ side) * LANES
                put(here + index * LANES, beyond, piece(2 + index))
                put(beyond, here + index * LANES, piece(2 + index).T)
            below = pieces[4 * LANES :, :].astype(jnp.float32)
            below = below[:4] + below[4:8] + below[8:12]
            for vector in range(4):
                lanes = pl.ds(pl.multiple_of(here + (vector % 2) * LANES, LANES), LANES)
                vectors[block, vector // 2 : vector // 2 + 1, lanes] = below[vector : vector + 1]


def early_kernel(number, turns, *refs):
    count = len(turns)
    put_grams(number, turns, refs[:count], refs[count : 2 * count], refs[-2], refs[-1])


def assemble_kernel(number, turns, *refs):
    count = len(turns)
    own, other, rest = refs[:count], refs[count : 2 * count], refs[2 * count :]
    _, _, bands, state_ref, grams, vectors, states_ref, innovations_ref = rest
    put_grams(number, turns, own, other, grams, vectors)
    chain(grams, vectors, bands, state_ref[...], states_ref, innovations_ref)


def chain_kernel(grams, vectors, bands, state_ref, states_ref, innovations_ref):
    chain(grams, vectors, bands, state_ref[...], states_ref, innovations_ref)


def shards(rows_h, rows_y, tile_block, tile_count, kappa, rate, smooth_gain, start_state):
    tm_size, grp_size = lax.axis_size("tm"), lax.axis_size("grp")
    state_size = lax.axis_size("state")
    tm_index, grp_index, core = (lax.axis_index(name) for name in ("tm", "grp", "state"))
    tile_num, row_num, half = rows_h.shape[1:]
    width = kappa.shape[2]
    own = rows_h[0]
    other = lax.ppermute(own, "state", [(i, (i + 1) % state_size) for i in range(state_size)])
    state = start_state.reshape(1, width)
    direct = tm_size in FLIPS
    states_shape = jax.ShapeDtypeStruct((tm_size, width), jnp.float32)

    def flip_over(array, turn):
        pairs = [
            (i * state_size + j, (i ^ flip_of(turn, tm_size, j)) * state_size + j)
            for i in range(tm_size)
            for j in range(state_size)
        ]
        return lax.ppermute(array, ("tm", "state"), pairs)

    def ring(array, step):
        pairs = [
            (i * state_size + j, (i + step) % grp_size * state_size + state_size - 1 - j)
            for i in range(grp_size)
            for j in range(state_size)
        ]
        return lax.ppermute(array, ("grp", "state"), pairs)

    def across(array):
        return lax.ppermute(array, "state", [(i, (i + 1) % state_size) for i in range(state_size)])

    if direct:
        row = lax.broadcasted_iota(jnp.int32, own.shape, 1)
        valid = jnp.where(row < tile_count[0][:, None, None], own, jnp.zeros((), own.dtype))
        second_half = jax.ShapeDtypeStruct((2 * LANES, LANES), jnp.bfloat16)
        blocks = tile_block[0, :, 0]
        *pieces, turned = pl.pallas_call(
            half_kernel,
            out_shape=[jax.ShapeDtypeStruct((2 * LANES + 32, LANES), jnp.bfloat16)] * tm_size
            + [jax.ShapeDtypeStruct((tile_num, half, row_num), jnp.bfloat16)],
            in_specs=[SMEM] + [VMEM] * 5,
            out_specs=[VMEM] * (tm_size + 1),
            scratch_shapes=[
                pltpu.VMEM((tm_size, 3 * LANES, LANES), jnp.float32),
                pltpu.VMEM((tm_size, 8, half), jnp.float32),
                pltpu.VMEM((32, LANES), jnp.float32),
                pltpu.VMEM((tile_num, row_num), jnp.float32),
            ],
            compiler_params=KERNEL,
        )(blocks, rows_y[0], valid, kappa[0], rate[0], smooth_gain[0])
        turns = range(tm_size - 1)
        parts = [flip_over(pieces[turn], turn) for turn in turns] + [pieces[-1]]
        pieces2 = pl.pallas_call(
            cross_kernel,
            out_shape=[second_half] * tm_size,
            in_specs=[SMEM] + [VMEM] * 2,
            out_specs=[VMEM] * tm_size,
            scratch_shapes=[pltpu.VMEM((tm_size, 2 * LANES, LANES), jnp.float32)],
            compiler_params=KERNEL,
        )(blocks, turned, other)
        parts2 = [flip_over(pieces2[turn], turn) for turn in turns] + [pieces2[-1]]
        half_coefficients = jax.ShapeDtypeStruct((tm_size, 8, LANES), jnp.float32)
        own_sum, here = pl.pallas_call(
            sum_kernel,
            out_shape=(jax.ShapeDtypeStruct((4 * LANES + 16, LANES), jnp.bfloat16), half_coefficients),
            in_specs=[VMEM] * (2 * tm_size),
            out_specs=(VMEM, VMEM),
            scratch_shapes=[pltpu.VMEM((16, LANES), jnp.float32)],
            compiler_params=KERNEL,
        )(*parts, *parts2)
        own_sums = [flip_over(own_sum, turn) for turn in turns] + [own_sum]
        bands = pl.pallas_call(
            band_kernel,
            out_shape=jax.ShapeDtypeStruct((tm_size, 16, width), jnp.float32),
            in_specs=[VMEM, VMEM],
            out_specs=VMEM,
            scratch_shapes=[pltpu.VMEM((3, tm_size, width), jnp.float32)],
            compiler_params=KERNEL,
        )(here, across(here))
        bands, own_sums[0] = lax.optimization_barrier((bands, own_sums[0]))
        other_sums = [across(values) for values in own_sums]
        whole = (
            jax.ShapeDtypeStruct((tm_size, width, width), jnp.bfloat16),
            jax.ShapeDtypeStruct((tm_size, 8, width), jnp.float32),
        )
        late = [tm_size - 2]
        early = [turn for turn in range(tm_size) if turn not in late]
        arrays = [own_sums[turn] for turn in early] + [other_sums[turn] for turn in early]
        grams, vectors = pl.pallas_call(
            functools.partial(early_kernel, tm_size, early),
            out_shape=whole,
            in_specs=[VMEM] * len(arrays),
            out_specs=[VMEM] * 2,
            compiler_params=KERNEL,
        )(*arrays)
        arrays = [own_sums[turn] for turn in late] + [other_sums[turn] for turn in late]
        grams, vectors, new_states, new_innovations = pl.pallas_call(
            functools.partial(assemble_kernel, tm_size, late),
            out_shape=whole + (states_shape, states_shape),
            in_specs=[VMEM] * (len(arrays) + 4),
            out_specs=[VMEM] * 4,
            input_output_aliases={len(arrays): 0, len(arrays) + 1: 1},
            compiler_params=KERNEL,
        )(*arrays, grams, vectors, bands, state)
        gains = bands[:, 2 * STEPS + 1]

        def run_group(state, group):
            if group == 0:
                return new_states, new_innovations
            return pl.pallas_call(
                chain_kernel,
                out_shape=(states_shape, states_shape),
                in_specs=[VMEM] * 4,
                out_specs=(VMEM, VMEM),
                compiler_params=KERNEL,
            )(grams, vectors, bands, state)
    else:
        readings = rows_y[0].astype(jnp.float32)
        meta = jnp.concatenate(
            [tile_block[0, :, 0], tile_count[0], jnp.stack([core, tm_index]).astype(jnp.int32)]
        )
        params = jnp.concatenate([kappa[0], rate[0], smooth_gain[0]], axis=0)
        gathered = lax.all_gather(params, "tm")
        gains = gathered[:, 2]
        vector = jax.ShapeDtypeStruct((1, width), jnp.float32)
        partial = jax.ShapeDtypeStruct((1, width + LANES), jnp.float32)
        acc = pltpu.VMEM((GROUP_ROWS, width + LANES), jnp.float32)

        def run_group(state, group):
            part = pl.pallas_call(
                functools.partial(first_kernel, 0),
                out_shape=partial,
                in_specs=[SMEM] + [VMEM] * 4,
                out_specs=VMEM,
                scratch_shapes=[acc],
                compiler_params=KERNEL,
            )(meta, readings, own, other, state)

            def lap(block, carry):
                state, part, states, innovations = carry
                here = lax.dynamic_index_in_dim(gathered, block, 0, False)
                own_meta = meta.at[2 * tile_num + 1].set((block + 1).astype(jnp.int32))
                state, innovation, part = pl.pallas_call(
                    step_kernel,
                    out_shape=(vector, vector, partial),
                    in_specs=[VMEM, SMEM] + [VMEM] * 6,
                    out_specs=(VMEM, VMEM, VMEM),
                    scratch_shapes=[acc],
                    compiler_params=KERNEL,
                )(lax.psum(part, "tm"), own_meta, readings, own, other, state, here[0:1], here[1:2])
                states = lax.dynamic_update_slice_in_dim(states, state, block, 0)
                innovations = lax.dynamic_update_slice_in_dim(innovations, innovation, block, 0)
                return state, part, states, innovations

            empty = jnp.zeros((tm_size, width), jnp.float32)
            return lax.fori_loop(0, tm_size, lap, (state, part, empty, empty))[2:]

    states = innovations = jnp.zeros((tm_size, width), jnp.float32)
    for group in range(grp_size):
        new_states, new_innovations = run_group(state, group)
        mine = grp_index == group
        states = jnp.where(mine, new_states, states)
        innovations = jnp.where(mine, new_innovations, innovations)
        if group < grp_size - 1:
            state = ring(new_states[-1:], 1)

    residual = jnp.zeros((1, width), jnp.float32)
    residuals = [None] * tm_size
    for group in reversed(range(grp_size)):
        running = residual
        for block in reversed(range(tm_size)):
            residuals[block] = running
            running = gains[block][None] * (running + innovations[block][None])
        if group > 0:
            arrived = ring(running, -1)
            residual = jnp.where(grp_index == group - 1, arrived, residual)
    smoothed = states + jnp.concatenate(residuals, 0)

    def out(values):
        piece = lax.dynamic_slice(values, (tm_index, core * half), (1, half))
        return piece.reshape(1, 1, half)

    return out(states), out(smoothed)


def solution(mesh):
    return jax.shard_map(
        shards,
        mesh=mesh,
        in_specs=(
            P(("runs", "grp"), "tm", None, "state"),
            P(("runs", "grp"), "tm", None),
            P(("runs", "grp"), "tm", None),
            P(("runs", "grp"), "tm"),
            P(("runs", "grp"), "tm", None),
            P(("runs", "grp"), "tm", None),
            P(("runs", "grp"), "tm", None),
            P("runs"),
        ),
        out_specs=(P(("runs", "grp"), "tm", "state"), P(("runs", "grp"), "tm", "state")),
        check_vma=False,
    )
```

```python
import functools

import jax
import jax.numpy as jnp
from jax import lax
from jax.experimental import pallas as pl
from jax.experimental.pallas import tpu as pltpu
from jax.sharding import PartitionSpec as P

STEPS = 4
LANES = 128
GROUP_ROWS = 16
VECTORS = 10
FLIPS = {1: (), 2: (1,), 4: (2, 1, 3)}

VMEM = pl.BlockSpec(memory_space=pltpu.VMEM)
KERNEL = pltpu.CompilerParams(vmem_limit_bytes=16 * 2**20)
SMEM = pl.BlockSpec(memory_space=pltpu.SMEM)


def stencil(field, coeff, decay):
    width = field.shape[1]
    cell = lax.broadcasted_iota(jnp.int32, field.shape, 1)
    for _ in range(STEPS):
        upper_cell = jnp.where(cell == 0, 0.0, pltpu.roll(field, 1, 1))
        lower_cell = jnp.where(cell == width - 1, 0.0, pltpu.roll(field, width - 1, 1))
        field = field + coeff * (upper_cell + lower_cell - 2.0 * field) - decay * field
    return field


def band_of(coeff, decay):
    width = coeff.shape[1]
    cell = lax.broadcasted_iota(jnp.int32, coeff.shape, 1)
    from_upper = jnp.where(cell == 0, 0.0, coeff)
    from_lower = jnp.where(cell == width - 1, 0.0, coeff)
    stay = 1.0 - 2.0 * coeff - decay
    band = {-1: from_upper, 0: stay, 1: from_lower}
    for _ in range(STEPS - 1):
        longer = {}
        for offset, values in band.items():
            for step, weight, turned in (
                (-1, from_upper, lambda: pltpu.roll(values, 1, 1)),
                (0, stay, lambda: values),
                (1, from_lower, lambda: pltpu.roll(values, width - 1, 1)),
            ):
                term = weight * turned()
                longer[offset + step] = longer[offset + step] + term if offset + step in longer else term
        band = longer
    return [band[offset] for offset in range(-STEPS, STEPS + 1)]


def apply_band(field, band):
    width = field.shape[1]
    total = band[STEPS : STEPS + 1] * field
    for offset in range(1, STEPS + 1):
        total = total + (
            band[STEPS - offset : STEPS - offset + 1] * pltpu.roll(field, offset, 1)
            + band[STEPS + offset : STEPS + offset + 1] * pltpu.roll(field, width - offset, 1)
        )
    return total


def row_pass(block, state, meta, y_ref, own_ref, other_ref, acc, part_ref):
    tile_num, row_num, half = own_ref.shape
    core = meta[2 * tile_num]
    own_at = pl.multiple_of(core * half, half)
    other_at = pl.multiple_of((1 - core) * half, half)
    state_own = state[:, pl.ds(own_at, half)]
    state_other = state[:, pl.ds(other_at, half)]
    lane = lax.broadcasted_iota(jnp.int32, (GROUP_ROWS, LANES), 1)
    row = lax.broadcasted_iota(jnp.int32, (GROUP_ROWS, LANES), 0)
    acc[...] = jnp.zeros_like(acc)

    def fold(values):
        total = values[:, :LANES]
        for start in range(LANES, half, LANES):
            total = total + values[:, start : start + LANES]
        return total

    def tile(index, carry):
        @pl.when(meta[index] == block)
        def _():
            live = meta[tile_num + index]
            readings = y_ref[pl.ds(index, 1), :]
            sum_own = jnp.zeros((GROUP_ROWS, half), jnp.float32)
            sum_other = jnp.zeros((GROUP_ROWS, half), jnp.float32)
            squares = jnp.zeros((GROUP_ROWS, LANES), jnp.float32)
            for start in range(0, row_num, GROUP_ROWS):
                own = own_ref[index, start : start + GROUP_ROWS, :].astype(jnp.float32)
                other = other_ref[index, start : start + GROUP_ROWS, :].astype(jnp.float32)
                valid = row + start < live
                product = fold(own * state_own) + fold(other * state_other)
                product = product - jnp.where(lane == row + start, readings, 0.0)
                weight = jnp.sum(product, axis=1, keepdims=True)
                weight = jnp.where(valid[:, :1], weight, 0.0)
                sum_own = sum_own + own * weight
                sum_other = sum_other + other * weight
                squares = squares + jnp.where(valid, fold(own * own) + fold(other * other), 0.0)
            acc[:, :half] += sum_own
            acc[:, half : 2 * half] += sum_other
            acc[:, 2 * half :] += squares

        return carry

    lax.fori_loop(0, tile_num, tile, 0)
    totals = jnp.sum(acc[...], axis=0, keepdims=True)
    part_ref[:, pl.ds(own_at, half)] = totals[:, :half]
    part_ref[:, pl.ds(other_at, half)] = totals[:, half : 2 * half]
    part_ref[:, 2 * half :] = totals[:, 2 * half :]


def first_kernel(block, meta, y_ref, own_ref, other_ref, state_ref, part_ref, acc):
    row_pass(block, state_ref, meta, y_ref, own_ref, other_ref, acc, part_ref)


def step_kernel(
    total_ref, meta, y_ref, own_ref, other_ref, state_ref, kappa_ref, rate_ref,
    next_ref, innovation_ref, part_ref, acc,
):
    width = state_ref.shape[1]
    trace_val = jnp.sum(total_ref[:, width:], axis=1, keepdims=True)
    lam_val = width / (2.0 * (width + trace_val))
    coeff, decay = kappa_ref[...], rate_ref[...]
    innovation = -lam_val * stencil(total_ref[:, :width], coeff, decay)
    next_ref[...] = stencil(state_ref[...], coeff, decay) + innovation
    innovation_ref[...] = innovation
    block = meta[2 * y_ref.shape[0] + 1]
    row_pass(block, next_ref, meta, y_ref, own_ref, other_ref, acc, part_ref)


def pieces_of(values):
    high = values.astype(jnp.bfloat16).astype(jnp.float32)
    middle = (values - high).astype(jnp.bfloat16).astype(jnp.float32)
    return high, middle, values - high - middle


def flip_of(turn, number, core):
    return FLIPS[number][:: 1 - 2 * core][turn]


def flip_here(turn, number, beside=0):
    if turn == number - 1:
        return 0
    on_core = [flip_of(turn, number, core) for core in range(2)]
    return jnp.where(lax.axis_index("state") == beside, on_core[0], on_core[1])


def half_kernel(blocks, y_ref, own_ref, kappa_ref, rate_ref, gain_ref, *refs):
    outs, (turned_ref, acc, vec, side, readings) = refs[:-5], refs[-5:]
    tile_num, row_num, _ = own_ref.shape
    number = len(outs)
    core, position = lax.axis_index("state"), lax.axis_index("tm")
    acc[...] = jnp.zeros_like(acc)
    vec[...] = jnp.zeros_like(vec)
    side[...] = jnp.zeros_like(side)
    readings[...] = y_ref[...].astype(jnp.float32)
    for index in range(tile_num):
        block = blocks[index]
        rows = own_ref[index]
        turned = rows.T
        turned_ref[index] = turned
        square = jnp.dot(turned, rows, preferred_element_type=jnp.float32)
        acc[block, 0:LANES] += square[:LANES, :LANES]
        acc[block, LANES : 2 * LANES] += square[:LANES, LANES:]
        acc[block, 2 * LANES : 3 * LANES] += square[LANES:, LANES:]
        values = jnp.broadcast_to(readings[index : index + 1, :], (8, row_num))
        vec[block] += jnp.dot(
            values.astype(jnp.bfloat16), rows, preferred_element_type=jnp.float32
        )
    line = lax.broadcasted_iota(jnp.int32, (LANES, LANES), 0)
    column = lax.broadcasted_iota(jnp.int32, (LANES, LANES), 1)
    for turn, out_ref in enumerate(outs):
        block = position ^ flip_here(turn, number)
        first, between, second = (acc[block, at * LANES : (at + 1) * LANES] for at in range(3))
        packed = jnp.where(line < column, first, jnp.where(line > column, second, 0.0))
        out_ref[0:LANES] = packed.astype(jnp.bfloat16)
        out_ref[LANES : 2 * LANES] = between.astype(jnp.bfloat16)
        values = [vec[block, 0:1, :LANES], vec[block, 0:1, LANES:]]
        for square in (first, second):
            values.append(jnp.sum(jnp.where(line == column, square, 0.0), axis=0, keepdims=True))
        for coefficient in (kappa_ref, rate_ref, gain_ref):
            for piece in range(2):
                at = pl.multiple_of((2 * core + piece) * LANES, LANES)
                values.append(coefficient[:, pl.ds(at, LANES)])
        for at, value in enumerate(values):
            for which, part in enumerate(pieces_of(value)):
                side[which * VECTORS + at : which * VECTORS + at + 1, :] = part
        out_ref[2 * LANES :] = side[...].astype(jnp.bfloat16)


def cross_kernel(blocks, turned_ref, other_ref, *refs):
    outs, acc = refs[:-1], refs[-1]
    number = len(outs)
    core, position = lax.axis_index("state"), lax.axis_index("tm")
    acc[...] = jnp.zeros_like(acc)
    for index in range(other_ref.shape[0]):
        block = blocks[index]
        for piece in range(2):
            at = pl.multiple_of((piece ^ core) * LANES, LANES)
            acc[block, piece * LANES : (piece + 1) * LANES] += jnp.dot(
                turned_ref[index, piece * LANES : (piece + 1) * LANES, :],
                other_ref[index, :, pl.ds(at, LANES)],
                preferred_element_type=jnp.float32,
            )
    for turn, out_ref in enumerate(outs):
        out_ref[...] = acc[position ^ flip_here(turn, number)].astype(jnp.bfloat16)


def sum_kernel(*refs):
    parts, (out_ref, coefficients, side) = refs[:-3], refs[-3:]
    number = len(parts) // 2
    position = lax.axis_index("tm")
    for at, some in enumerate((parts[:number], parts[number:])):
        total = some[0][: 2 * LANES].astype(jnp.float32)
        for part in some[1:]:
            total = total + part[: 2 * LANES].astype(jnp.float32)
        out_ref[2 * at * LANES : 2 * (at + 1) * LANES] = total.astype(jnp.bfloat16)
    values = None
    for turn, part in enumerate(parts[:number]):
        below = part[2 * LANES :].astype(jnp.float32)
        below = below[:VECTORS] + below[VECTORS : 2 * VECTORS] + below[2 * VECTORS : 3 * VECTORS]
        coefficients[position ^ flip_here(turn, number), 0 : VECTORS - 4] = below[4:]
        values = below[:4] if values is None else values + below[:4]
    side[...] = jnp.zeros_like(side)
    for which, part in enumerate(pieces_of(values)):
        side[which * 4 : which * 4 + 4, :] = part
    out_ref[4 * LANES :] = side[...].astype(jnp.bfloat16)


def band_kernel(here_ref, there_ref, band_ref, whole):
    core = lax.axis_index("state")
    block_num = here_ref.shape[0]
    for source, side in ((here_ref, core), (there_ref, 1 - core)):
        for block in range(block_num):
            for at in range(VECTORS - 4):
                lanes = pl.ds(pl.multiple_of((2 * side + at % 2) * LANES, LANES), LANES)
                whole[at // 2, block : block + 1, lanes] = source[block, at : at + 1]
    band = band_of(whole[0], whole[1]) + [whole[2]]
    for at, values in enumerate(band):
        for block in range(block_num):
            band_ref[block, at : at + 1, :] = values[block : block + 1]


def chain(grams, vectors, bands, state, states_ref, innovations_ref):
    width = state.shape[1]
    line = lax.broadcasted_iota(jnp.int32, (16, width), 0)
    for block in range(grams.shape[0]):
        info, diagonal = vectors[block, 0:1, :], vectors[block, 1:2, :]
        band = bands[block, : 2 * STEPS + 1, :]
        high, middle, low = pieces_of(state)
        split = jnp.where(line == 0, high, jnp.where(line == 1, middle, jnp.where(line == 2, low, 0.0)))
        product = jnp.dot(
            split.astype(jnp.bfloat16), grams[block], preferred_element_type=jnp.float32
        )
        product = jnp.sum(product, axis=0, keepdims=True) + diagonal * state
        trace_val = jnp.sum(diagonal, axis=1, keepdims=True)
        lam_val = width / (2.0 * (width + trace_val))
        innovation = -lam_val * apply_band(product - info, band)
        state = apply_band(state, band) + innovation
        states_ref[block : block + 1, :] = state
        innovations_ref[block : block + 1, :] = innovation


def put_grams(number, turns, own, other, grams, vectors):
    core, position = lax.axis_index("state"), lax.axis_index("tm")
    half = 2 * LANES
    line = lax.broadcasted_iota(jnp.int32, (LANES, LANES), 0)
    column = lax.broadcasted_iota(jnp.int32, (LANES, LANES), 1)
    for at, turn in enumerate(turns):
        flip, flip_other = flip_here(turn, number), flip_here(turn, number, 1)
        for pieces, side, block in (
            (own[at], core, position ^ flip),
            (other[at], 1 - core, position ^ flip_other),
        ):

            def piece(index):
                return pieces[index * LANES : (index + 1) * LANES, :]

            def put(row, column, values):
                row, column = pl.multiple_of(row, LANES), pl.multiple_of(column, LANES)
                grams[block, pl.ds(row, LANES), pl.ds(column, LANES)] = values.astype(jnp.bfloat16)

            here, there = side * half, (1 - side) * half
            packed = piece(0).astype(jnp.float32)
            turned = packed.T
            put(here, here, jnp.where(line < column, packed, turned))
            put(here + LANES, here + LANES, jnp.where(line > column, packed, turned))
            put(here, here + LANES, piece(1))
            put(here + LANES, here, piece(1).T)
            for index in range(2):
                beyond = there + (index ^ side) * LANES
                put(here + index * LANES, beyond, piece(2 + index))
                put(beyond, here + index * LANES, piece(2 + index).T)
            below = pieces[4 * LANES :, :].astype(jnp.float32)
            below = below[:4] + below[4:8] + below[8:12]
            for vector in range(4):
                lanes = pl.ds(pl.multiple_of(here + (vector % 2) * LANES, LANES), LANES)
                vectors[block, vector // 2 : vector // 2 + 1, lanes] = below[vector : vector + 1]


def early_kernel(number, turns, *refs):
    count = len(turns)
    put_grams(number, turns, refs[:count], refs[count : 2 * count], refs[-2], refs[-1])


def assemble_kernel(number, turns, *refs):
    count = len(turns)
    own, other, rest = refs[:count], refs[count : 2 * count], refs[2 * count :]
    _, _, bands, state_ref, grams, vectors, states_ref, innovations_ref = rest
    put_grams(number, turns, own, other, grams, vectors)
    chain_kernel(0, grams, vectors, bands, state_ref, states_ref, innovations_ref)


def chain_kernel(group, grams, vectors, bands, state_ref, states_ref, innovations_ref):
    @pl.when(lax.axis_index("grp") == group)
    def _():
        chain(grams, vectors, bands, state_ref[...], states_ref, innovations_ref)


def shards(rows_h, rows_y, tile_block, tile_count, kappa, rate, smooth_gain, start_state):
    tm_size, grp_size = lax.axis_size("tm"), lax.axis_size("grp")
    state_size = lax.axis_size("state")
    tm_index, grp_index, core = (lax.axis_index(name) for name in ("tm", "grp", "state"))
    tile_num, row_num, half = rows_h.shape[1:]
    width = kappa.shape[2]
    own = rows_h[0]
    other = lax.ppermute(own, "state", [(i, (i + 1) % state_size) for i in range(state_size)])
    state = start_state.reshape(1, width)
    direct = tm_size in FLIPS
    states_shape = jax.ShapeDtypeStruct((tm_size, width), jnp.float32)

    def flip_over(array, turn):
        pairs = [
            (i * state_size + j, (i ^ flip_of(turn, tm_size, j)) * state_size + j)
            for i in range(tm_size)
            for j in range(state_size)
        ]
        return lax.ppermute(array, ("tm", "state"), pairs)

    def ring(array, step):
        pairs = [
            (i * state_size + j, (i + step) % grp_size * state_size + state_size - 1 - j)
            for i in range(grp_size)
            for j in range(state_size)
        ]
        return lax.ppermute(array, ("grp", "state"), pairs)

    def across(array):
        return lax.ppermute(array, "state", [(i, (i + 1) % state_size) for i in range(state_size)])

    if direct:
        row = lax.broadcasted_iota(jnp.int32, own.shape, 1)
        valid = jnp.where(row < tile_count[0][:, None, None], own, jnp.zeros((), own.dtype))
        second_half = jax.ShapeDtypeStruct((2 * LANES, LANES), jnp.bfloat16)
        blocks = tile_block[0, :, 0]
        *pieces, turned = pl.pallas_call(
            half_kernel,
            out_shape=[jax.ShapeDtypeStruct((2 * LANES + 32, LANES), jnp.bfloat16)] * tm_size
            + [jax.ShapeDtypeStruct((tile_num, half, row_num), jnp.bfloat16)],
            in_specs=[SMEM] + [VMEM] * 5,
            out_specs=[VMEM] * (tm_size + 1),
            scratch_shapes=[
                pltpu.VMEM((tm_size, 3 * LANES, LANES), jnp.float32),
                pltpu.VMEM((tm_size, 8, half), jnp.float32),
                pltpu.VMEM((32, LANES), jnp.float32),
                pltpu.VMEM((tile_num, row_num), jnp.float32),
            ],
            compiler_params=KERNEL,
        )(blocks, rows_y[0], valid, kappa[0], rate[0], smooth_gain[0])
        turns = range(tm_size - 1)
        parts = [flip_over(pieces[turn], turn) for turn in turns] + [pieces[-1]]
        pieces2 = pl.pallas_call(
            cross_kernel,
            out_shape=[second_half] * tm_size,
            in_specs=[SMEM] + [VMEM] * 2,
            out_specs=[VMEM] * tm_size,
            scratch_shapes=[pltpu.VMEM((tm_size, 2 * LANES, LANES), jnp.float32)],
            compiler_params=KERNEL,
        )(blocks, turned, other)
        parts2 = [flip_over(pieces2[turn], turn) for turn in turns] + [pieces2[-1]]
        half_coefficients = jax.ShapeDtypeStruct((tm_size, 8, LANES), jnp.float32)
        own_sum, here = pl.pallas_call(
            sum_kernel,
            out_shape=(jax.ShapeDtypeStruct((4 * LANES + 16, LANES), jnp.bfloat16), half_coefficients),
            in_specs=[VMEM] * (2 * tm_size),
            out_specs=(VMEM, VMEM),
            scratch_shapes=[pltpu.VMEM((16, LANES), jnp.float32)],
            compiler_params=KERNEL,
        )(*parts, *parts2)
        own_sums = [flip_over(own_sum, turn) for turn in turns] + [own_sum]
        bands = pl.pallas_call(
            band_kernel,
            out_shape=jax.ShapeDtypeStruct((tm_size, 16, width), jnp.float32),
            in_specs=[VMEM, VMEM],
            out_specs=VMEM,
            scratch_shapes=[pltpu.VMEM((3, tm_size, width), jnp.float32)],
            compiler_params=KERNEL,
        )(here, across(here))
        bands, own_sums[0] = lax.optimization_barrier((bands, own_sums[0]))
        other_sums = [across(values) for values in own_sums]
        whole = (
            jax.ShapeDtypeStruct((tm_size, width, width), jnp.bfloat16),
            jax.ShapeDtypeStruct((tm_size, 8, width), jnp.float32),
        )
        late = [tm_size - 2]
        early = [turn for turn in range(tm_size) if turn not in late]
        arrays = [own_sums[turn] for turn in early] + [other_sums[turn] for turn in early]
        grams, vectors = pl.pallas_call(
            functools.partial(early_kernel, tm_size, early),
            out_shape=whole,
            in_specs=[VMEM] * len(arrays),
            out_specs=[VMEM] * 2,
            compiler_params=KERNEL,
        )(*arrays)
        arrays = [own_sums[turn] for turn in late] + [other_sums[turn] for turn in late]
        grams, vectors, new_states, new_innovations = pl.pallas_call(
            functools.partial(assemble_kernel, tm_size, late),
            out_shape=whole + (states_shape, states_shape),
            in_specs=[VMEM] * (len(arrays) + 4),
            out_specs=[VMEM] * 4,
            input_output_aliases={len(arrays): 0, len(arrays) + 1: 1},
            compiler_params=KERNEL,
        )(*arrays, grams, vectors, bands, state)
        gains = bands[:, 2 * STEPS + 1]

        def run_group(state, group):
            if group == 0:
                return new_states, new_innovations
            return pl.pallas_call(
                functools.partial(chain_kernel, group),
                out_shape=(states_shape, states_shape),
                in_specs=[VMEM] * 4,
                out_specs=(VMEM, VMEM),
                compiler_params=KERNEL,
            )(grams, vectors, bands, state)
    else:
        readings = rows_y[0].astype(jnp.float32)
        meta = jnp.concatenate(
            [tile_block[0, :, 0], tile_count[0], jnp.stack([core, tm_index]).astype(jnp.int32)]
        )
        params = jnp.concatenate([kappa[0], rate[0], smooth_gain[0]], axis=0)
        gathered = lax.all_gather(params, "tm")
        gains = gathered[:, 2]
        vector = jax.ShapeDtypeStruct((1, width), jnp.float32)
        partial = jax.ShapeDtypeStruct((1, width + LANES), jnp.float32)
        acc = pltpu.VMEM((GROUP_ROWS, width + LANES), jnp.float32)

        def run_group(state, group):
            part = pl.pallas_call(
                functools.partial(first_kernel, 0),
                out_shape=partial,
                in_specs=[SMEM] + [VMEM] * 4,
                out_specs=VMEM,
                scratch_shapes=[acc],
                compiler_params=KERNEL,
            )(meta, readings, own, other, state)

            def lap(block, carry):
                state, part, states, innovations = carry
                here = lax.dynamic_index_in_dim(gathered, block, 0, False)
                own_meta = meta.at[2 * tile_num + 1].set((block + 1).astype(jnp.int32))
                state, innovation, part = pl.pallas_call(
                    step_kernel,
                    out_shape=(vector, vector, partial),
                    in_specs=[VMEM, SMEM] + [VMEM] * 6,
                    out_specs=(VMEM, VMEM, VMEM),
                    scratch_shapes=[acc],
                    compiler_params=KERNEL,
                )(lax.psum(part, "tm"), own_meta, readings, own, other, state, here[0:1], here[1:2])
                states = lax.dynamic_update_slice_in_dim(states, state, block, 0)
                innovations = lax.dynamic_update_slice_in_dim(innovations, innovation, block, 0)
                return state, part, states, innovations

            empty = jnp.zeros((tm_size, width), jnp.float32)
            return lax.fori_loop(0, tm_size, lap, (state, part, empty, empty))[2:]

    states = innovations = jnp.zeros((tm_size, width), jnp.float32)
    for group in range(grp_size):
        new_states, new_innovations = run_group(state, group)
        mine = grp_index == group
        states = jnp.where(mine, new_states, states)
        innovations = jnp.where(mine, new_innovations, innovations)
        if group < grp_size - 1:
            state = ring(new_states[-1:], 1)

    residual = jnp.zeros((1, width), jnp.float32)
    residuals = [None] * tm_size
    for group in reversed(range(grp_size)):
        running = residual
        for block in reversed(range(tm_size)):
            residuals[block] = running
            running = gains[block][None] * (running + innovations[block][None])
        if group > 0:
            arrived = ring(running, -1)
            residual = jnp.where(grp_index == group - 1, arrived, residual)
    smoothed = states + jnp.concatenate(residuals, 0)

    def out(values):
        piece = lax.dynamic_slice(values, (tm_index, core * half), (1, half))
        return piece.reshape(1, 1, half)

    return out(states), out(smoothed)


def solution(mesh):
    return jax.shard_map(
        shards,
        mesh=mesh,
        in_specs=(
            P(("runs", "grp"), "tm", None, "state"),
            P(("runs", "grp"), "tm", None),
            P(("runs", "grp"), "tm", None),
            P(("runs", "grp"), "tm"),
            P(("runs", "grp"), "tm", None),
            P(("runs", "grp"), "tm", None),
            P(("runs", "grp"), "tm", None),
            P("runs"),
        ),
        out_specs=(P(("runs", "grp"), "tm", "state"), P(("runs", "grp"), "tm", "state")),
        check_vma=False,
    )
```

```python
import functools

import jax
import jax.numpy as jnp
from jax import lax
from jax.experimental import pallas as pl
from jax.experimental.pallas import tpu as pltpu
from jax.sharding import PartitionSpec as P

STEPS = 4
LANES = 128
GROUP_ROWS = 16
VECTORS = 10
FLIPS = {1: (), 2: (1,), 4: (2, 1, 3)}

VMEM = pl.BlockSpec(memory_space=pltpu.VMEM)
KERNEL = pltpu.CompilerParams(vmem_limit_bytes=16 * 2**20)
SMEM = pl.BlockSpec(memory_space=pltpu.SMEM)


def stencil(field, coeff, decay):
    width = field.shape[1]
    cell = lax.broadcasted_iota(jnp.int32, field.shape, 1)
    for _ in range(STEPS):
        upper_cell = jnp.where(cell == 0, 0.0, pltpu.roll(field, 1, 1))
        lower_cell = jnp.where(cell == width - 1, 0.0, pltpu.roll(field, width - 1, 1))
        field = field + coeff * (upper_cell + lower_cell - 2.0 * field) - decay * field
    return field


def band_of(coeff, decay):
    width = coeff.shape[1]
    cell = lax.broadcasted_iota(jnp.int32, coeff.shape, 1)
    from_upper = jnp.where(cell == 0, 0.0, coeff)
    from_lower = jnp.where(cell == width - 1, 0.0, coeff)
    stay = 1.0 - 2.0 * coeff - decay
    band = {-1: from_upper, 0: stay, 1: from_lower}
    for _ in range(STEPS - 1):
        longer = {}
        for offset, values in band.items():
            for step, weight, turned in (
                (-1, from_upper, lambda: pltpu.roll(values, 1, 1)),
                (0, stay, lambda: values),
                (1, from_lower, lambda: pltpu.roll(values, width - 1, 1)),
            ):
                term = weight * turned()
                longer[offset + step] = longer[offset + step] + term if offset + step in longer else term
        band = longer
    return [band[offset] for offset in range(-STEPS, STEPS + 1)]


def apply_band(field, band):
    width = field.shape[1]
    total = band[STEPS : STEPS + 1] * field
    for offset in range(1, STEPS + 1):
        total = total + (
            band[STEPS - offset : STEPS - offset + 1] * pltpu.roll(field, offset, 1)
            + band[STEPS + offset : STEPS + offset + 1] * pltpu.roll(field, width - offset, 1)
        )
    return total


def row_pass(block, state, meta, y_ref, own_ref, other_ref, acc, part_ref):
    tile_num, row_num, half = own_ref.shape
    core = meta[2 * tile_num]
    own_at = pl.multiple_of(core * half, half)
    other_at = pl.multiple_of((1 - core) * half, half)
    state_own = state[:, pl.ds(own_at, half)]
    state_other = state[:, pl.ds(other_at, half)]
    lane = lax.broadcasted_iota(jnp.int32, (GROUP_ROWS, LANES), 1)
    row = lax.broadcasted_iota(jnp.int32, (GROUP_ROWS, LANES), 0)
    acc[...] = jnp.zeros_like(acc)

    def fold(values):
        total = values[:, :LANES]
        for start in range(LANES, half, LANES):
            total = total + values[:, start : start + LANES]
        return total

    def tile(index, carry):
        @pl.when(meta[index] == block)
        def _():
            live = meta[tile_num + index]
            readings = y_ref[pl.ds(index, 1), :]
            sum_own = jnp.zeros((GROUP_ROWS, half), jnp.float32)
            sum_other = jnp.zeros((GROUP_ROWS, half), jnp.float32)
            squares = jnp.zeros((GROUP_ROWS, LANES), jnp.float32)
            for start in range(0, row_num, GROUP_ROWS):
                own = own_ref[index, start : start + GROUP_ROWS, :].astype(jnp.float32)
                other = other_ref[index, start : start + GROUP_ROWS, :].astype(jnp.float32)
                valid = row + start < live
                product = fold(own * state_own) + fold(other * state_other)
                product = product - jnp.where(lane == row + start, readings, 0.0)
                weight = jnp.sum(product, axis=1, keepdims=True)
                weight = jnp.where(valid[:, :1], weight, 0.0)
                sum_own = sum_own + own * weight
                sum_other = sum_other + other * weight
                squares = squares + jnp.where(valid, fold(own * own) + fold(other * other), 0.0)
            acc[:, :half] += sum_own
            acc[:, half : 2 * half] += sum_other
            acc[:, 2 * half :] += squares

        return carry

    lax.fori_loop(0, tile_num, tile, 0)
    totals = jnp.sum(acc[...], axis=0, keepdims=True)
    part_ref[:, pl.ds(own_at, half)] = totals[:, :half]
    part_ref[:, pl.ds(other_at, half)] = totals[:, half : 2 * half]
    part_ref[:, 2 * half :] = totals[:, 2 * half :]


def first_kernel(block, meta, y_ref, own_ref, other_ref, state_ref, part_ref, acc):
    row_pass(block, state_ref, meta, y_ref, own_ref, other_ref, acc, part_ref)


def step_kernel(
    total_ref, meta, y_ref, own_ref, other_ref, state_ref, kappa_ref, rate_ref,
    next_ref, innovation_ref, part_ref, acc,
):
    width = state_ref.shape[1]
    trace_val = jnp.sum(total_ref[:, width:], axis=1, keepdims=True)
    lam_val = width / (2.0 * (width + trace_val))
    coeff, decay = kappa_ref[...], rate_ref[...]
    innovation = -lam_val * stencil(total_ref[:, :width], coeff, decay)
    next_ref[...] = stencil(state_ref[...], coeff, decay) + innovation
    innovation_ref[...] = innovation
    block = meta[2 * y_ref.shape[0] + 1]
    row_pass(block, next_ref, meta, y_ref, own_ref, other_ref, acc, part_ref)


def pieces_of(values):
    high = values.astype(jnp.bfloat16).astype(jnp.float32)
    middle = (values - high).astype(jnp.bfloat16).astype(jnp.float32)
    return high, middle, values - high - middle


def flip_of(turn, number, core):
    return FLIPS[number][:: 1 - 2 * core][turn]


def flip_here(turn, number, beside=0):
    if turn == number - 1:
        return 0
    on_core = [flip_of(turn, number, core) for core in range(2)]
    return jnp.where(lax.axis_index("state") == beside, on_core[0], on_core[1])


def half_kernel(blocks, y_ref, own_ref, kappa_ref, rate_ref, gain_ref, *refs):
    outs, (turned_ref, acc, vec, side, readings, values) = refs[:-6], refs[-6:]
    tile_num, row_num, _ = own_ref.shape
    number = len(outs)
    core, position = lax.axis_index("state"), lax.axis_index("tm")
    acc[...] = jnp.zeros_like(acc)
    vec[...] = jnp.zeros_like(vec)
    side[...] = jnp.zeros_like(side)
    readings[...] = y_ref[...].astype(jnp.float32)
    for at, coefficient in enumerate((kappa_ref, rate_ref, gain_ref)):
        for piece in range(2):
            lanes = pl.ds(pl.multiple_of((2 * core + piece) * LANES, LANES), LANES)
            values[4 + 2 * at + piece : 5 + 2 * at + piece, :] = coefficient[:, lanes]
    for index in range(tile_num):
        block = blocks[index]
        rows = own_ref[index]
        turned = rows.T
        turned_ref[index] = turned
        observed = jnp.broadcast_to(readings[index : index + 1, :], (16, row_num))
        both = jnp.concatenate([turned, observed.astype(jnp.bfloat16)], axis=0)
        square = jnp.dot(both, rows, preferred_element_type=jnp.float32)
        acc[block, 0:LANES] += square[:LANES, :LANES]
        acc[block, LANES : 2 * LANES] += square[:LANES, LANES:]
        acc[block, 2 * LANES : 3 * LANES] += square[LANES : 2 * LANES, LANES:]
        vec[block] += square[2 * LANES : 2 * LANES + 8, :]
    line = lax.broadcasted_iota(jnp.int32, (LANES, LANES), 0)
    column = lax.broadcasted_iota(jnp.int32, (LANES, LANES), 1)
    for turn, out_ref in enumerate(outs):
        block = position ^ flip_here(turn, number)
        first, between, second = (acc[block, at * LANES : (at + 1) * LANES] for at in range(3))
        packed = jnp.where(line < column, first, jnp.where(line > column, second, 0.0))
        out_ref[0:LANES] = packed.astype(jnp.bfloat16)
        out_ref[LANES : 2 * LANES] = between.astype(jnp.bfloat16)
        values[0:1, :] = vec[block, 0:1, :LANES]
        values[1:2, :] = vec[block, 0:1, LANES:]
        for at, square in ((2, first), (3, second)):
            values[at : at + 1, :] = jnp.sum(
                jnp.where(line == column, square, 0.0), axis=0, keepdims=True
            )
        for which, part in enumerate(pieces_of(values[...])):
            side[which * VECTORS : (which + 1) * VECTORS, :] = part
        out_ref[2 * LANES :] = side[...].astype(jnp.bfloat16)


def cross_kernel(blocks, turned_ref, other_ref, *refs):
    outs, acc = refs[:-1], refs[-1]
    number = len(outs)
    core, position = lax.axis_index("state"), lax.axis_index("tm")
    acc[...] = jnp.zeros_like(acc)
    for index in range(other_ref.shape[0]):
        block = blocks[index]
        for piece in range(2):
            at = pl.multiple_of((piece ^ core) * LANES, LANES)
            acc[block, piece * LANES : (piece + 1) * LANES] += jnp.dot(
                turned_ref[index, piece * LANES : (piece + 1) * LANES, :],
                other_ref[index, :, pl.ds(at, LANES)],
                preferred_element_type=jnp.float32,
            )
    for turn, out_ref in enumerate(outs):
        out_ref[...] = acc[position ^ flip_here(turn, number)].astype(jnp.bfloat16)


def sum_kernel(*refs):
    parts, (out_ref, coefficients, side) = refs[:-3], refs[-3:]
    number = len(parts) // 2
    position = lax.axis_index("tm")
    for at, some in enumerate((parts[:number], parts[number:])):
        total = some[0][: 2 * LANES].astype(jnp.float32)
        for part in some[1:]:
            total = total + part[: 2 * LANES].astype(jnp.float32)
        out_ref[2 * at * LANES : 2 * (at + 1) * LANES] = total.astype(jnp.bfloat16)
    values = None
    for turn, part in enumerate(parts[:number]):
        below = part[2 * LANES :].astype(jnp.float32)
        below = below[:VECTORS] + below[VECTORS : 2 * VECTORS] + below[2 * VECTORS : 3 * VECTORS]
        coefficients[position ^ flip_here(turn, number), 0 : VECTORS - 4] = below[4:]
        values = below[:4] if values is None else values + below[:4]
    side[...] = jnp.zeros_like(side)
    for which, part in enumerate(pieces_of(values)):
        side[which * 4 : which * 4 + 4, :] = part
    out_ref[4 * LANES :] = side[...].astype(jnp.bfloat16)


def band_kernel(here_ref, there_ref, band_ref, whole):
    core = lax.axis_index("state")
    block_num = here_ref.shape[0]
    for source, side in ((here_ref, core), (there_ref, 1 - core)):
        for block in range(block_num):
            for at in range(VECTORS - 4):
                lanes = pl.ds(pl.multiple_of((2 * side + at % 2) * LANES, LANES), LANES)
                whole[at // 2, block : block + 1, lanes] = source[block, at : at + 1]
    band = band_of(whole[0], whole[1]) + [whole[2]]
    for at, values in enumerate(band):
        for block in range(block_num):
            band_ref[block, at : at + 1, :] = values[block : block + 1]


def chain(grams, vectors, bands, state, states_ref, innovations_ref):
    width = state.shape[1]
    line = lax.broadcasted_iota(jnp.int32, (16, width), 0)
    for block in range(grams.shape[0]):
        info, diagonal = vectors[block, 0:1, :], vectors[block, 1:2, :]
        band = bands[block, : 2 * STEPS + 1, :]
        high, middle, low = pieces_of(state)
        split = jnp.where(line == 0, high, jnp.where(line == 1, middle, jnp.where(line == 2, low, 0.0)))
        product = jnp.dot(
            split.astype(jnp.bfloat16), grams[block], preferred_element_type=jnp.float32
        )
        product = jnp.sum(product, axis=0, keepdims=True) + diagonal * state
        trace_val = jnp.sum(diagonal, axis=1, keepdims=True)
        lam_val = width / (2.0 * (width + trace_val))
        innovation = -lam_val * apply_band(product - info, band)
        state = apply_band(state, band) + innovation
        states_ref[block : block + 1, :] = state
        innovations_ref[block : block + 1, :] = innovation


def put_grams(number, turns, own, other, grams, vectors):
    core, position = lax.axis_index("state"), lax.axis_index("tm")
    half = 2 * LANES
    line = lax.broadcasted_iota(jnp.int32, (LANES, LANES), 0)
    column = lax.broadcasted_iota(jnp.int32, (LANES, LANES), 1)
    for at, turn in enumerate(turns):
        flip, flip_other = flip_here(turn, number), flip_here(turn, number, 1)
        for pieces, side, block in (
            (own[at], core, position ^ flip),
            (other[at], 1 - core, position ^ flip_other),
        ):

            def piece(index):
                return pieces[index * LANES : (index + 1) * LANES, :]

            def put(row, column, values):
                row, column = pl.multiple_of(row, LANES), pl.multiple_of(column, LANES)
                grams[block, pl.ds(row, LANES), pl.ds(column, LANES)] = values.astype(jnp.bfloat16)

            here, there = side * half, (1 - side) * half
            packed = piece(0).astype(jnp.float32)
            turned = packed.T
            put(here, here, jnp.where(line < column, packed, turned))
            put(here + LANES, here + LANES, jnp.where(line > column, packed, turned))
            put(here, here + LANES, piece(1))
            put(here + LANES, here, piece(1).T)
            for index in range(2):
                beyond = there + (index ^ side) * LANES
                put(here + index * LANES, beyond, piece(2 + index))
                put(beyond, here + index * LANES, piece(2 + index).T)
            below = pieces[4 * LANES :, :].astype(jnp.float32)
            below = below[:4] + below[4:8] + below[8:12]
            for vector in range(4):
                lanes = pl.ds(pl.multiple_of(here + (vector % 2) * LANES, LANES), LANES)
                vectors[block, vector // 2 : vector // 2 + 1, lanes] = below[vector : vector + 1]


def early_kernel(number, turns, *refs):
    count = len(turns)
    put_grams(number, turns, refs[:count], refs[count : 2 * count], refs[-2], refs[-1])


def assemble_kernel(number, turns, *refs):
    count = len(turns)
    own, other, rest = refs[:count], refs[count : 2 * count], refs[2 * count :]
    _, _, bands, state_ref, grams, vectors, states_ref, innovations_ref = rest
    put_grams(number, turns, own, other, grams, vectors)
    chain_kernel(0, grams, vectors, bands, state_ref, states_ref, innovations_ref)


def chain_kernel(group, grams, vectors, bands, state_ref, states_ref, innovations_ref):
    @pl.when(lax.axis_index("grp") == group)
    def _():
        chain(grams, vectors, bands, state_ref[...], states_ref, innovations_ref)


def shards(rows_h, rows_y, tile_block, tile_count, kappa, rate, smooth_gain, start_state):
    tm_size, grp_size = lax.axis_size("tm"), lax.axis_size("grp")
    state_size = lax.axis_size("state")
    tm_index, grp_index, core = (lax.axis_index(name) for name in ("tm", "grp", "state"))
    tile_num, row_num, half = rows_h.shape[1:]
    width = kappa.shape[2]
    own = rows_h[0]
    other = lax.ppermute(own, "state", [(i, (i + 1) % state_size) for i in range(state_size)])
    state = start_state.reshape(1, width)
    direct = tm_size in FLIPS
    states_shape = jax.ShapeDtypeStruct((tm_size, width), jnp.float32)

    def flip_over(array, turn):
        pairs = [
            (i * state_size + j, (i ^ flip_of(turn, tm_size, j)) * state_size + j)
            for i in range(tm_size)
            for j in range(state_size)
        ]
        return lax.ppermute(array, ("tm", "state"), pairs)

    def ring(array, step):
        pairs = [
            (i * state_size + j, (i + step) % grp_size * state_size + state_size - 1 - j)
            for i in range(grp_size)
            for j in range(state_size)
        ]
        return lax.ppermute(array, ("grp", "state"), pairs)

    def across(array):
        return lax.ppermute(array, "state", [(i, (i + 1) % state_size) for i in range(state_size)])

    if direct:
        row = lax.broadcasted_iota(jnp.int32, own.shape, 1)
        valid = jnp.where(row < tile_count[0][:, None, None], own, jnp.zeros((), own.dtype))
        second_half = jax.ShapeDtypeStruct((2 * LANES, LANES), jnp.bfloat16)
        blocks = tile_block[0, :, 0]
        *pieces, turned = pl.pallas_call(
            half_kernel,
            out_shape=[jax.ShapeDtypeStruct((2 * LANES + 32, LANES), jnp.bfloat16)] * tm_size
            + [jax.ShapeDtypeStruct((tile_num, half, row_num), jnp.bfloat16)],
            in_specs=[SMEM] + [VMEM] * 5,
            out_specs=[VMEM] * (tm_size + 1),
            scratch_shapes=[
                pltpu.VMEM((tm_size, 3 * LANES, LANES), jnp.float32),
                pltpu.VMEM((tm_size, 8, half), jnp.float32),
                pltpu.VMEM((32, LANES), jnp.float32),
                pltpu.VMEM((tile_num, row_num), jnp.float32),
                pltpu.VMEM((VECTORS, LANES), jnp.float32),
            ],
            compiler_params=KERNEL,
        )(blocks, rows_y[0], valid, kappa[0], rate[0], smooth_gain[0])
        turns = range(tm_size - 1)
        parts = [flip_over(pieces[turn], turn) for turn in turns] + [pieces[-1]]
        pieces2 = pl.pallas_call(
            cross_kernel,
            out_shape=[second_half] * tm_size,
            in_specs=[SMEM] + [VMEM] * 2,
            out_specs=[VMEM] * tm_size,
            scratch_shapes=[pltpu.VMEM((tm_size, 2 * LANES, LANES), jnp.float32)],
            compiler_params=KERNEL,
        )(blocks, turned, other)
        parts2 = [flip_over(pieces2[turn], turn) for turn in turns] + [pieces2[-1]]
        half_coefficients = jax.ShapeDtypeStruct((tm_size, 8, LANES), jnp.float32)
        own_sum, here = pl.pallas_call(
            sum_kernel,
            out_shape=(jax.ShapeDtypeStruct((4 * LANES + 16, LANES), jnp.bfloat16), half_coefficients),
            in_specs=[VMEM] * (2 * tm_size),
            out_specs=(VMEM, VMEM),
            scratch_shapes=[pltpu.VMEM((16, LANES), jnp.float32)],
            compiler_params=KERNEL,
        )(*parts, *parts2)
        own_sums = [flip_over(own_sum, turn) for turn in turns] + [own_sum]
        bands = pl.pallas_call(
            band_kernel,
            out_shape=jax.ShapeDtypeStruct((tm_size, 16, width), jnp.float32),
            in_specs=[VMEM, VMEM],
            out_specs=VMEM,
            scratch_shapes=[pltpu.VMEM((3, tm_size, width), jnp.float32)],
            compiler_params=KERNEL,
        )(here, across(here))
        bands, own_sums[0] = lax.optimization_barrier((bands, own_sums[0]))
        other_sums = [across(values) for values in own_sums]
        whole = (
            jax.ShapeDtypeStruct((tm_size, width, width), jnp.bfloat16),
            jax.ShapeDtypeStruct((tm_size, 8, width), jnp.float32),
        )
        late = [tm_size - 2]
        early = [turn for turn in range(tm_size) if turn not in late]
        arrays = [own_sums[turn] for turn in early] + [other_sums[turn] for turn in early]
        grams, vectors = pl.pallas_call(
            functools.partial(early_kernel, tm_size, early),
            out_shape=whole,
            in_specs=[VMEM] * len(arrays),
            out_specs=[VMEM] * 2,
            compiler_params=KERNEL,
        )(*arrays)
        arrays = [own_sums[turn] for turn in late] + [other_sums[turn] for turn in late]
        grams, vectors, new_states, new_innovations = pl.pallas_call(
            functools.partial(assemble_kernel, tm_size, late),
            out_shape=whole + (states_shape, states_shape),
            in_specs=[VMEM] * (len(arrays) + 4),
            out_specs=[VMEM] * 4,
            input_output_aliases={len(arrays): 0, len(arrays) + 1: 1},
            compiler_params=KERNEL,
        )(*arrays, grams, vectors, bands, state)
        gains = bands[:, 2 * STEPS + 1]

        def run_group(state, group):
            if group == 0:
                return new_states, new_innovations
            return pl.pallas_call(
                functools.partial(chain_kernel, group),
                out_shape=(states_shape, states_shape),
                in_specs=[VMEM] * 4,
                out_specs=(VMEM, VMEM),
                compiler_params=KERNEL,
            )(grams, vectors, bands, state)
    else:
        readings = rows_y[0].astype(jnp.float32)
        meta = jnp.concatenate(
            [tile_block[0, :, 0], tile_count[0], jnp.stack([core, tm_index]).astype(jnp.int32)]
        )
        params = jnp.concatenate([kappa[0], rate[0], smooth_gain[0]], axis=0)
        gathered = lax.all_gather(params, "tm")
        gains = gathered[:, 2]
        vector = jax.ShapeDtypeStruct((1, width), jnp.float32)
        partial = jax.ShapeDtypeStruct((1, width + LANES), jnp.float32)
        acc = pltpu.VMEM((GROUP_ROWS, width + LANES), jnp.float32)

        def run_group(state, group):
            part = pl.pallas_call(
                functools.partial(first_kernel, 0),
                out_shape=partial,
                in_specs=[SMEM] + [VMEM] * 4,
                out_specs=VMEM,
                scratch_shapes=[acc],
                compiler_params=KERNEL,
            )(meta, readings, own, other, state)

            def lap(block, carry):
                state, part, states, innovations = carry
                here = lax.dynamic_index_in_dim(gathered, block, 0, False)
                own_meta = meta.at[2 * tile_num + 1].set((block + 1).astype(jnp.int32))
                state, innovation, part = pl.pallas_call(
                    step_kernel,
                    out_shape=(vector, vector, partial),
                    in_specs=[VMEM, SMEM] + [VMEM] * 6,
                    out_specs=(VMEM, VMEM, VMEM),
                    scratch_shapes=[acc],
                    compiler_params=KERNEL,
                )(lax.psum(part, "tm"), own_meta, readings, own, other, state, here[0:1], here[1:2])
                states = lax.dynamic_update_slice_in_dim(states, state, block, 0)
                innovations = lax.dynamic_update_slice_in_dim(innovations, innovation, block, 0)
                return state, part, states, innovations

            empty = jnp.zeros((tm_size, width), jnp.float32)
            return lax.fori_loop(0, tm_size, lap, (state, part, empty, empty))[2:]

    states = innovations = jnp.zeros((tm_size, width), jnp.float32)
    for group in range(grp_size):
        new_states, new_innovations = run_group(state, group)
        mine = grp_index == group
        states = jnp.where(mine, new_states, states)
        innovations = jnp.where(mine, new_innovations, innovations)
        if group < grp_size - 1:
            state = ring(new_states[-1:], 1)

    residual = jnp.zeros((1, width), jnp.float32)
    residuals = [None] * tm_size
    for group in reversed(range(grp_size)):
        running = residual
        for block in reversed(range(tm_size)):
            residuals[block] = running
            running = gains[block][None] * (running + innovations[block][None])
        if group > 0:
            arrived = ring(running, -1)
            residual = jnp.where(grp_index == group - 1, arrived, residual)
    smoothed = states + jnp.concatenate(residuals, 0)

    def out(values):
        piece = lax.dynamic_slice(values, (tm_index, core * half), (1, half))
        return piece.reshape(1, 1, half)

    return out(states), out(smoothed)


def solution(mesh):
    return jax.shard_map(
        shards,
        mesh=mesh,
        in_specs=(
            P(("runs", "grp"), "tm", None, "state"),
            P(("runs", "grp"), "tm", None),
            P(("runs", "grp"), "tm", None),
            P(("runs", "grp"), "tm"),
            P(("runs", "grp"), "tm", None),
            P(("runs", "grp"), "tm", None),
            P(("runs", "grp"), "tm", None),
            P("runs"),
        ),
        out_specs=(P(("runs", "grp"), "tm", "state"), P(("runs", "grp"), "tm", "state")),
        check_vma=False,
    )
```

```python
import functools

import jax
import jax.numpy as jnp
from jax import lax
from jax.experimental import pallas as pl
from jax.experimental.pallas import tpu as pltpu
from jax.sharding import PartitionSpec as P

STEPS = 4
LANES = 128
GROUP_ROWS = 16
VECTORS = 10
FLIPS = {1: (), 2: (1,), 4: (2, 1, 3)}

VMEM = pl.BlockSpec(memory_space=pltpu.VMEM)
KERNEL = pltpu.CompilerParams(vmem_limit_bytes=16 * 2**20)
SMEM = pl.BlockSpec(memory_space=pltpu.SMEM)


def stencil(field, coeff, decay):
    width = field.shape[1]
    cell = lax.broadcasted_iota(jnp.int32, field.shape, 1)
    for _ in range(STEPS):
        upper_cell = jnp.where(cell == 0, 0.0, pltpu.roll(field, 1, 1))
        lower_cell = jnp.where(cell == width - 1, 0.0, pltpu.roll(field, width - 1, 1))
        field = field + coeff * (upper_cell + lower_cell - 2.0 * field) - decay * field
    return field


def band_of(coeff, decay):
    width = coeff.shape[1]
    cell = lax.broadcasted_iota(jnp.int32, coeff.shape, 1)
    from_upper = jnp.where(cell == 0, 0.0, coeff)
    from_lower = jnp.where(cell == width - 1, 0.0, coeff)
    stay = 1.0 - 2.0 * coeff - decay
    band = {-1: from_upper, 0: stay, 1: from_lower}
    for _ in range(STEPS - 1):
        longer = {}
        for offset, values in band.items():
            for step, weight, turned in (
                (-1, from_upper, lambda: pltpu.roll(values, 1, 1)),
                (0, stay, lambda: values),
                (1, from_lower, lambda: pltpu.roll(values, width - 1, 1)),
            ):
                term = weight * turned()
                longer[offset + step] = longer[offset + step] + term if offset + step in longer else term
        band = longer
    return [band[offset] for offset in range(-STEPS, STEPS + 1)]


def apply_band(field, band):
    width = field.shape[1]
    total = band[STEPS : STEPS + 1] * field
    for offset in range(1, STEPS + 1):
        total = total + (
            band[STEPS - offset : STEPS - offset + 1] * pltpu.roll(field, offset, 1)
            + band[STEPS + offset : STEPS + offset + 1] * pltpu.roll(field, width - offset, 1)
        )
    return total


def row_pass(block, state, meta, y_ref, own_ref, other_ref, acc, part_ref):
    tile_num, row_num, half = own_ref.shape
    core = meta[2 * tile_num]
    own_at = pl.multiple_of(core * half, half)
    other_at = pl.multiple_of((1 - core) * half, half)
    state_own = state[:, pl.ds(own_at, half)]
    state_other = state[:, pl.ds(other_at, half)]
    lane = lax.broadcasted_iota(jnp.int32, (GROUP_ROWS, LANES), 1)
    row = lax.broadcasted_iota(jnp.int32, (GROUP_ROWS, LANES), 0)
    acc[...] = jnp.zeros_like(acc)

    def fold(values):
        total = values[:, :LANES]
        for start in range(LANES, half, LANES):
            total = total + values[:, start : start + LANES]
        return total

    def tile(index, carry):
        @pl.when(meta[index] == block)
        def _():
            live = meta[tile_num + index]
            readings = y_ref[pl.ds(index, 1), :]
            sum_own = jnp.zeros((GROUP_ROWS, half), jnp.float32)
            sum_other = jnp.zeros((GROUP_ROWS, half), jnp.float32)
            squares = jnp.zeros((GROUP_ROWS, LANES), jnp.float32)
            for start in range(0, row_num, GROUP_ROWS):
                own = own_ref[index, start : start + GROUP_ROWS, :].astype(jnp.float32)
                other = other_ref[index, start : start + GROUP_ROWS, :].astype(jnp.float32)
                valid = row + start < live
                product = fold(own * state_own) + fold(other * state_other)
                product = product - jnp.where(lane == row + start, readings, 0.0)
                weight = jnp.sum(product, axis=1, keepdims=True)
                weight = jnp.where(valid[:, :1], weight, 0.0)
                sum_own = sum_own + own * weight
                sum_other = sum_other + other * weight
                squares = squares + jnp.where(valid, fold(own * own) + fold(other * other), 0.0)
            acc[:, :half] += sum_own
            acc[:, half : 2 * half] += sum_other
            acc[:, 2 * half :] += squares

        return carry

    lax.fori_loop(0, tile_num, tile, 0)
    totals = jnp.sum(acc[...], axis=0, keepdims=True)
    part_ref[:, pl.ds(own_at, half)] = totals[:, :half]
    part_ref[:, pl.ds(other_at, half)] = totals[:, half : 2 * half]
    part_ref[:, 2 * half :] = totals[:, 2 * half :]


def first_kernel(block, meta, y_ref, own_ref, other_ref, state_ref, part_ref, acc):
    row_pass(block, state_ref, meta, y_ref, own_ref, other_ref, acc, part_ref)


def step_kernel(
    total_ref, meta, y_ref, own_ref, other_ref, state_ref, kappa_ref, rate_ref,
    next_ref, innovation_ref, part_ref, acc,
):
    width = state_ref.shape[1]
    trace_val = jnp.sum(total_ref[:, width:], axis=1, keepdims=True)
    lam_val = width / (2.0 * (width + trace_val))
    coeff, decay = kappa_ref[...], rate_ref[...]
    innovation = -lam_val * stencil(total_ref[:, :width], coeff, decay)
    next_ref[...] = stencil(state_ref[...], coeff, decay) + innovation
    innovation_ref[...] = innovation
    block = meta[2 * y_ref.shape[0] + 1]
    row_pass(block, next_ref, meta, y_ref, own_ref, other_ref, acc, part_ref)


def pieces_of(values):
    high = values.astype(jnp.bfloat16).astype(jnp.float32)
    middle = (values - high).astype(jnp.bfloat16).astype(jnp.float32)
    return high, middle, values - high - middle


def flip_of(turn, number, core):
    return FLIPS[number][:: 1 - 2 * core][turn]


def flip_here(turn, number, beside=0):
    if turn == number - 1:
        return 0
    on_core = [flip_of(turn, number, core) for core in range(2)]
    return jnp.where(lax.axis_index("state") == beside, on_core[0], on_core[1])


def half_kernel(blocks, counts, y_ref, own_ref, kappa_ref, rate_ref, gain_ref, *refs):
    outs, (turned_ref, acc, vec, side, readings, values) = refs[:-6], refs[-6:]
    tile_num, row_num, _ = own_ref.shape
    number = len(outs)
    core, position = lax.axis_index("state"), lax.axis_index("tm")
    acc[...] = jnp.zeros_like(acc)
    vec[...] = jnp.zeros_like(vec)
    side[...] = jnp.zeros_like(side)
    readings[...] = y_ref[...].astype(jnp.float32)
    for at, coefficient in enumerate((kappa_ref, rate_ref, gain_ref)):
        for piece in range(2):
            lanes = pl.ds(pl.multiple_of((2 * core + piece) * LANES, LANES), LANES)
            values[4 + 2 * at + piece : 5 + 2 * at + piece, :] = coefficient[:, lanes]
    row = lax.broadcasted_iota(jnp.int32, own_ref.shape[1:], 0)
    for index in range(tile_num):
        block = blocks[index]
        rows = jnp.where(row < counts[index], own_ref[index].astype(jnp.float32), 0.0)
        rows = rows.astype(jnp.bfloat16)
        turned = rows.T
        turned_ref[index] = turned
        observed = jnp.broadcast_to(readings[index : index + 1, :], (16, row_num))
        both = jnp.concatenate([turned, observed.astype(jnp.bfloat16)], axis=0)
        square = jnp.dot(both, rows, preferred_element_type=jnp.float32)
        acc[block, 0:LANES] += square[:LANES, :LANES]
        acc[block, LANES : 2 * LANES] += square[:LANES, LANES:]
        acc[block, 2 * LANES : 3 * LANES] += square[LANES : 2 * LANES, LANES:]
        vec[block] += square[2 * LANES : 2 * LANES + 8, :]
    line = lax.broadcasted_iota(jnp.int32, (LANES, LANES), 0)
    column = lax.broadcasted_iota(jnp.int32, (LANES, LANES), 1)
    for turn, out_ref in enumerate(outs):
        block = position ^ flip_here(turn, number)
        first, between, second = (acc[block, at * LANES : (at + 1) * LANES] for at in range(3))
        packed = jnp.where(line < column, first, jnp.where(line > column, second, 0.0))
        out_ref[0:LANES] = packed.astype(jnp.bfloat16)
        out_ref[LANES : 2 * LANES] = between.astype(jnp.bfloat16)
        values[0:1, :] = vec[block, 0:1, :LANES]
        values[1:2, :] = vec[block, 0:1, LANES:]
        for at, square in ((2, first), (3, second)):
            values[at : at + 1, :] = jnp.sum(
                jnp.where(line == column, square, 0.0), axis=0, keepdims=True
            )
        for which, part in enumerate(pieces_of(values[...])):
            side[which * VECTORS : (which + 1) * VECTORS, :] = part
        out_ref[2 * LANES :] = side[...].astype(jnp.bfloat16)


def cross_kernel(blocks, turned_ref, other_ref, *refs):
    outs, acc = refs[:-1], refs[-1]
    number = len(outs)
    core, position = lax.axis_index("state"), lax.axis_index("tm")
    acc[...] = jnp.zeros_like(acc)
    for index in range(other_ref.shape[0]):
        block = blocks[index]
        for piece in range(2):
            at = pl.multiple_of((piece ^ core) * LANES, LANES)
            acc[block, piece * LANES : (piece + 1) * LANES] += jnp.dot(
                turned_ref[index, piece * LANES : (piece + 1) * LANES, :],
                other_ref[index, :, pl.ds(at, LANES)],
                preferred_element_type=jnp.float32,
            )
    for turn, out_ref in enumerate(outs):
        out_ref[...] = acc[position ^ flip_here(turn, number)].astype(jnp.bfloat16)


def sum_kernel(*refs):
    parts, (out_ref, coefficients, side) = refs[:-3], refs[-3:]
    number = len(parts) // 2
    position = lax.axis_index("tm")
    for at, some in enumerate((parts[:number], parts[number:])):
        total = some[0][: 2 * LANES].astype(jnp.float32)
        for part in some[1:]:
            total = total + part[: 2 * LANES].astype(jnp.float32)
        out_ref[2 * at * LANES : 2 * (at + 1) * LANES] = total.astype(jnp.bfloat16)
    values = None
    for turn, part in enumerate(parts[:number]):
        below = part[2 * LANES :].astype(jnp.float32)
        below = below[:VECTORS] + below[VECTORS : 2 * VECTORS] + below[2 * VECTORS : 3 * VECTORS]
        coefficients[position ^ flip_here(turn, number), 0 : VECTORS - 4] = below[4:]
        values = below[:4] if values is None else values + below[:4]
    side[...] = jnp.zeros_like(side)
    for which, part in enumerate(pieces_of(values)):
        side[which * 4 : which * 4 + 4, :] = part
    out_ref[4 * LANES :] = side[...].astype(jnp.bfloat16)


def band_kernel(here_ref, there_ref, band_ref, whole):
    core = lax.axis_index("state")
    block_num = here_ref.shape[0]
    for source, side in ((here_ref, core), (there_ref, 1 - core)):
        for block in range(block_num):
            for at in range(VECTORS - 4):
                lanes = pl.ds(pl.multiple_of((2 * side + at % 2) * LANES, LANES), LANES)
                whole[at // 2, block : block + 1, lanes] = source[block, at : at + 1]
    band = band_of(whole[0], whole[1]) + [whole[2]]
    for at, values in enumerate(band):
        for block in range(block_num):
            band_ref[block, at : at + 1, :] = values[block : block + 1]


def chain(grams, vectors, bands, state, states_ref, innovations_ref):
    width = state.shape[1]
    line = lax.broadcasted_iota(jnp.int32, (16, width), 0)
    for block in range(grams.shape[0]):
        info, diagonal = vectors[block, 0:1, :], vectors[block, 1:2, :]
        band = bands[block, : 2 * STEPS + 1, :]
        high, middle, low = pieces_of(state)
        split = jnp.where(line == 0, high, jnp.where(line == 1, middle, jnp.where(line == 2, low, 0.0)))
        product = jnp.dot(
            split.astype(jnp.bfloat16), grams[block], preferred_element_type=jnp.float32
        )
        product = jnp.sum(product, axis=0, keepdims=True) + diagonal * state
        trace_val = jnp.sum(diagonal, axis=1, keepdims=True)
        lam_val = width / (2.0 * (width + trace_val))
        innovation = -lam_val * apply_band(product - info, band)
        state = apply_band(state, band) + innovation
        states_ref[block : block + 1, :] = state
        innovations_ref[block : block + 1, :] = innovation


def put_grams(number, turns, own, other, grams, vectors):
    core, position = lax.axis_index("state"), lax.axis_index("tm")
    half = 2 * LANES
    line = lax.broadcasted_iota(jnp.int32, (LANES, LANES), 0)
    column = lax.broadcasted_iota(jnp.int32, (LANES, LANES), 1)
    for at, turn in enumerate(turns):
        flip, flip_other = flip_here(turn, number), flip_here(turn, number, 1)
        for pieces, side, block in (
            (own[at], core, position ^ flip),
            (other[at], 1 - core, position ^ flip_other),
        ):

            def piece(index):
                return pieces[index * LANES : (index + 1) * LANES, :]

            def put(row, column, values):
                row, column = pl.multiple_of(row, LANES), pl.multiple_of(column, LANES)
                grams[block, pl.ds(row, LANES), pl.ds(column, LANES)] = values.astype(jnp.bfloat16)

            here, there = side * half, (1 - side) * half
            packed = piece(0).astype(jnp.float32)
            turned = packed.T
            put(here, here, jnp.where(line < column, packed, turned))
            put(here + LANES, here + LANES, jnp.where(line > column, packed, turned))
            put(here, here + LANES, piece(1))
            put(here + LANES, here, piece(1).T)
            for index in range(2):
                beyond = there + (index ^ side) * LANES
                put(here + index * LANES, beyond, piece(2 + index))
                put(beyond, here + index * LANES, piece(2 + index).T)
            below = pieces[4 * LANES :, :].astype(jnp.float32)
            below = below[:4] + below[4:8] + below[8:12]
            for vector in range(4):
                lanes = pl.ds(pl.multiple_of(here + (vector % 2) * LANES, LANES), LANES)
                vectors[block, vector // 2 : vector // 2 + 1, lanes] = below[vector : vector + 1]


def early_kernel(number, turns, *refs):
    count = len(turns)
    put_grams(number, turns, refs[:count], refs[count : 2 * count], refs[-2], refs[-1])


def assemble_kernel(number, turns, *refs):
    count = len(turns)
    own, other, rest = refs[:count], refs[count : 2 * count], refs[2 * count :]
    _, _, bands, state_ref, grams, vectors, states_ref, innovations_ref = rest
    put_grams(number, turns, own, other, grams, vectors)
    chain_kernel(0, grams, vectors, bands, state_ref, states_ref, innovations_ref)


def chain_kernel(group, grams, vectors, bands, state_ref, states_ref, innovations_ref):
    @pl.when(lax.axis_index("grp") == group)
    def _():
        chain(grams, vectors, bands, state_ref[...], states_ref, innovations_ref)


def shards(rows_h, rows_y, tile_block, tile_count, kappa, rate, smooth_gain, start_state):
    tm_size, grp_size = lax.axis_size("tm"), lax.axis_size("grp")
    state_size = lax.axis_size("state")
    tm_index, grp_index, core = (lax.axis_index(name) for name in ("tm", "grp", "state"))
    tile_num, row_num, half = rows_h.shape[1:]
    width = kappa.shape[2]
    own = rows_h[0]
    other = lax.ppermute(own, "state", [(i, (i + 1) % state_size) for i in range(state_size)])
    state = start_state.reshape(1, width)
    direct = tm_size in FLIPS
    states_shape = jax.ShapeDtypeStruct((tm_size, width), jnp.float32)

    def flip_over(array, turn):
        pairs = [
            (i * state_size + j, (i ^ flip_of(turn, tm_size, j)) * state_size + j)
            for i in range(tm_size)
            for j in range(state_size)
        ]
        return lax.ppermute(array, ("tm", "state"), pairs)

    def ring(array, step):
        pairs = [
            (i * state_size + j, (i + step) % grp_size * state_size + state_size - 1 - j)
            for i in range(grp_size)
            for j in range(state_size)
        ]
        return lax.ppermute(array, ("grp", "state"), pairs)

    def across(array):
        return lax.ppermute(array, "state", [(i, (i + 1) % state_size) for i in range(state_size)])

    if direct:
        valid = jnp.where(own == own, own, jnp.zeros((), own.dtype))
        second_half = jax.ShapeDtypeStruct((2 * LANES, LANES), jnp.bfloat16)
        blocks = tile_block[0, :, 0]
        *pieces, turned = pl.pallas_call(
            half_kernel,
            out_shape=[jax.ShapeDtypeStruct((2 * LANES + 32, LANES), jnp.bfloat16)] * tm_size
            + [jax.ShapeDtypeStruct((tile_num, half, row_num), jnp.bfloat16)],
            in_specs=[SMEM] * 2 + [VMEM] * 5,
            out_specs=[VMEM] * (tm_size + 1),
            scratch_shapes=[
                pltpu.VMEM((tm_size, 3 * LANES, LANES), jnp.float32),
                pltpu.VMEM((tm_size, 8, half), jnp.float32),
                pltpu.VMEM((32, LANES), jnp.float32),
                pltpu.VMEM((tile_num, row_num), jnp.float32),
                pltpu.VMEM((VECTORS, LANES), jnp.float32),
            ],
            compiler_params=KERNEL,
        )(blocks, tile_count[0], rows_y[0], valid, kappa[0], rate[0], smooth_gain[0])
        turns = range(tm_size - 1)
        parts = [flip_over(pieces[turn], turn) for turn in turns] + [pieces[-1]]
        pieces2 = pl.pallas_call(
            cross_kernel,
            out_shape=[second_half] * tm_size,
            in_specs=[SMEM] + [VMEM] * 2,
            out_specs=[VMEM] * tm_size,
            scratch_shapes=[pltpu.VMEM((tm_size, 2 * LANES, LANES), jnp.float32)],
            compiler_params=KERNEL,
        )(blocks, turned, other)
        parts2 = [flip_over(pieces2[turn], turn) for turn in turns] + [pieces2[-1]]
        half_coefficients = jax.ShapeDtypeStruct((tm_size, 8, LANES), jnp.float32)
        own_sum, here = pl.pallas_call(
            sum_kernel,
            out_shape=(jax.ShapeDtypeStruct((4 * LANES + 16, LANES), jnp.bfloat16), half_coefficients),
            in_specs=[VMEM] * (2 * tm_size),
            out_specs=(VMEM, VMEM),
            scratch_shapes=[pltpu.VMEM((16, LANES), jnp.float32)],
            compiler_params=KERNEL,
        )(*parts, *parts2)
        own_sums = [flip_over(own_sum, turn) for turn in turns] + [own_sum]
        bands = pl.pallas_call(
            band_kernel,
            out_shape=jax.ShapeDtypeStruct((tm_size, 16, width), jnp.float32),
            in_specs=[VMEM, VMEM],
            out_specs=VMEM,
            scratch_shapes=[pltpu.VMEM((3, tm_size, width), jnp.float32)],
            compiler_params=KERNEL,
        )(here, across(here))
        bands, own_sums[0] = lax.optimization_barrier((bands, own_sums[0]))
        other_sums = [across(values) for values in own_sums]
        whole = (
            jax.ShapeDtypeStruct((tm_size, width, width), jnp.bfloat16),
            jax.ShapeDtypeStruct((tm_size, 8, width), jnp.float32),
        )
        late = [tm_size - 2]
        early = [turn for turn in range(tm_size) if turn not in late]
        arrays = [own_sums[turn] for turn in early] + [other_sums[turn] for turn in early]
        grams, vectors = pl.pallas_call(
            functools.partial(early_kernel, tm_size, early),
            out_shape=whole,
            in_specs=[VMEM] * len(arrays),
            out_specs=[VMEM] * 2,
            compiler_params=KERNEL,
        )(*arrays)
        arrays = [own_sums[turn] for turn in late] + [other_sums[turn] for turn in late]
        grams, vectors, new_states, new_innovations = pl.pallas_call(
            functools.partial(assemble_kernel, tm_size, late),
            out_shape=whole + (states_shape, states_shape),
            in_specs=[VMEM] * (len(arrays) + 4),
            out_specs=[VMEM] * 4,
            input_output_aliases={len(arrays): 0, len(arrays) + 1: 1},
            compiler_params=KERNEL,
        )(*arrays, grams, vectors, bands, state)
        gains = bands[:, 2 * STEPS + 1]

        def run_group(state, group):
            if group == 0:
                return new_states, new_innovations
            return pl.pallas_call(
                functools.partial(chain_kernel, group),
                out_shape=(states_shape, states_shape),
                in_specs=[VMEM] * 4,
                out_specs=(VMEM, VMEM),
                compiler_params=KERNEL,
            )(grams, vectors, bands, state)
    else:
        readings = rows_y[0].astype(jnp.float32)
        meta = jnp.concatenate(
            [tile_block[0, :, 0], tile_count[0], jnp.stack([core, tm_index]).astype(jnp.int32)]
        )
        params = jnp.concatenate([kappa[0], rate[0], smooth_gain[0]], axis=0)
        gathered = lax.all_gather(params, "tm")
        gains = gathered[:, 2]
        vector = jax.ShapeDtypeStruct((1, width), jnp.float32)
        partial = jax.ShapeDtypeStruct((1, width + LANES), jnp.float32)
        acc = pltpu.VMEM((GROUP_ROWS, width + LANES), jnp.float32)

        def run_group(state, group):
            part = pl.pallas_call(
                functools.partial(first_kernel, 0),
                out_shape=partial,
                in_specs=[SMEM] + [VMEM] * 4,
                out_specs=VMEM,
                scratch_shapes=[acc],
                compiler_params=KERNEL,
            )(meta, readings, own, other, state)

            def lap(block, carry):
                state, part, states, innovations = carry
                here = lax.dynamic_index_in_dim(gathered, block, 0, False)
                own_meta = meta.at[2 * tile_num + 1].set((block + 1).astype(jnp.int32))
                state, innovation, part = pl.pallas_call(
                    step_kernel,
                    out_shape=(vector, vector, partial),
                    in_specs=[VMEM, SMEM] + [VMEM] * 6,
                    out_specs=(VMEM, VMEM, VMEM),
                    scratch_shapes=[acc],
                    compiler_params=KERNEL,
                )(lax.psum(part, "tm"), own_meta, readings, own, other, state, here[0:1], here[1:2])
                states = lax.dynamic_update_slice_in_dim(states, state, block, 0)
                innovations = lax.dynamic_update_slice_in_dim(innovations, innovation, block, 0)
                return state, part, states, innovations

            empty = jnp.zeros((tm_size, width), jnp.float32)
            return lax.fori_loop(0, tm_size, lap, (state, part, empty, empty))[2:]

    states = innovations = jnp.zeros((tm_size, width), jnp.float32)
    for group in range(grp_size):
        new_states, new_innovations = run_group(state, group)
        mine = grp_index == group
        states = jnp.where(mine, new_states, states)
        innovations = jnp.where(mine, new_innovations, innovations)
        if group < grp_size - 1:
            state = ring(new_states[-1:], 1)

    residual = jnp.zeros((1, width), jnp.float32)
    residuals = [None] * tm_size
    for group in reversed(range(grp_size)):
        running = residual
        for block in reversed(range(tm_size)):
            residuals[block] = running
            running = gains[block][None] * (running + innovations[block][None])
        if group > 0:
            arrived = ring(running, -1)
            residual = jnp.where(grp_index == group - 1, arrived, residual)
    smoothed = states + jnp.concatenate(residuals, 0)

    def out(values):
        piece = lax.dynamic_slice(values, (tm_index, core * half), (1, half))
        return piece.reshape(1, 1, half)

    return out(states), out(smoothed)


def solution(mesh):
    return jax.shard_map(
        shards,
        mesh=mesh,
        in_specs=(
            P(("runs", "grp"), "tm", None, "state"),
            P(("runs", "grp"), "tm", None),
            P(("runs", "grp"), "tm", None),
            P(("runs", "grp"), "tm"),
            P(("runs", "grp"), "tm", None),
            P(("runs", "grp"), "tm", None),
            P(("runs", "grp"), "tm", None),
            P("runs"),
        ),
        out_specs=(P(("runs", "grp"), "tm", "state"), P(("runs", "grp"), "tm", "state")),
        check_vma=False,
    )
```

```python
import functools

import jax
import jax.numpy as jnp
from jax import lax
from jax.experimental import pallas as pl
from jax.experimental.pallas import tpu as pltpu
from jax.sharding import PartitionSpec as P

STEPS = 4
LANES = 128
GROUP_ROWS = 16
VECTORS = 10
FLIPS = {1: (), 2: (1,), 4: (2, 1, 3)}

VMEM = pl.BlockSpec(memory_space=pltpu.VMEM)
KERNEL = pltpu.CompilerParams(vmem_limit_bytes=16 * 2**20)
SMEM = pl.BlockSpec(memory_space=pltpu.SMEM)


def stencil(field, coeff, decay):
    width = field.shape[1]
    cell = lax.broadcasted_iota(jnp.int32, field.shape, 1)
    for _ in range(STEPS):
        upper_cell = jnp.where(cell == 0, 0.0, pltpu.roll(field, 1, 1))
        lower_cell = jnp.where(cell == width - 1, 0.0, pltpu.roll(field, width - 1, 1))
        field = field + coeff * (upper_cell + lower_cell - 2.0 * field) - decay * field
    return field


def band_of(coeff, decay):
    width = coeff.shape[1]
    cell = lax.broadcasted_iota(jnp.int32, coeff.shape, 1)
    from_upper = jnp.where(cell == 0, 0.0, coeff)
    from_lower = jnp.where(cell == width - 1, 0.0, coeff)
    stay = 1.0 - 2.0 * coeff - decay
    band = {-1: from_upper, 0: stay, 1: from_lower}
    for _ in range(STEPS - 1):
        longer = {}
        for offset, values in band.items():
            for step, weight, turned in (
                (-1, from_upper, lambda: pltpu.roll(values, 1, 1)),
                (0, stay, lambda: values),
                (1, from_lower, lambda: pltpu.roll(values, width - 1, 1)),
            ):
                term = weight * turned()
                longer[offset + step] = longer[offset + step] + term if offset + step in longer else term
        band = longer
    return [band[offset] for offset in range(-STEPS, STEPS + 1)]


def apply_band(field, band):
    width = field.shape[1]
    total = band[STEPS : STEPS + 1] * field
    for offset in range(1, STEPS + 1):
        total = total + (
            band[STEPS - offset : STEPS - offset + 1] * pltpu.roll(field, offset, 1)
            + band[STEPS + offset : STEPS + offset + 1] * pltpu.roll(field, width - offset, 1)
        )
    return total


def row_pass(block, state, meta, y_ref, own_ref, other_ref, acc, part_ref):
    tile_num, row_num, half = own_ref.shape
    core = meta[2 * tile_num]
    own_at = pl.multiple_of(core * half, half)
    other_at = pl.multiple_of((1 - core) * half, half)
    state_own = state[:, pl.ds(own_at, half)]
    state_other = state[:, pl.ds(other_at, half)]
    lane = lax.broadcasted_iota(jnp.int32, (GROUP_ROWS, LANES), 1)
    row = lax.broadcasted_iota(jnp.int32, (GROUP_ROWS, LANES), 0)
    acc[...] = jnp.zeros_like(acc)

    def fold(values):
        total = values[:, :LANES]
        for start in range(LANES, half, LANES):
            total = total + values[:, start : start + LANES]
        return total

    def tile(index, carry):
        @pl.when(meta[index] == block)
        def _():
            live = meta[tile_num + index]
            readings = y_ref[pl.ds(index, 1), :]
            sum_own = jnp.zeros((GROUP_ROWS, half), jnp.float32)
            sum_other = jnp.zeros((GROUP_ROWS, half), jnp.float32)
            squares = jnp.zeros((GROUP_ROWS, LANES), jnp.float32)
            for start in range(0, row_num, GROUP_ROWS):
                own = own_ref[index, start : start + GROUP_ROWS, :].astype(jnp.float32)
                other = other_ref[index, start : start + GROUP_ROWS, :].astype(jnp.float32)
                valid = row + start < live
                product = fold(own * state_own) + fold(other * state_other)
                product = product - jnp.where(lane == row + start, readings, 0.0)
                weight = jnp.sum(product, axis=1, keepdims=True)
                weight = jnp.where(valid[:, :1], weight, 0.0)
                sum_own = sum_own + own * weight
                sum_other = sum_other + other * weight
                squares = squares + jnp.where(valid, fold(own * own) + fold(other * other), 0.0)
            acc[:, :half] += sum_own
            acc[:, half : 2 * half] += sum_other
            acc[:, 2 * half :] += squares

        return carry

    lax.fori_loop(0, tile_num, tile, 0)
    totals = jnp.sum(acc[...], axis=0, keepdims=True)
    part_ref[:, pl.ds(own_at, half)] = totals[:, :half]
    part_ref[:, pl.ds(other_at, half)] = totals[:, half : 2 * half]
    part_ref[:, 2 * half :] = totals[:, 2 * half :]


def first_kernel(block, meta, y_ref, own_ref, other_ref, state_ref, part_ref, acc):
    row_pass(block, state_ref, meta, y_ref, own_ref, other_ref, acc, part_ref)


def step_kernel(
    total_ref, meta, y_ref, own_ref, other_ref, state_ref, kappa_ref, rate_ref,
    next_ref, innovation_ref, part_ref, acc,
):
    width = state_ref.shape[1]
    trace_val = jnp.sum(total_ref[:, width:], axis=1, keepdims=True)
    lam_val = width / (2.0 * (width + trace_val))
    coeff, decay = kappa_ref[...], rate_ref[...]
    innovation = -lam_val * stencil(total_ref[:, :width], coeff, decay)
    next_ref[...] = stencil(state_ref[...], coeff, decay) + innovation
    innovation_ref[...] = innovation
    block = meta[2 * y_ref.shape[0] + 1]
    row_pass(block, next_ref, meta, y_ref, own_ref, other_ref, acc, part_ref)


def pieces_of(values):
    high = values.astype(jnp.bfloat16).astype(jnp.float32)
    middle = (values - high).astype(jnp.bfloat16).astype(jnp.float32)
    return high, middle, values - high - middle


def flip_of(turn, number, core):
    return FLIPS[number][:: 1 - 2 * core][turn]


def flip_here(turn, number, beside=0):
    if turn == number - 1:
        return 0
    on_core = [flip_of(turn, number, core) for core in range(2)]
    return jnp.where(lax.axis_index("state") == beside, on_core[0], on_core[1])


def half_kernel(blocks, counts, y_ref, own_ref, kappa_ref, rate_ref, gain_ref, *refs):
    outs, (turned_ref, acc, vec, side, readings, values) = refs[:-6], refs[-6:]
    tile_num, row_num, _ = own_ref.shape
    number = len(outs)
    core, position = lax.axis_index("state"), lax.axis_index("tm")
    acc[...] = jnp.zeros_like(acc)
    vec[...] = jnp.zeros_like(vec)
    side[...] = jnp.zeros_like(side)
    readings[...] = y_ref[...].astype(jnp.float32)
    for at, coefficient in enumerate((kappa_ref, rate_ref, gain_ref)):
        for piece in range(2):
            lanes = pl.ds(pl.multiple_of((2 * core + piece) * LANES, LANES), LANES)
            values[4 + 2 * at + piece : 5 + 2 * at + piece, :] = coefficient[:, lanes]
    row = lax.broadcasted_iota(jnp.int32, (1, row_num), 1)
    for index in range(tile_num):
        block = blocks[index]
        rows = own_ref[index]
        live = jnp.where(row < counts[index], 1.0, 0.0).astype(jnp.bfloat16)
        turned = rows.T * live
        turned_ref[index] = turned
        observed = jnp.broadcast_to(readings[index : index + 1, :], (16, row_num))
        both = jnp.concatenate([turned, observed.astype(jnp.bfloat16) * live], axis=0)
        square = jnp.dot(both, rows, preferred_element_type=jnp.float32)
        acc[block, 0:LANES] += square[:LANES, :LANES]
        acc[block, LANES : 2 * LANES] += square[:LANES, LANES:]
        acc[block, 2 * LANES : 3 * LANES] += square[LANES : 2 * LANES, LANES:]
        vec[block] += square[2 * LANES : 2 * LANES + 8, :]
    line = lax.broadcasted_iota(jnp.int32, (LANES, LANES), 0)
    column = lax.broadcasted_iota(jnp.int32, (LANES, LANES), 1)
    for turn, out_ref in enumerate(outs):
        block = position ^ flip_here(turn, number)
        first, between, second = (acc[block, at * LANES : (at + 1) * LANES] for at in range(3))
        packed = jnp.where(line < column, first, jnp.where(line > column, second, 0.0))
        out_ref[0:LANES] = packed.astype(jnp.bfloat16)
        out_ref[LANES : 2 * LANES] = between.astype(jnp.bfloat16)
        values[0:1, :] = vec[block, 0:1, :LANES]
        values[1:2, :] = vec[block, 0:1, LANES:]
        for at, square in ((2, first), (3, second)):
            values[at : at + 1, :] = jnp.sum(
                jnp.where(line == column, square, 0.0), axis=0, keepdims=True
            )
        for which, part in enumerate(pieces_of(values[...])):
            side[which * VECTORS : (which + 1) * VECTORS, :] = part
        out_ref[2 * LANES :] = side[...].astype(jnp.bfloat16)


def cross_kernel(blocks, turned_ref, other_ref, *refs):
    outs, acc = refs[:-1], refs[-1]
    number = len(outs)
    core, position = lax.axis_index("state"), lax.axis_index("tm")
    acc[...] = jnp.zeros_like(acc)
    for index in range(other_ref.shape[0]):
        block = blocks[index]
        for piece in range(2):
            at = pl.multiple_of((piece ^ core) * LANES, LANES)
            acc[block, piece * LANES : (piece + 1) * LANES] += jnp.dot(
                turned_ref[index, piece * LANES : (piece + 1) * LANES, :],
                other_ref[index, :, pl.ds(at, LANES)],
                preferred_element_type=jnp.float32,
            )
    for turn, out_ref in enumerate(outs):
        out_ref[...] = acc[position ^ flip_here(turn, number)].astype(jnp.bfloat16)


def sum_kernel(*refs):
    parts, (out_ref, coefficients, side) = refs[:-3], refs[-3:]
    number = len(parts) // 2
    position = lax.axis_index("tm")
    for at, some in enumerate((parts[:number], parts[number:])):
        total = some[0][: 2 * LANES].astype(jnp.float32)
        for part in some[1:]:
            total = total + part[: 2 * LANES].astype(jnp.float32)
        out_ref[2 * at * LANES : 2 * (at + 1) * LANES] = total.astype(jnp.bfloat16)
    values = None
    for turn, part in enumerate(parts[:number]):
        below = part[2 * LANES :].astype(jnp.float32)
        below = below[:VECTORS] + below[VECTORS : 2 * VECTORS] + below[2 * VECTORS : 3 * VECTORS]
        coefficients[position ^ flip_here(turn, number), 0 : VECTORS - 4] = below[4:]
        values = below[:4] if values is None else values + below[:4]
    side[...] = jnp.zeros_like(side)
    for which, part in enumerate(pieces_of(values)):
        side[which * 4 : which * 4 + 4, :] = part
    out_ref[4 * LANES :] = side[...].astype(jnp.bfloat16)


def band_kernel(here_ref, there_ref, band_ref, whole):
    core = lax.axis_index("state")
    block_num = here_ref.shape[0]
    for source, side in ((here_ref, core), (there_ref, 1 - core)):
        for block in range(block_num):
            for at in range(VECTORS - 4):
                lanes = pl.ds(pl.multiple_of((2 * side + at % 2) * LANES, LANES), LANES)
                whole[at // 2, block : block + 1, lanes] = source[block, at : at + 1]
    band = band_of(whole[0], whole[1]) + [whole[2]]
    for at, values in enumerate(band):
        for block in range(block_num):
            band_ref[block, at : at + 1, :] = values[block : block + 1]


def chain(grams, vectors, bands, state, states_ref, innovations_ref):
    width = state.shape[1]
    line = lax.broadcasted_iota(jnp.int32, (16, width), 0)
    for block in range(grams.shape[0]):
        info, diagonal = vectors[block, 0:1, :], vectors[block, 1:2, :]
        band = bands[block, : 2 * STEPS + 1, :]
        high, middle, low = pieces_of(state)
        split = jnp.where(line == 0, high, jnp.where(line == 1, middle, jnp.where(line == 2, low, 0.0)))
        product = jnp.dot(
            split.astype(jnp.bfloat16), grams[block], preferred_element_type=jnp.float32
        )
        product = jnp.sum(product, axis=0, keepdims=True) + diagonal * state
        trace_val = jnp.sum(diagonal, axis=1, keepdims=True)
        lam_val = width / (2.0 * (width + trace_val))
        innovation = -lam_val * apply_band(product - info, band)
        state = apply_band(state, band) + innovation
        states_ref[block : block + 1, :] = state
        innovations_ref[block : block + 1, :] = innovation


def put_grams(number, turns, own, other, grams, vectors):
    core, position = lax.axis_index("state"), lax.axis_index("tm")
    half = 2 * LANES
    line = lax.broadcasted_iota(jnp.int32, (LANES, LANES), 0)
    column = lax.broadcasted_iota(jnp.int32, (LANES, LANES), 1)
    for at, turn in enumerate(turns):
        flip, flip_other = flip_here(turn, number), flip_here(turn, number, 1)
        for pieces, side, block in (
            (own[at], core, position ^ flip),
            (other[at], 1 - core, position ^ flip_other),
        ):

            def piece(index):
                return pieces[index * LANES : (index + 1) * LANES, :]

            def put(row, column, values):
                row, column = pl.multiple_of(row, LANES), pl.multiple_of(column, LANES)
                grams[block, pl.ds(row, LANES), pl.ds(column, LANES)] = values.astype(jnp.bfloat16)

            here, there = side * half, (1 - side) * half
            packed = piece(0).astype(jnp.float32)
            turned = packed.T
            put(here, here, jnp.where(line < column, packed, turned))
            put(here + LANES, here + LANES, jnp.where(line > column, packed, turned))
            put(here, here + LANES, piece(1))
            put(here + LANES, here, piece(1).T)
            for index in range(2):
                beyond = there + (index ^ side) * LANES
                put(here + index * LANES, beyond, piece(2 + index))
                put(beyond, here + index * LANES, piece(2 + index).T)
            below = pieces[4 * LANES :, :].astype(jnp.float32)
            below = below[:4] + below[4:8] + below[8:12]
            for vector in range(4):
                lanes = pl.ds(pl.multiple_of(here + (vector % 2) * LANES, LANES), LANES)
                vectors[block, vector // 2 : vector // 2 + 1, lanes] = below[vector : vector + 1]


def early_kernel(number, turns, *refs):
    count = len(turns)
    put_grams(number, turns, refs[:count], refs[count : 2 * count], refs[-2], refs[-1])


def assemble_kernel(number, turns, *refs):
    count = len(turns)
    own, other, rest = refs[:count], refs[count : 2 * count], refs[2 * count :]
    _, _, bands, state_ref, grams, vectors, states_ref, innovations_ref = rest
    put_grams(number, turns, own, other, grams, vectors)
    chain_kernel(0, grams, vectors, bands, state_ref, states_ref, innovations_ref)


def chain_kernel(group, grams, vectors, bands, state_ref, states_ref, innovations_ref):
    @pl.when(lax.axis_index("grp") == group)
    def _():
        chain(grams, vectors, bands, state_ref[...], states_ref, innovations_ref)


def shards(rows_h, rows_y, tile_block, tile_count, kappa, rate, smooth_gain, start_state):
    tm_size, grp_size = lax.axis_size("tm"), lax.axis_size("grp")
    state_size = lax.axis_size("state")
    tm_index, grp_index, core = (lax.axis_index(name) for name in ("tm", "grp", "state"))
    tile_num, row_num, half = rows_h.shape[1:]
    width = kappa.shape[2]
    own = rows_h[0]
    other = lax.ppermute(own, "state", [(i, (i + 1) % state_size) for i in range(state_size)])
    state = start_state.reshape(1, width)
    direct = tm_size in FLIPS
    states_shape = jax.ShapeDtypeStruct((tm_size, width), jnp.float32)

    def flip_over(array, turn):
        pairs = [
            (i * state_size + j, (i ^ flip_of(turn, tm_size, j)) * state_size + j)
            for i in range(tm_size)
            for j in range(state_size)
        ]
        return lax.ppermute(array, ("tm", "state"), pairs)

    def ring(array, step):
        pairs = [
            (i * state_size + j, (i + step) % grp_size * state_size + state_size - 1 - j)
            for i in range(grp_size)
            for j in range(state_size)
        ]
        return lax.ppermute(array, ("grp", "state"), pairs)

    def across(array):
        return lax.ppermute(array, "state", [(i, (i + 1) % state_size) for i in range(state_size)])

    if direct:
        valid = jnp.where(own == own, own, jnp.zeros((), own.dtype))
        second_half = jax.ShapeDtypeStruct((2 * LANES, LANES), jnp.bfloat16)
        blocks = tile_block[0, :, 0]
        *pieces, turned = pl.pallas_call(
            half_kernel,
            out_shape=[jax.ShapeDtypeStruct((2 * LANES + 32, LANES), jnp.bfloat16)] * tm_size
            + [jax.ShapeDtypeStruct((tile_num, half, row_num), jnp.bfloat16)],
            in_specs=[SMEM] * 2 + [VMEM] * 5,
            out_specs=[VMEM] * (tm_size + 1),
            scratch_shapes=[
                pltpu.VMEM((tm_size, 3 * LANES, LANES), jnp.float32),
                pltpu.VMEM((tm_size, 8, half), jnp.float32),
                pltpu.VMEM((32, LANES), jnp.float32),
                pltpu.VMEM((tile_num, row_num), jnp.float32),
                pltpu.VMEM((VECTORS, LANES), jnp.float32),
            ],
            compiler_params=KERNEL,
        )(blocks, tile_count[0], rows_y[0], valid, kappa[0], rate[0], smooth_gain[0])
        turns = range(tm_size - 1)
        parts = [flip_over(pieces[turn], turn) for turn in turns] + [pieces[-1]]
        pieces2 = pl.pallas_call(
            cross_kernel,
            out_shape=[second_half] * tm_size,
            in_specs=[SMEM] + [VMEM] * 2,
            out_specs=[VMEM] * tm_size,
            scratch_shapes=[pltpu.VMEM((tm_size, 2 * LANES, LANES), jnp.float32)],
            compiler_params=KERNEL,
        )(blocks, turned, other)
        parts2 = [flip_over(pieces2[turn], turn) for turn in turns] + [pieces2[-1]]
        half_coefficients = jax.ShapeDtypeStruct((tm_size, 8, LANES), jnp.float32)
        own_sum, here = pl.pallas_call(
            sum_kernel,
            out_shape=(jax.ShapeDtypeStruct((4 * LANES + 16, LANES), jnp.bfloat16), half_coefficients),
            in_specs=[VMEM] * (2 * tm_size),
            out_specs=(VMEM, VMEM),
            scratch_shapes=[pltpu.VMEM((16, LANES), jnp.float32)],
            compiler_params=KERNEL,
        )(*parts, *parts2)
        own_sums = [flip_over(own_sum, turn) for turn in turns] + [own_sum]
        bands = pl.pallas_call(
            band_kernel,
            out_shape=jax.ShapeDtypeStruct((tm_size, 16, width), jnp.float32),
            in_specs=[VMEM, VMEM],
            out_specs=VMEM,
            scratch_shapes=[pltpu.VMEM((3, tm_size, width), jnp.float32)],
            compiler_params=KERNEL,
        )(here, across(here))
        bands, own_sums[0] = lax.optimization_barrier((bands, own_sums[0]))
        other_sums = [across(values) for values in own_sums]
        whole = (
            jax.ShapeDtypeStruct((tm_size, width, width), jnp.bfloat16),
            jax.ShapeDtypeStruct((tm_size, 8, width), jnp.float32),
        )
        late = [tm_size - 2]
        early = [turn for turn in range(tm_size) if turn not in late]
        arrays = [own_sums[turn] for turn in early] + [other_sums[turn] for turn in early]
        grams, vectors = pl.pallas_call(
            functools.partial(early_kernel, tm_size, early),
            out_shape=whole,
            in_specs=[VMEM] * len(arrays),
            out_specs=[VMEM] * 2,
            compiler_params=KERNEL,
        )(*arrays)
        arrays = [own_sums[turn] for turn in late] + [other_sums[turn] for turn in late]
        grams, vectors, new_states, new_innovations = pl.pallas_call(
            functools.partial(assemble_kernel, tm_size, late),
            out_shape=whole + (states_shape, states_shape),
            in_specs=[VMEM] * (len(arrays) + 4),
            out_specs=[VMEM] * 4,
            input_output_aliases={len(arrays): 0, len(arrays) + 1: 1},
            compiler_params=KERNEL,
        )(*arrays, grams, vectors, bands, state)
        gains = bands[:, 2 * STEPS + 1]

        def run_group(state, group):
            if group == 0:
                return new_states, new_innovations
            return pl.pallas_call(
                functools.partial(chain_kernel, group),
                out_shape=(states_shape, states_shape),
                in_specs=[VMEM] * 4,
                out_specs=(VMEM, VMEM),
                compiler_params=KERNEL,
            )(grams, vectors, bands, state)
    else:
        readings = rows_y[0].astype(jnp.float32)
        meta = jnp.concatenate(
            [tile_block[0, :, 0], tile_count[0], jnp.stack([core, tm_index]).astype(jnp.int32)]
        )
        params = jnp.concatenate([kappa[0], rate[0], smooth_gain[0]], axis=0)
        gathered = lax.all_gather(params, "tm")
        gains = gathered[:, 2]
        vector = jax.ShapeDtypeStruct((1, width), jnp.float32)
        partial = jax.ShapeDtypeStruct((1, width + LANES), jnp.float32)
        acc = pltpu.VMEM((GROUP_ROWS, width + LANES), jnp.float32)

        def run_group(state, group):
            part = pl.pallas_call(
                functools.partial(first_kernel, 0),
                out_shape=partial,
                in_specs=[SMEM] + [VMEM] * 4,
                out_specs=VMEM,
                scratch_shapes=[acc],
                compiler_params=KERNEL,
            )(meta, readings, own, other, state)

            def lap(block, carry):
                state, part, states, innovations = carry
                here = lax.dynamic_index_in_dim(gathered, block, 0, False)
                own_meta = meta.at[2 * tile_num + 1].set((block + 1).astype(jnp.int32))
                state, innovation, part = pl.pallas_call(
                    step_kernel,
                    out_shape=(vector, vector, partial),
                    in_specs=[VMEM, SMEM] + [VMEM] * 6,
                    out_specs=(VMEM, VMEM, VMEM),
                    scratch_shapes=[acc],
                    compiler_params=KERNEL,
                )(lax.psum(part, "tm"), own_meta, readings, own, other, state, here[0:1], here[1:2])
                states = lax.dynamic_update_slice_in_dim(states, state, block, 0)
                innovations = lax.dynamic_update_slice_in_dim(innovations, innovation, block, 0)
                return state, part, states, innovations

            empty = jnp.zeros((tm_size, width), jnp.float32)
            return lax.fori_loop(0, tm_size, lap, (state, part, empty, empty))[2:]

    states = innovations = jnp.zeros((tm_size, width), jnp.float32)
    for group in range(grp_size):
        new_states, new_innovations = run_group(state, group)
        mine = grp_index == group
        states = jnp.where(mine, new_states, states)
        innovations = jnp.where(mine, new_innovations, innovations)
        if group < grp_size - 1:
            state = ring(new_states[-1:], 1)

    residual = jnp.zeros((1, width), jnp.float32)
    residuals = [None] * tm_size
    for group in reversed(range(grp_size)):
        running = residual
        for block in reversed(range(tm_size)):
            residuals[block] = running
            running = gains[block][None] * (running + innovations[block][None])
        if group > 0:
            arrived = ring(running, -1)
            residual = jnp.where(grp_index == group - 1, arrived, residual)
    smoothed = states + jnp.concatenate(residuals, 0)

    def out(values):
        piece = lax.dynamic_slice(values, (tm_index, core * half), (1, half))
        return piece.reshape(1, 1, half)

    return out(states), out(smoothed)


def solution(mesh):
    return jax.shard_map(
        shards,
        mesh=mesh,
        in_specs=(
            P(("runs", "grp"), "tm", None, "state"),
            P(("runs", "grp"), "tm", None),
            P(("runs", "grp"), "tm", None),
            P(("runs", "grp"), "tm"),
            P(("runs", "grp"), "tm", None),
            P(("runs", "grp"), "tm", None),
            P(("runs", "grp"), "tm", None),
            P("runs"),
        ),
        out_specs=(P(("runs", "grp"), "tm", "state"), P(("runs", "grp"), "tm", "state")),
        check_vma=False,
    )
```
